32 devices in a mesh: fsdp: 16 (over z, y, core), tp: 2 (over x).
Axes of the slice: x: 2, y: 2, z: 4, core: 2. Of those that a mesh axis runs over, the one named last changes fastest.
Arguments:
- tokens_in: bfloat16 [256, 196, 768], P(('fsdp', 'tp')), may hold values from -6 to 6
- out_grad: bfloat16 [256, 196, 768], P(('fsdp', 'tp')), may hold values from -6 to 6
- image_counts: int32 [16], P('fsdp'), may hold values from 1 to 16, 192 in all
- norm_params: float32 [4, 768], replicated, may hold values from -0.9 to 1.9, as said below
- w_qkv: float32 [3, 768, 768], P(None, 'fsdp', 'tp'), may hold values from -0.21875 to 0.21875
- bias_qv: float32 [2, 768], P(None, ('tp', 'fsdp')), may hold values from -3 to 3
- w_out: float32 [768, 768], P('tp', 'fsdp'), may hold values from -2.5 to 2.5
- w_fc1: float32 [768, 3072], P('fsdp', 'tp'), may hold values from -0.21875 to 0.21875
- bias_fc1: float32 [3072], P(('tp', 'fsdp')), may hold values from -3 to 3
- w_fc2: float32 [3072, 768], P('tp', 'fsdp'), may hold values from -0.109375 to 0.109375
- bias_out: float32 [2, 768], replicated, may hold values from -3 to 3
- first_norm: float32 [4, 768], replicated, may hold values from -1976.7312 to 1976.7312
- first_qkv: float32 [3, 768, 768], P(None, 'fsdp', 'tp'), may hold values from -593.01935 to 593.01935
- first_bias_qv: float32 [2, 768], P(None, ('tp', 'fsdp')), may hold values from -1976.7312 to 1976.7312
- first_out: float32 [768, 768], P('tp', 'fsdp'), may hold values from -94.08 to 94.08
- first_fc1: float32 [768, 3072], P('fsdp', 'tp'), may hold values from -60.48 to 60.48
- first_bias_fc1: float32 [3072], P(('tp', 'fsdp')), may hold values from -60.48 to 60.48
- first_fc2: float32 [3072, 768], P('tp', 'fsdp'), may hold values from -107.52 to 107.52
- first_bias_out: float32 [2, 768], replicated, may hold values from -174.72 to 174.72
- second_norm: float32 [4, 768], replicated, may hold values from 1477.1814 to 14771.814
- second_qkv: float32 [3, 768, 768], P(None, 'fsdp', 'tp'), may hold values from 134.8731 to 1348.7308
- second_bias_qv: float32 [2, 768], P(None, ('tp', 'fsdp')), may hold values from 1477.1814 to 14771.814
- second_out: float32 [768, 768], P('tp', 'fsdp'), may hold values from 3.01056 to 30.1056
- second_fc1: float32 [768, 3072], P('fsdp', 'tp'), may hold values from 1.354752 to 13.54752
- second_bias_fc1: float32 [3072], P(('tp', 'fsdp')), may hold values from 1.354752 to 13.54752
- second_fc2: float32 [3072, 768], P('tp', 'fsdp'), may hold values from 4.51584 to 45.1584
- second_bias_out: float32 [2, 768], replicated, may hold values from 12.04224 to 120.4224
Outputs:
- block_out: bfloat16 [256, 196, 768], P(('fsdp', 'tp'))
- grad_tokens: float32 [256, 196, 768], P(('fsdp', 'tp'))
- grad_norm: float32 [4, 768], replicated
- grad_qkv: float32 [3, 768, 768], P(None, 'fsdp', 'tp')
- grad_bias_qv: float32 [2, 768], P(None, ('tp', 'fsdp'))
- grad_out: float32 [768, 768], P('tp', 'fsdp')
- grad_fc1: float32 [768, 3072], P('fsdp', 'tp')
- grad_bias_fc1: float32 [3072], P(('tp', 'fsdp'))
- grad_fc2: float32 [3072, 768], P('tp', 'fsdp')
- grad_bias_out: float32 [2, 768], replicated
- step_norm: float32 [4, 768], replicated
- new_qkv: float32 [3, 768, 768], P(None, 'fsdp', 'tp')
- step_bias_qv: float32 [2, 768], P(None, ('tp', 'fsdp'))
- step_out: float32 [768, 768], P('tp', 'fsdp')
- new_fc1: float32 [768, 3072], P('fsdp', 'tp')
- step_bias_fc1: float32 [3072], P(('tp', 'fsdp'))
- new_fc2: float32 [3072, 768], P('tp', 'fsdp')
- step_bias_out: float32 [2, 768], replicated
- new_first_norm: float32 [4, 768], replicated
- new_first_qkv: float32 [3, 768, 768], P(None, 'fsdp', 'tp')
- new_first_bias_qv: float32 [2, 768], P(None, ('tp', 'fsdp'))
- new_first_out: float32 [768, 768], P('tp', 'fsdp')
- new_first_fc1: float32 [768, 3072], P('fsdp', 'tp')
- new_first_bias_fc1: float32 [3072], P(('tp', 'fsdp'))
- new_first_fc2: float32 [3072, 768], P('tp', 'fsdp')
- new_first_bias_out: float32 [2, 768], replicated
- new_second_norm: float32 [4, 768], replicated
- new_second_qkv: float32 [3, 768, 768], P(None, 'fsdp', 'tp')
- new_second_bias_qv: float32 [2, 768], P(None, ('tp', 'fsdp'))
- new_second_out: float32 [768, 768], P('tp', 'fsdp')
- new_second_fc1: float32 [768, 3072], P('fsdp', 'tp')
- new_second_bias_fc1: float32 [3072], P(('tp', 'fsdp'))
- new_second_fc2: float32 [3072, 768], P('tp', 'fsdp')
- new_second_bias_out: float32 [2, 768], replicated
The draws below stay inside these ranges and needn't reach their ends.
Inputs may be any that keep to these rules, and one draw needn't show every extreme that they name: image_counts[g] live images fill slots 0 to image_counts[g] - 1 of group g; at least one group is full. `norm_params`: rows 0 and 2 are gains, rows 1 and 3 shifts.
All inputs are finite; a program needn't handle non-finite values.
Results may differ from the reference program's by a relative error of at most 0.013.
Values may be sent and summed in bfloat16 or wider, within the bound.
A program may use at most 320 MiB of HBM per device.

```python
import math
import jax
import jax.numpy as jnp
import numpy as np
from jax import lax

D = 768
HEADS = 12
HEAD_DIM = 64
FF = 3072
SEQ = 196
IMG_DEV = 16
ADAM_STEP = 10
IMAGES = 256
N_FSDP = 16


def draw_norm_params(key, part):
    spread = jnp.clip(0.25 * jax.random.normal(key, (4, D), jnp.float32), -0.9, 0.9)
    centre = jnp.array([1.0, 0.0, 1.0, 0.0], jnp.float32)[:, None]
    return centre + spread


def steps_of(own_key, shape, pieces, low, largest):
    loudness, own = 1.0, jax.random.fold_in(own_key, 6)
    for axis_at, blocks in pieces:
        steps = jnp.exp(jax.random.uniform(jax.random.fold_in(own, axis_at), (blocks,), jnp.float32, low / len(pieces), largest / len(pieces)))
        loudness = loudness * jnp.repeat(steps, shape[axis_at] // blocks).reshape([-1 if axis == axis_at else 1 for axis in range(len(shape))])
    return loudness


def profile(amount, total, bound, skew):
    weights = [(1 << 20) // math.isqrt(grade ** skew) + 1 for grade in range(2, amount + 1)]
    rest, given = total - bound - (amount - 1), [1] * (amount - 1)
    while rest > 0:
        movable = [i for i in range(amount - 1) if given[i] < bound]
        pool, remaining = sum([weights[i] for i in movable]), rest
        for i in movable:
            addition = min(bound - given[i], max(1, remaining * weights[i] // pool), rest)
            given[i] = given[i] + addition
            rest = rest - addition
    return np.array([bound] + given)


def ragged_sizes(rng, amount, total, limit, lean):
    if amount == 2:
        one = jax.random.randint(rng, (), max(1, total - limit), min(limit, total - 1) + 1)
        return jnp.stack([one, total - one])
    sizes = jnp.asarray(profile(amount, total, limit, lean), jnp.int32)
    twos = (amount - 1) // 2
    donor, taker = sizes[1:1 + 2 * twos:2], sizes[2:2 + 2 * twos:2]
    slack = jnp.minimum(donor - 1, limit - taker)
    moved = jax.random.randint(jax.random.fold_in(rng, 1), (twos,), 0, 1 << 20) % (slack + 1)
    sizes = sizes.at[1:1 + 2 * twos:2].set(donor - moved).at[2:2 + 2 * twos:2].set(taker + moved)
    return sizes[jax.random.permutation(jax.random.fold_in(rng, 2), amount)]


def bell_draw(own_key, shape, scale, reach, pieces=(), dtype=jnp.bfloat16):
    values = scale * jax.random.normal(own_key, shape, jnp.float32)
    if pieces:
        values = values * steps_of(own_key, shape, pieces, -0.22, 0.18)
    return jnp.clip(values, -reach, reach).astype(dtype)


def setup_inputs(seed: int = 0) -> dict:
    keys = jax.random.split(jax.random.key(seed), 28)
    return {
        "tokens_in": bell_draw(keys[0], (IMAGES, SEQ, D), 1.0, 6.0, ((0, 32),)),
        "out_grad": bell_draw(keys[1], (IMAGES, SEQ, D), 1.0, 6.0, ((0, 32),)),
        "image_counts": ragged_sizes(keys[2], N_FSDP, N_FSDP * IMG_DEV * 3 // 4, IMG_DEV, 2).astype(jnp.int32),
        "norm_params": draw_norm_params(jax.random.fold_in(keys[27], 71), 0),
        "w_qkv": bell_draw(keys[4], (3, D, D), D ** -0.5, 0.21875, ((1, 16), (2, 2)), jnp.float32),
        "bias_qv": bell_draw(keys[5], (2, D), 0.5, 3.0, ((1, 32),), jnp.float32),
        "w_out": bell_draw(keys[6], (D, D), (max(1, D * 14 // (8 * SEQ))) ** -0.5, 2.5, ((0, 2), (1, 16)), jnp.float32),
        "w_fc1": bell_draw(keys[7], (D, FF), D ** -0.5, 0.21875, ((0, 16), (1, 2)), jnp.float32),
        "bias_fc1": bell_draw(keys[8], (FF,), 0.5, 3.0, ((0, 32),), jnp.float32),
        "w_fc2": bell_draw(keys[9], (FF, D), FF ** -0.5, 0.109375, ((0, 2), (1, 16)), jnp.float32),
        "bias_out": bell_draw(keys[10], (2, D), 0.5, 3.0, (), jnp.float32),
        "first_norm": bell_draw(keys[11], (4, D), (0.13 * (IMAGES * SEQ * D * max(1, D * 14 // (8 * SEQ)) ** -1) ** 0.5), 1976.7312, (), jnp.float32),
        "first_qkv": bell_draw(keys[12], (3, D, D), (0.039 * (IMAGES * SEQ * D * max(1, D * 14 // (8 * SEQ)) ** -1) ** 0.5), 593.01935, ((1, 16), (2, 2)), jnp.float32),
        "first_bias_qv": bell_draw(keys[13], (2, D), (0.13 * (IMAGES * SEQ * D * max(1, D * 14 // (8 * SEQ)) ** -1) ** 0.5), 1976.7312, ((1, 32),), jnp.float32),
        "first_out": bell_draw(keys[14], (D, D), (0.07 * (IMAGES * SEQ) ** 0.5), 94.08, ((0, 2), (1, 16)), jnp.float32),
        "first_fc1": bell_draw(keys[15], (D, FF), (0.045 * (IMAGES * SEQ) ** 0.5), 60.48, ((0, 16), (1, 2)), jnp.float32),
        "first_bias_fc1": bell_draw(keys[16], (FF,), (0.045 * (IMAGES * SEQ) ** 0.5), 60.48, ((0, 32),), jnp.float32),
        "first_fc2": bell_draw(keys[17], (FF, D), (0.08 * (IMAGES * SEQ) ** 0.5), 107.52, ((0, 2), (1, 16)), jnp.float32),
        "first_bias_out": bell_draw(keys[18], (2, D), (0.13 * (IMAGES * SEQ) ** 0.5), 174.72, (), jnp.float32),
        "second_norm": jnp.clip(jnp.exp(jax.random.uniform(keys[19], (4, D), jnp.float32, math.log(1477.1814), math.log(14771.814))), 1477.1814, 14771.814),
        "second_qkv": jnp.clip(jnp.exp(math.log(1348.7308) - 2.30258503 * jax.random.uniform(keys[20], (3, D, D), jnp.float32) ** steps_of(keys[20], (3, D, D), ((1, 16), (2, 2)), -0.2, 0.2)), 134.8731, 1348.7308),
        "second_bias_qv": jnp.clip(jnp.exp(math.log(14771.814) - 2.3025851 * jax.random.uniform(keys[21], (2, D), jnp.float32) ** steps_of(keys[21], (2, D), ((1, 32),), -0.2, 0.2)), 1477.1814, 14771.814),
        "second_out": jnp.clip(jnp.exp(math.log(30.1056) - 2.3025851 * jax.random.uniform(keys[22], (D, D), jnp.float32) ** steps_of(keys[22], (D, D), ((0, 2), (1, 16)), -0.2, 0.2)), 3.01056, 30.1056),
        "second_fc1": jnp.clip(jnp.exp(math.log(13.54752) - 2.3025851 * jax.random.uniform(keys[23], (D, FF), jnp.float32) ** steps_of(keys[23], (D, FF), ((0, 16), (1, 2)), -0.2, 0.2)), 1.354752, 13.54752),
        "second_bias_fc1": jnp.clip(jnp.exp(math.log(13.54752) - 2.3025851 * jax.random.uniform(keys[24], (FF,), jnp.float32) ** steps_of(keys[24], (FF,), ((0, 32),), -0.2, 0.2)), 1.354752, 13.54752),
        "second_fc2": jnp.clip(jnp.exp(math.log(45.1584) - 2.3025851 * jax.random.uniform(keys[25], (FF, D), jnp.float32) ** steps_of(keys[25], (FF, D), ((0, 2), (1, 16)), -0.2, 0.2)), 4.51584, 45.1584),
        "second_bias_out": jnp.clip(jnp.exp(jax.random.uniform(keys[26], (2, D), jnp.float32, math.log(12.04224), math.log(120.4224))), 12.04224, 120.4224),
    }


@jax.custom_vjp
def low(v):
    return lax.optimization_barrier(v.astype(jnp.bfloat16)).astype(jnp.float32)

@jax.custom_vjp
def low_back(v):
    return v

def low_keep(v):
    return (low(v), None)

def low_pass(kept, grad):
    return (grad,)

def back_keep(v):
    return (v, None)

def back_low(kept, grad):
    return (low(grad),)
low.defvjp(low_keep, low_pass)
low_back.defvjp(back_keep, back_low)
norm_eps = 1e-06
learn_rate = 0.02
beta_one = 0.9
beta_two = 0.999
adam_eps = 1e-08
decay_rate = 0.05

def layer_norm(rows_in, gain_vec, shift_vec):
    centre = rows_in - lax.optimization_barrier(jnp.mean(rows_in, axis=-1, keepdims=True))
    spread = lax.optimization_barrier(jnp.mean(centre * centre, axis=-1, keepdims=True))
    return centre * lax.rsqrt(spread + norm_eps) * gain_vec + shift_vec

def matmul(left, right):
    return jnp.dot(left, right, precision=lax.Precision.HIGHEST)

def block(inputs, params):
    norm_params, w_qkv, bias_qv, w_out, w_fc1, bias_fc1, w_fc2, bias_out = params
    images = inputs.shape[0]
    shape_heads = (images, SEQ, HEADS, HEAD_DIM)
    score_scale = HEAD_DIM ** (-0.5)
    qkv_low = low(w_qkv)
    bqv_low = low(bias_qv)
    hidden_one = low(layer_norm(inputs, norm_params[0], norm_params[1]))
    queries = low(low_back(matmul(hidden_one, qkv_low[0]) + bqv_low[0])).reshape(shape_heads)
    key_vecs = low(low_back(matmul(hidden_one, qkv_low[1]))).reshape(shape_heads)
    value_vecs = low(low_back(matmul(hidden_one, qkv_low[2]) + bqv_low[1])).reshape(shape_heads)
    scores = low_back(jnp.einsum('gqhe,gkhe->ghqk', queries, key_vecs, precision=lax.Precision.HIGHEST) * score_scale)
    probs_low = low(jax.nn.softmax(scores, axis=-1))
    context = jnp.einsum('ghqk,gkhe->gqhe', probs_low, value_vecs, precision=lax.Precision.HIGHEST)
    context = low(low_back(context.reshape(images, SEQ, D)))
    attn_sum = low_back(matmul(context, low(w_out)))
    middle = inputs + attn_sum + bias_out[0]
    hidden_two = low(layer_norm(middle, norm_params[2], norm_params[3]))
    pre_act = low_back(matmul(hidden_two, low(w_fc1)) + low(bias_fc1))
    activated = low(jax.nn.gelu(pre_act, approximate=False))
    mlp_sum = low_back(matmul(activated, low(w_fc2)))
    return middle + mlp_sum + bias_out[1]

def add_pair(running, addend):
    return running + addend

def adamw(parameter, gradient, moment_one, moment_two, decay_on):
    one_new = beta_one * moment_one + (1.0 - beta_one) * gradient
    two_new = beta_two * moment_two + (1.0 - beta_two) * gradient * gradient
    one_hat = one_new / (1.0 - beta_one ** ADAM_STEP)
    two_hat = two_new / (1.0 - beta_two ** ADAM_STEP)
    update = one_hat / (jnp.sqrt(two_hat) + adam_eps) + decay_on * parameter
    return (-learn_rate * update, one_new, two_new)

def reference(tokens_in, out_grad, image_counts, norm_params, w_qkv, bias_qv, w_out, w_fc1, bias_fc1, w_fc2, bias_out, first_norm, first_qkv, first_bias_qv, first_out, first_fc1, first_bias_fc1, first_fc2, first_bias_out, second_norm, second_qkv, second_bias_qv, second_out, second_fc1, second_bias_fc1, second_fc2, second_bias_out):
    params = (norm_params, w_qkv, bias_qv, w_out, w_fc1, bias_fc1, w_fc2, bias_out)
    inputs = tokens_in.astype(jnp.float32).reshape(N_FSDP, IMG_DEV, SEQ, D)
    cotangent = out_grad.astype(jnp.float32).reshape(N_FSDP, IMG_DEV, SEQ, D)

    def one_group(totals, sliced):
        group_in, group_cot, group_count = sliced
        live_mask = (jnp.arange(IMG_DEV) < group_count).astype(jnp.float32)
        outputs, pullback = jax.vjp(block, group_in, params)
        grad_in, grad_params = pullback(group_cot * live_mask[:, None, None])
        totals = jax.tree.map(add_pair, totals, grad_params)
        return (totals, (outputs.astype(jnp.bfloat16), grad_in))
    zeros_init = jax.tree.map(jnp.zeros_like, params)
    grads, (outs_all, grads_in) = lax.scan(one_group, zeros_init, (inputs, cotangent, image_counts))
    block_out = outs_all.reshape(IMAGES, SEQ, D)
    grad_tokens = grads_in.reshape(IMAGES, SEQ, D)
    g_norm, g_qkv, g_bqv, g_out, g_fc1, g_bfc1, g_fc2, g_bout = grads
    s_norm, a_norm, b_norm = adamw(norm_params, g_norm, first_norm, second_norm, 0.0)
    s_qkv, a_qkv, b_qkv = adamw(w_qkv, g_qkv, first_qkv, second_qkv, decay_rate)
    s_bqv, a_bqv, b_bqv = adamw(bias_qv, g_bqv, first_bias_qv, second_bias_qv, 0.0)
    s_out, a_out, b_out = adamw(w_out, g_out, first_out, second_out, decay_rate)
    s_fc1, a_fc1, b_fc1 = adamw(w_fc1, g_fc1, first_fc1, second_fc1, decay_rate)
    s_bfc1, a_bfc1, b_bfc1 = adamw(bias_fc1, g_bfc1, first_bias_fc1, second_bias_fc1, 0.0)
    s_fc2, a_fc2, b_fc2 = adamw(w_fc2, g_fc2, first_fc2, second_fc2, decay_rate)
    s_bout, a_bout, b_bout = adamw(bias_out, g_bout, first_bias_out, second_bias_out, 0.0)
    return (block_out, grad_tokens, g_norm, g_qkv, g_bqv, g_out, g_fc1, g_bfc1, g_fc2, g_bout, s_norm, w_qkv + s_qkv, s_bqv, s_out, w_fc1 + s_fc1, s_bfc1, w_fc2 + s_fc2, s_bout, a_norm, a_qkv, a_bqv, a_out, a_fc1, a_bfc1, a_fc2, a_bout, b_norm, b_qkv, b_bqv, b_out, b_fc1, b_bfc1, b_fc2, b_bout)
```

```python
import functools

import jax
import jax.numpy as jnp
from jax import lax
from jax.experimental import pallas as pl
from jax.experimental.pallas import tpu as pltpu
from jax.sharding import PartitionSpec as P

HEAD_DIM = 64
ADAM_STEP = 10


norm_eps = 1e-06
learn_rate = 0.02
beta_one = 0.9
beta_two = 0.999
adam_eps = 1e-08
decay_rate = 0.05


def layer_norm(rows_in, gain_vec, shift_vec):
    centre = rows_in - jnp.mean(rows_in, axis=-1, keepdims=True)
    spread = jnp.mean(centre * centre, axis=-1, keepdims=True)
    return centre * lax.rsqrt(spread + norm_eps) * gain_vec + shift_vec


def exact_gelu(rows_in):
    return jax.nn.gelu(rows_in, approximate=False)


def adamw(parameter, gradient, moment_one, moment_two, decay_on):
    one_new = beta_one * moment_one + (1.0 - beta_one) * gradient
    two_new = beta_two * moment_two + (1.0 - beta_two) * gradient * gradient
    one_hat = one_new / (1.0 - beta_one**ADAM_STEP)
    two_hat = two_new / (1.0 - beta_two**ADAM_STEP)
    update = one_hat / (jnp.sqrt(two_hat) + adam_eps) + decay_on * parameter
    return (-learn_rate * update, one_new, two_new)


def per_device(
    tokens_in,
    out_grad,
    image_counts,
    norm_params,
    w_qkv,
    bias_qv,
    w_out,
    w_fc1,
    bias_fc1,
    w_fc2,
    bias_out,
    first_norm,
    first_qkv,
    first_bias_qv,
    first_out,
    first_fc1,
    first_bias_fc1,
    first_fc2,
    first_bias_out,
    second_norm,
    second_qkv,
    second_bias_qv,
    second_out,
    second_fc1,
    second_bias_fc1,
    second_fc2,
    second_bias_out,
):
    images = tokens_in.shape[0]
    seq_len = tokens_in.shape[1]
    score_scale = HEAD_DIM ** (-0.5)
    inputs = tokens_in.astype(jnp.float32)
    slot_ids = lax.axis_index("tp") * images + jnp.arange(images)
    live_mask = (slot_ids < image_counts[0]).astype(jnp.float32)
    live_grad = out_grad.astype(jnp.float32) * live_mask[:, None, None]
    qkv_all, bqv_all, wout_all = (
        lax.all_gather(w_qkv.astype(jnp.bfloat16), "fsdp", axis=1, tiled=True),
        lax.all_gather(bias_qv.astype(jnp.bfloat16), "fsdp", axis=1, tiled=True),
        lax.all_gather(w_out.astype(jnp.bfloat16), "fsdp", axis=1, tiled=True),
    )
    fc1_all, bfc1_all, fc2_all = (
        lax.all_gather(w_fc1.astype(jnp.bfloat16), "fsdp", axis=0, tiled=True),
        lax.all_gather(bias_fc1.astype(jnp.bfloat16), "fsdp", axis=0, tiled=True),
        lax.all_gather(w_fc2.astype(jnp.bfloat16), "fsdp", axis=1, tiled=True),
    )
    hidden_one = layer_norm(inputs, norm_params[0], norm_params[1]).astype(jnp.bfloat16)
    qkv_use, bqv_use, wout_use = (
        lax.all_gather(qkv_all, "tp", axis=2, tiled=True),
        lax.all_gather(bqv_all, "tp", axis=1, tiled=True),
        lax.all_gather(wout_all, "tp", axis=0, tiled=True),
    )
    group_images = hidden_one.shape[0]
    projected = jnp.einsum("gsd,cdf->cgsf", hidden_one, qkv_use, preferred_element_type=jnp.float32)
    width_local = projected.shape[3]
    shape_heads = (group_images, seq_len, width_local // HEAD_DIM, HEAD_DIM)
    queries = (projected[0] + bqv_use[0]).astype(jnp.bfloat16).reshape(shape_heads)
    key_vecs = projected[1].astype(jnp.bfloat16).reshape(shape_heads)
    value_vecs = (projected[2] + bqv_use[1]).astype(jnp.bfloat16).reshape(shape_heads)
    scores = (
        jnp.einsum("gqhe,gkhe->ghqk", queries, key_vecs, preferred_element_type=jnp.float32)
        * score_scale
    )
    log_total = jax.nn.logsumexp(scores, axis=-1, keepdims=True)
    probs_low = jnp.exp(scores - log_total).astype(jnp.bfloat16)
    context = jnp.einsum(
        "ghqk,gkhe->gqhe", probs_low, value_vecs, preferred_element_type=jnp.float32
    )
    context = context.astype(jnp.bfloat16).reshape(group_images, seq_len, width_local)
    attn_part = jnp.einsum("gsf,fd->gsd", context, wout_use, preferred_element_type=jnp.float32)
    middle = inputs + attn_part + bias_out[0]
    hidden_two = layer_norm(middle, norm_params[2], norm_params[3]).astype(jnp.bfloat16)
    mlp_in = lax.all_gather(hidden_two, "tp", axis=0, tiled=True)
    fc1_use, bfc1_use, fc2_use = (fc1_all, bfc1_all, fc2_all)
    pre_act = (
        jnp.einsum("gsd,df->gsf", mlp_in, fc1_use, preferred_element_type=jnp.float32) + bfc1_use
    )
    activated = exact_gelu(pre_act).astype(jnp.bfloat16)
    mlp_part = jnp.einsum("gsf,fd->gsd", activated, fc2_use, preferred_element_type=jnp.float32)
    mlp_sum = lax.psum_scatter(
        mlp_part.astype(jnp.bfloat16), "tp", scatter_dimension=0, tiled=True
    ).astype(jnp.float32)
    block_out = (middle + mlp_sum + bias_out[1]).astype(jnp.bfloat16)
    grad_mlp = live_grad.astype(jnp.bfloat16)
    grad_mlp_in = lax.all_gather(grad_mlp, "tp", axis=0, tiled=True)
    grad_w2 = jnp.einsum("gsf,gsd->fd", activated, grad_mlp_in, preferred_element_type=jnp.float32)
    grad_act = jnp.einsum("gsd,fd->gsf", grad_mlp_in, fc2_use, preferred_element_type=jnp.float32)
    gelu_out, gelu_pull = jax.vjp(exact_gelu, pre_act)
    grad_pre = gelu_pull(grad_act)[0].astype(jnp.bfloat16)
    grad_b1 = jnp.sum(grad_pre.astype(jnp.float32), axis=(0, 1))
    grad_w1 = jnp.einsum("gsd,gsf->df", mlp_in, grad_pre, preferred_element_type=jnp.float32)
    grad_h2_part = jnp.einsum("gsf,df->gsd", grad_pre, fc1_use, preferred_element_type=jnp.float32)
    grad_h2 = lax.psum_scatter(
        grad_h2_part.astype(jnp.bfloat16), "tp", scatter_dimension=0, tiled=True
    ).astype(jnp.float32)
    norm_two, norm_two_pull = jax.vjp(layer_norm, middle, norm_params[2], norm_params[3])
    grad_mid_ln, grad_gain_two, grad_shift_two = norm_two_pull(grad_h2)
    grad_middle = live_grad + grad_mid_ln
    grad_attn = grad_middle.astype(jnp.bfloat16)
    grad_wo = jnp.einsum("gsf,gsd->fd", context, grad_attn, preferred_element_type=jnp.float32)
    grad_ctx = jnp.einsum("gsd,fd->gsf", grad_attn, wout_use, preferred_element_type=jnp.float32)
    grad_ctx = grad_ctx.astype(jnp.bfloat16).reshape(shape_heads)
    scores_again = (
        jnp.einsum("gqhe,gkhe->ghqk", queries, key_vecs, preferred_element_type=jnp.float32)
        * score_scale
    )
    probs_again = jnp.exp(scores_again - log_total)
    grad_probs = jnp.einsum(
        "gqhe,gkhe->ghqk", grad_ctx, value_vecs, preferred_element_type=jnp.float32
    )
    row_terms = jnp.sum(probs_again * grad_probs, axis=-1, keepdims=True)
    grad_scores = (probs_again * (grad_probs - row_terms)).astype(jnp.bfloat16)
    grad_query = (
        jnp.einsum("ghqk,gkhe->gqhe", grad_scores, key_vecs, preferred_element_type=jnp.float32)
        * score_scale
    ).astype(jnp.bfloat16)
    grad_keys = (
        jnp.einsum("ghqk,gqhe->gkhe", grad_scores, queries, preferred_element_type=jnp.float32)
        * score_scale
    ).astype(jnp.bfloat16)
    grad_values = jnp.einsum(
        "ghqk,gqhe->gkhe",
        probs_again.astype(jnp.bfloat16),
        grad_ctx,
        preferred_element_type=jnp.float32,
    ).astype(jnp.bfloat16)
    grad_proj = jnp.stack([grad_query, grad_keys, grad_values]).reshape(
        3, group_images, seq_len, width_local
    )
    grad_bqv = jnp.stack(
        [
            jnp.sum(grad_proj[0].astype(jnp.float32), axis=(0, 1)),
            jnp.sum(grad_proj[2].astype(jnp.float32), axis=(0, 1)),
        ]
    )
    grad_wqkv = jnp.einsum(
        "gsd,cgsf->cdf", hidden_one, grad_proj, preferred_element_type=jnp.float32
    )
    grad_h1_part = jnp.einsum(
        "cgsf,cdf->gsd", grad_proj, qkv_use, preferred_element_type=jnp.float32
    )
    grad_wqkv, grad_bqv, grad_wo = (
        lax.psum_scatter(
            grad_wqkv.astype(jnp.bfloat16), "tp", scatter_dimension=2, tiled=True
        ).astype(jnp.float32),
        lax.psum_scatter(
            grad_bqv.astype(jnp.bfloat16), "tp", scatter_dimension=1, tiled=True
        ).astype(jnp.float32),
        lax.psum_scatter(
            grad_wo.astype(jnp.bfloat16), "tp", scatter_dimension=0, tiled=True
        ).astype(jnp.float32),
    )
    norm_one, norm_one_pull = jax.vjp(layer_norm, inputs, norm_params[0], norm_params[1])
    grad_in_ln, grad_gain_one, grad_shift_one = norm_one_pull(grad_h1_part)
    grad_tokens = grad_middle + grad_in_ln
    g_qkv, g_bqv, g_out, g_fc1, g_bfc1, g_fc2 = (
        lax.psum_scatter(grad_wqkv, "fsdp", scatter_dimension=1, tiled=True),
        lax.psum_scatter(grad_bqv, "fsdp", scatter_dimension=1, tiled=True),
        lax.psum_scatter(grad_wo, "fsdp", scatter_dimension=1, tiled=True),
        lax.psum_scatter(grad_w1, "fsdp", scatter_dimension=0, tiled=True),
        lax.psum_scatter(grad_b1, "fsdp", scatter_dimension=0, tiled=True),
        lax.psum_scatter(grad_w2, "fsdp", scatter_dimension=1, tiled=True),
    )
    norm_terms = jnp.stack([grad_gain_one, grad_shift_one, grad_gain_two, grad_shift_two])
    bias_terms = jnp.stack([jnp.sum(grad_middle, axis=(0, 1)), jnp.sum(live_grad, axis=(0, 1))])
    g_norm, g_bout = lax.psum((norm_terms, bias_terms), ("fsdp", "tp"))
    s_norm, a_norm, b_norm = adamw(norm_params, g_norm, first_norm, second_norm, 0.0)
    s_qkv, a_qkv, b_qkv = adamw(w_qkv, g_qkv, first_qkv, second_qkv, decay_rate)
    s_bqv, a_bqv, b_bqv = adamw(bias_qv, g_bqv, first_bias_qv, second_bias_qv, 0.0)
    s_out, a_out, b_out = adamw(w_out, g_out, first_out, second_out, decay_rate)
    s_fc1, a_fc1, b_fc1 = adamw(w_fc1, g_fc1, first_fc1, second_fc1, decay_rate)
    s_bfc1, a_bfc1, b_bfc1 = adamw(bias_fc1, g_bfc1, first_bias_fc1, second_bias_fc1, 0.0)
    s_fc2, a_fc2, b_fc2 = adamw(w_fc2, g_fc2, first_fc2, second_fc2, decay_rate)
    s_bout, a_bout, b_bout = adamw(bias_out, g_bout, first_bias_out, second_bias_out, 0.0)
    return (
        block_out,
        grad_tokens,
        g_norm,
        g_qkv,
        g_bqv,
        g_out,
        g_fc1,
        g_bfc1,
        g_fc2,
        g_bout,
        s_norm,
        w_qkv + s_qkv,
        s_bqv,
        s_out,
        w_fc1 + s_fc1,
        s_bfc1,
        w_fc2 + s_fc2,
        s_bout,
        a_norm,
        a_qkv,
        a_bqv,
        a_out,
        a_fc1,
        a_bfc1,
        a_fc2,
        a_bout,
        b_norm,
        b_qkv,
        b_bqv,
        b_out,
        b_fc1,
        b_bfc1,
        b_fc2,
        b_bout,
    )


F32, BF16 = jnp.float32, jnp.bfloat16
MESH_IDS = pl.DeviceIdType.MESH
VMEM_BYTES = 62 * 2**20

NZ, NY, NCORE, NTP = 4, 2, 2, 2
HALF = 256
NEG = -1e30
LANES = 256


def dot(a, b, ca, cb):
    return lax.dot_general(a, b, (((ca,), (cb,)), ((), ())), preferred_element_type=F32)


def normed(v):
    centre = v - jnp.mean(v, axis=-1, keepdims=True)
    rstd = lax.rsqrt(jnp.mean(centre * centre, axis=-1, keepdims=True) + norm_eps)
    return centre * rstd, rstd


def norm_back(e, gain, xhat, rstd):
    eg = e * gain
    m1 = jnp.mean(eg, axis=-1, keepdims=True)
    m2 = jnp.mean(eg * xhat, axis=-1, keepdims=True)
    return rstd * (eg - m1 - xhat * m2)


def pad_rows(v, rows):
    return jnp.concatenate([v, jnp.zeros((rows - v.shape[0], v.shape[1]), v.dtype)], axis=0)


def load_columns(ref, r):
    return jnp.concatenate([ref[j, r, :] for j in range(ref.shape[0])], axis=1)


def store_columns(ref, r, v):
    for j in range(ref.shape[0]):
        ref[j, r, :] = v[:, 128 * j : 128 * j + 128]


class Place:
    def __init__(self):
        f = lax.axis_index("fsdp")
        self.x = lax.axis_index("tp")
        self.z = f // (NY * NCORE)
        self.y = lax.rem(f // NCORE, NY)
        self.c = lax.rem(f, NCORE)
        self.sib = self.at(self.z, self.y, 1 - self.c, self.x)
        self.peer_x = self.at(self.z, self.y, self.c, 1 - self.x)
        self.peer_y = self.at(self.z, 1 - self.y, self.c, self.x)
        self.other_z = [lax.rem(self.z + d, NZ) for d in range(1, NZ)]
        self.peers_z = [self.at(o, self.y, self.c, self.x) for o in self.other_z]
        self.lanes = pl.ds(pl.multiple_of(self.x * HALF, HALF), HALF)
        self.lanes_other = pl.ds(pl.multiple_of((1 - self.x) * HALF, HALF), HALF)

    def pick(self, v):
        return jnp.where(self.x == 0, v[..., :HALF], v[..., HALF:])

    def at(self, z, y, c, x):
        return {"fsdp": (z * NY + y) * NCORE + c, "tp": x}

    def barrier(self):
        sem = pltpu.get_barrier_semaphore()
        everyone = [self.sib, self.peer_x, self.peer_y] + self.peers_z
        for d in everyone:
            pl.semaphore_signal(sem, inc=1, device_id=d, device_id_type=MESH_IDS)
        pl.semaphore_wait(sem, len(everyone))


def remote(src, dst, send, recv, device):
    return pltpu.make_async_remote_copy(
        src_ref=src, dst_ref=dst, send_sem=send, recv_sem=recv, device_id=device, device_id_type=MESH_IDS
    )


def start_all(copies):
    for k in copies:
        k.start()


def wait_all(copies):
    for k in copies:
        k.wait()


AG_SEMS = 7


def gather_steps(at, buf, own, send, recv, local, y_first):
    x, y, z, c, lanes = at.x, at.y, at.z, at.c, at.lanes
    mine = buf.at[z, y, c, :, lanes]
    keep = pltpu.make_async_copy(own, mine, local)
    s0 = [remote(own, mine, send.at[d], recv.at[d], at.peers_z[d]) for d in range(NZ - 1)]
    line = buf.at[:, y, c, :, lanes]
    s1 = remote(line, line, send.at[3], recv.at[3], at.peer_y if y_first else at.peer_x)
    if y_first:
        plane, rest = buf.at[:, :, c, :, lanes], buf.at[:, :, c, :, at.lanes_other]
    else:
        plane, rest = buf.at[:, y, c], buf.at[:, 1 - y, c]
    s2 = remote(plane, plane, send.at[4], recv.at[4], at.peer_x if y_first else at.peer_y)
    sib_a = remote(plane, plane, send.at[5], recv.at[5], at.sib)
    sib_b = remote(rest, rest, send.at[6], recv.at[6], at.sib)

    def step0():
        keep.start()
        start_all(s0)

    def step1():
        keep.wait()
        wait_all(s0)
        s1.start()

    def step2():
        s1.wait()
        s2.start()
        sib_a.start()

    def step3():
        s2.wait()
        sib_b.start()

    def step4():
        sib_a.wait()
        sib_b.wait()

    return [step0, step1, step2, step3, step4]


RS_SEMS = 6


def scatter_steps(at, grad, r0, r1, r2, r3, out, send, recv, x_first):
    x, y, z, c = at.x, at.y, at.z, at.c
    s0 = remote(grad.at[:, :, 1 - c], r0, send.at[0], recv.at[0], at.sib)
    if x_first:
        s1 = remote(r0.at[:, :, :, at.lanes_other], r1, send.at[1], recv.at[1], at.peer_x)
        s2 = remote(r1.at[:, 1 - y], r2, send.at[2], recv.at[2], at.peer_y)
    else:
        s1 = remote(r0.at[:, 1 - y], r1, send.at[1], recv.at[1], at.peer_y)
        s2 = remote(r1.at[:, :, at.lanes_other], r2, send.at[2], recv.at[2], at.peer_x)
    s3 = [
        remote(r2.at[at.other_z[d]], r3.at[d], send.at[3 + d], recv.at[3 + d], at.peers_z[d])
        for d in range(NZ - 1)
    ]

    def add(a, b):
        return (a.astype(F32) + b.astype(F32)).astype(BF16)

    def step0():
        s0.start()

    def step1():
        s0.wait()

        def body(k, _):
            r0[k] = add(r0[k], grad[k, :, c])
            return 0

        lax.fori_loop(0, NZ, body, 0)
        s1.start()

    def step2():
        s1.wait()

        def body(k, _):
            r1[k] = add(r1[k], at.pick(r0[k]) if x_first else r0[k, y])
            return 0

        lax.fori_loop(0, NZ, body, 0)
        s2.start()

    def step3():
        s2.wait()

        def body(k, _):
            r2[k] = add(r2[k], r1[k, y] if x_first else at.pick(r1[k]))
            return 0

        lax.fori_loop(0, NZ, body, 0)
        start_all(s3)

    def step4():
        wait_all(s3)
        total = r2[z].astype(F32)
        for d in range(NZ - 1):
            total = total + r3[d].astype(F32)
        out[...] = total

    return [step0, step1, step2, step3, step4]


def scatter_scratch(chunks, rows):
    wide = NTP * HALF
    return [
        pltpu.VMEM((chunks, 2, NZ, NY, rows, wide), BF16),
        pltpu.VMEM((chunks, NZ, NY, rows, HALF), BF16),
        pltpu.VMEM((chunks, NZ, rows, wide), BF16),
        pltpu.VMEM((chunks, 2, NZ, rows, HALF), BF16),
        pltpu.VMEM((chunks, 2, NZ - 1, rows, HALF), BF16),
        pltpu.SemaphoreType.DMA((chunks, 2, RS_SEMS)),
        pltpu.SemaphoreType.DMA((chunks, 2, RS_SEMS)),
    ]


def scatter_both(at, k, grads, scratch, outs):
    r0, r1a, r1b, r2, r3, send, recv = scratch
    first = scatter_steps(
        at, grads[0], r0.at[k, 0], r1a.at[k], r2.at[k, 0], r3.at[k, 0], outs[0], send.at[k, 0], recv.at[k, 0], True
    )
    second = scatter_steps(
        at, grads[1], r0.at[k, 1], r1b.at[k], r2.at[k, 1], r3.at[k, 1], outs[1], send.at[k, 1], recv.at[k, 1], False
    )
    return [both(a, b) for a, b in zip(first, second)]


def both(a, b):
    def run():
        a()
        b()

    return run


def gather_both(at, buf, own, sems):
    send, recv, local = sems
    first = gather_steps(at, buf.at[0], own.at[0], send.at[0], recv.at[0], local.at[0], True)
    second = gather_steps(at, buf.at[1], own.at[1], send.at[1], recv.at[1], local.at[1], False)
    return [both(a, b) for a, b in zip(first, second)]


def run_slot(plan, key, counters):
    for want, steps in plan.get(key, {}).items():
        cond = None
        for have, value in zip(counters, want):
            test = have == value
            cond = test if cond is None else jnp.logical_and(cond, test)

        def go(steps=steps):
            for s in steps:
                s()

        pl.when(cond)(go)


def planned(entries):
    plan = {}
    for key, want, step in entries:
        plan.setdefault(key, {}).setdefault(want, []).append(step)
    return plan


def matrix(ref):
    v = ref[...]
    return v.reshape(v.shape[0] * v.shape[1] * v.shape[2] * v.shape[3], v.shape[4])


def left_half(rows):
    return lax.broadcasted_iota(jnp.int32, (rows, 2 * HEAD_DIM), 1) < HEAD_DIM


def split_heads(v, left):
    zero = jnp.zeros_like(v)
    return jnp.concatenate([jnp.where(left, v, zero), jnp.where(left, zero, v)], axis=0)


def projection(a, b):
    return jnp.concatenate([a, b[:, 0:128], b[:, HALF : HALF + 128]], axis=1)


def out_columns(b):
    return jnp.concatenate([b[:, 128:HALF], b[:, HALF + 128 :]], axis=1)


def spread(pieces, width, row, total):
    col = lax.broadcasted_iota(jnp.int32, (128, total), 1).astype(F32)
    lane = lax.broadcasted_iota(jnp.int32, (128, total), 0).astype(F32)
    owner = jnp.floor((col + 0.5) * (1.0 / width))
    pick = (col - owner * width == lane).astype(BF16)
    spreaded = dot(pieces.astype(BF16), pick, 1, 0)
    at_row = lax.broadcasted_iota(jnp.int32, spreaded.shape, 0).astype(F32)
    col = lax.broadcasted_iota(jnp.int32, spreaded.shape, 1).astype(F32)
    owner = jnp.floor((col + 0.5) * (1.0 / width))
    return jnp.sum(jnp.where(at_row == owner * 8.0 + row, spreaded, 0.0), axis=0, keepdims=True)


def attention_kernel(
    dims,
    x_hbm, norm_ref, bout_ref, wqkv_ref, wout_ref, wfc1_ref, wfc2_ref, bqv_ref, bfc1_ref,
    qkv_hbm, ctx_hbm, mid_hbm, p_hbm, watt_hbm, wff_hbm, own_hbm, bias_ref,
    x_s, h1, qkv_s, ctx_s, mid_s, p_s, watt, own, pieces, bias_s,
    ag_send, ag_recv, ag_local, sm_send, sm_recv, out_sem, in_sem,
):
    images, seq, sp, groups, chunks, early = dims
    at = Place()
    x_copy = pltpu.make_async_copy(x_hbm, x_s, in_sem.at[0])
    x_copy.start()
    own_rows = wqkv_ref.shape[2]
    rows = images * seq
    for g in range(groups):
        cols = slice(128 * g, 128 * g + 128)
        own[g, 0] = jnp.concatenate([wqkv_ref[0, :, cols], wqkv_ref[1, :, cols]], axis=1).astype(BF16)
        own[g, 1] = jnp.concatenate([wqkv_ref[2, :, cols], wout_ref[:, cols]], axis=1).astype(BF16)
    pieces[at.x, at.z, at.y, at.c] = jnp.zeros((8, 128), F32)
    pieces[at.x, at.z, at.y, at.c, 0:1, 0 : bfc1_ref.shape[1]] = bfc1_ref[...]
    pieces[at.x, at.z, at.y, at.c, 1:3, 0 : bqv_ref.shape[1]] = bqv_ref[...]

    def sems(k):
        return ag_send.at[k], ag_recv.at[k], ag_local.at[k]

    steps = [gather_both(at, watt.at[g], own.at[g], sems(g)) for g in range(groups)]
    steps += [gather_both(at, wff_hbm.at[f], own.at[groups + f], sems(groups + f)) for f in range(early)]
    here = pieces.at[at.x, at.z, at.y, at.c]
    line = pieces.at[at.x, :, at.y, at.c]
    plane = pieces.at[at.x, :, :, at.c]
    cube = pieces.at[:, :, :, at.c]
    bias_steps = [[remote(here, here, sm_send.at[d], sm_recv.at[d], at.peers_z[d]) for d in range(NZ - 1)]]
    bias_steps += [
        [remote(r, r, sm_send.at[3 + k], sm_recv.at[3 + k], d)]
        for k, (r, d) in enumerate([(line, at.peer_y), (plane, at.peer_x), (cube, at.sib)])
    ]

    at.barrier()
    steps[0][0]()
    start_all(bias_steps[0])
    steps[1][0]()
    for f in range(chunks - groups):
        cols = slice(HALF * f, HALF * f + HALF)
        own[groups + f, 0] = wfc1_ref[:, cols].astype(BF16)
        own[groups + f, 1] = wfc2_ref[:, cols].astype(BF16)
    late = pltpu.make_async_copy(own.at[pl.ds(groups + early, chunks - groups - early)], own_hbm, in_sem.at[1])
    late.start()
    x_copy.wait()

    block = rows // 7

    def first_norm(j, _):
        r = pl.ds(pl.multiple_of(j * block, 16), block)
        xhat, _r = normed(x_s[r, :].astype(F32))
        store_columns(mid_s, r, xhat * norm_ref[0:1, :] + norm_ref[1:2, :])
        return 0

    def by_image(i, _):
        h = pad_rows(load_columns(mid_s, pl.ds(i, seq, stride=images)), sp)
        h1[pl.ds(pl.multiple_of(i * sp, 16), sp), :] = h.astype(BF16)
        return 0

    lax.fori_loop(0, 7, first_norm, 0)
    steps[0][1]()
    wait_all(bias_steps[0])
    start_all(bias_steps[1])
    steps[2][0]()
    lax.fori_loop(0, images, by_image, 0)
    steps[0][2]()
    wait_all(bias_steps[1])
    start_all(bias_steps[2])
    steps[1][1]()
    steps[0][3]()
    wait_all(bias_steps[2])
    start_all(bias_steps[3])
    steps[1][2]()
    wait_all(bias_steps[3])
    flat = pieces[...].reshape(NTP * NZ * NY * NCORE * 8, 128)
    width = bqv_ref.shape[1]
    model = width * NTP * NZ * NY * NCORE
    bias_q = spread(flat, width, 1.0, model)
    bias_v = spread(flat, width, 2.0, model)
    for g in range(groups):
        parts = []
        for t in range(NTP):
            parts += [bias_q[:, t * own_rows + 128 * g : t * own_rows + 128 * g + 128], jnp.zeros((1, 128), F32)]
        for t in range(NTP):
            parts.append(bias_v[:, t * own_rows + 128 * g : t * own_rows + 128 * g + 128])
        bias_s[g] = jnp.concatenate(parts, axis=1)
    width = bfc1_ref.shape[1]
    bias_ff = spread(flat, width, 0.0, width * NTP * NZ * NY * NCORE)
    per = bias_ff.shape[1] // NTP
    for f in range(chunks - groups):
        bias_ref[f] = jnp.concatenate(
            [bias_ff[:, t * per + f * HALF : t * per + f * HALF + HALF] for t in range(NTP)], axis=1
        )
    steps[0][4]()

    when = {1: [None, None, None, (0, 1), (1, 0)], 2: [None, (0, 1), (0, 3), (1, 1), (2, 0)]}
    place = [[(0, 3), (1, 1), (1, 3), (2, 1), (2, 3)], [(1, 2), (2, 0), (2, 2), (3, 0), (3, 2)]]
    for f in range(early):
        when[groups + f] = place[f]
    plan = planned(
        [("out" if w[0] == groups else "tile", w[1:] if w[0] == groups else w, steps[k][s])
         for k, ws in when.items() for s, w in enumerate(ws) if w is not None]
    )

    pair = 2
    tr = pair * sp
    left = left_half(sp)
    live_key = lax.broadcasted_iota(jnp.int32, (sp, sp), 0) < seq
    tiles = images // pair

    def group(g, _):
        def tile(i, _):
            run_slot(plan, "tile", (g, i))
            r = pl.ds(pl.multiple_of(i * tr, 16), tr)
            w = projection(matrix(watt.at[g, 0]), matrix(watt.at[g, 1]))
            qkv = (dot(h1[r, :], w, 1, 0) + bias_s[g]).astype(BF16)
            qkv_s[g, r, :] = qkv
            for a in range(pair):
                part = qkv[a * sp : (a + 1) * sp]
                for t in range(NTP):
                    q = part[:, t * HALF : t * HALF + 128] * jnp.asarray(HEAD_DIM ** (-0.5), BF16)
                    k = part[:, t * HALF + 128 : t * HALF + HALF]
                    v = part[:, 2 * HALF + t * 128 : 2 * HALF + t * 128 + 128]
                    st = dot(split_heads(k, left), q, 1, 1)
                    vt = v.T
                    cs = []
                    for h in range(2):
                        s = jnp.where(live_key, st[h * sp : (h + 1) * sp], NEG)
                        e = jnp.exp(s - jnp.max(s, axis=0, keepdims=True))
                        p = (e * (1.0 / jnp.sum(e, axis=0, keepdims=True))).astype(BF16)
                        p_s[g, i * pair + a, t, h] = jnp.concatenate([p, jnp.zeros((sp, LANES - sp), BF16)], axis=1)
                        cs.append(dot(vt[h * HEAD_DIM : (h + 1) * HEAD_DIM], p, 1, 0))
                    c2 = jnp.concatenate(cs, axis=0).T.astype(BF16)
                    ctx_s[g, pl.ds(pl.multiple_of(i * tr + a * sp, 16), sp), t * 128 : (t + 1) * 128] = c2
            pltpu.make_async_copy(qkv_s.at[g, r], qkv_hbm.at[g, r], out_sem.at[0, g, i]).start()
            pltpu.make_async_copy(ctx_s.at[g, r], ctx_hbm.at[g, r], out_sem.at[1, g, i]).start()
            im = pl.ds(i * pair, pair)
            pltpu.make_async_copy(p_s.at[g, im], p_hbm.at[g, im], out_sem.at[2, g, i]).start()
            return 0

        lax.fori_loop(0, tiles, tile, 0)
        pltpu.make_async_copy(watt.at[g], watt_hbm.at[g], in_sem.at[2 + g]).start()
        return 0

    lax.fori_loop(0, groups, group, 0)

    def project_out(i, _):
        run_slot(plan, "out", (i,))
        r = pl.ds(pl.multiple_of(i * tr, 16), tr)
        w = jnp.concatenate([out_columns(matrix(watt.at[g, 1])) for g in range(groups)], axis=1)
        c = jnp.concatenate([ctx_s[g, r, :] for g in range(groups)], axis=1)
        attn = dot(c, w, 1, 1)
        for a in range(pair):
            store_columns(mid_s, pl.ds(i * pair + a, seq, stride=images), attn[a * sp : a * sp + seq])
        return 0

    lax.fori_loop(0, tiles, project_out, 0)

    def residual(j, _):
        r = pl.ds(pl.multiple_of(j * block, 16), block)
        store_columns(mid_s, r, load_columns(mid_s, r) + x_s[r, :].astype(F32) + bout_ref[0:1, :])
        pltpu.make_async_copy(mid_s.at[:, r], mid_hbm.at[:, r], out_sem.at[3, 0, j]).start()
        return 0

    lax.fori_loop(0, 7, residual, 0)

    def drain(k, _):
        g, i = k // tiles, lax.rem(k, tiles)
        r = pl.ds(pl.multiple_of(i * tr, 16), tr)
        pltpu.make_async_copy(qkv_s.at[g, r], qkv_hbm.at[g, r], out_sem.at[0, g, i]).wait()
        pltpu.make_async_copy(ctx_s.at[g, r], ctx_hbm.at[g, r], out_sem.at[1, g, i]).wait()
        im = pl.ds(i * pair, pair)
        pltpu.make_async_copy(p_s.at[g, im], p_hbm.at[g, im], out_sem.at[2, g, i]).wait()
        return 0

    lax.fori_loop(0, groups * tiles, drain, 0)
    for g in range(groups):
        pltpu.make_async_copy(watt.at[g], watt_hbm.at[g], in_sem.at[2 + g]).wait()
    for j in range(7):
        r = pl.ds(j * block, block)
        pltpu.make_async_copy(mid_s.at[:, r], mid_hbm.at[:, r], out_sem.at[3, 0, j]).wait()
    late.wait()


def feed_forward_kernel(
    dims,
    counts_ref, norm_ref, bout_ref, bias_ref, mid_hbm, og_hbm, wff_hbm, own_hbm,
    bo_hbm, dmid_hbm, late_hbm, sums_ref, b1g_ref, gff_ref,
    wff, own, h2, h2t, dm, dmt, mlp, dh2, act, dpre, grad, mid_s,
    r0, r1a, r1b, r2, r3, rs_send, rs_recv,
    ag_send, ag_recv, ag_local, in_sem, mid_sem, out_sem,
):
    images, seq, sp, chunks, early, summed = dims
    rows = images * seq
    padded = h2.shape[0]
    block = rows // 7
    at = Place()
    og_copy = pltpu.make_async_copy(og_hbm, dm.at[pl.ds(0, rows)], in_sem.at[0])
    own_copy = pltpu.make_async_copy(own_hbm, own, in_sem.at[1])
    w_copies = [pltpu.make_async_copy(wff_hbm.at[f], wff.at[f], in_sem.at[2 + f]) for f in range(early)]
    own_copy.start()
    og_copy.start()

    def mid_copy(i):
        r = pl.ds(pl.multiple_of(i * block, 16), block)
        return pltpu.make_async_copy(mid_hbm.at[:, r], mid_s.at[lax.rem(i, 3)], mid_sem.at[lax.rem(i, 3)])

    mid_copy(0).start()
    start_all(w_copies)
    late = chunks - early
    gather = {
        early + k: gather_both(
            at, wff.at[early + k], own.at[k], (ag_send.at[k], ag_recv.at[k], ag_local.at[k])
        )
        for k in range(late)
    }
    scratch = (r0, r1a, r1b, r2, r3, rs_send, rs_recv)
    scatter = [
        scatter_both(
            at, k, (grad.at[k % 2, 0], grad.at[k % 2, 1]), scratch, (gff_ref.at[k, 0], gff_ref.at[k, 1])
        )
        for k in range(summed)
    ]
    at.barrier()
    own_copy.wait()
    gather[early][0]()
    og_copy.wait()
    count = counts_ref[0]

    first = at.x * images
    image = lax.rem(lax.broadcasted_iota(jnp.int32, (block, 1), 0), images) + first
    live = jnp.where(image < count, 1.0, 0.0).astype(F32)

    def second_norm(i, _):
        pl.when(i + 1 < 7)(lambda: mid_copy(i + 1).start())
        mid_copy(i).wait()
        r = pl.ds(pl.multiple_of(i * block, 16), block)
        xhat, _r = normed(load_columns(mid_s.at[lax.rem(i, 3)], slice(None)))
        h2[r, :] = (xhat * norm_ref[2:3, :] + norm_ref[3:4, :]).astype(BF16)
        dm[r, :] = (dm[r, :].astype(F32) * live).astype(BF16)
        mlp[r, :] = jnp.zeros((block, mlp.shape[1]), F32)
        dh2[r, :] = jnp.zeros((block, mlp.shape[1]), F32)
        return 0

    rest = pl.ds(rows, padded - rows)
    for ref in (h2, dm, act, dpre):
        ref[rest, :] = jnp.zeros((padded - rows, ref.shape[1]), BF16)
    lax.fori_loop(0, 7, second_norm, 0)
    gather[early][1]()
    gather[early + 1][0]()

    def turn(j, _):
        r = pl.ds(pl.multiple_of(j * 128, 128), 128)
        h2t[:, r] = h2[r, :].T
        dmt[:, r] = dm[r, :].T
        return 0

    lax.fori_loop(0, padded // 128, turn, 0)
    wait_all(w_copies)

    entries = []
    for k in range(late):
        first = 4 * (early + k)
        slots = [max(0, first - 11), max(0, first - 8), first - 6, first - 3, first]
        for s in range(5):
            if not (k == 0 and s < 2) and not (k == 1 and s < 1):
                entries.append((slots[s], gather[early + k][s]))
    for k in range(summed):
        for s, lag in enumerate((4, 6, 8, 10, 13)):
            entries.append((4 * k + lag, scatter[k][s]))
    entries.sort(key=lambda e: e[0])
    plan = planned([(slot % 4, (slot // 4,), step) for slot, step in entries if slot < 4 * chunks])
    tail = [step for slot, step in entries if slot >= 4 * chunks]

    def chunk(f, _):
        b1 = bias_ref[f]
        for i in range(2):
            run_slot(plan, i, (f,))
            r = pl.ds(i * (rows // 2), rows // 2)
            w1, w2 = matrix(wff.at[f, 0]), matrix(wff.at[f, 1])
            pre = dot(h2[r, :], w1, 1, 0) + b1
            phi = 0.5 + 0.5 * lax.erf(pre * 0.7071067811865476)
            a = (pre * phi).astype(BF16)
            slope = phi + pre * (jnp.exp(-0.5 * pre * pre) * 0.3989422804014327)
            d = (dot(dm[r, :], w2, 1, 0) * slope).astype(BF16)
            act[r, :] = a
            dpre[r, :] = d
            mlp[r, :] += dot(a, w2, 1, 1)
            dh2[r, :] += dot(d, w1, 1, 1)
        slot = lax.rem(f, 2)
        shape = grad.shape[2:]
        run_slot(plan, 2, (f,))
        b1g_ref[f] = jnp.sum(dpre[...].astype(F32), axis=0, keepdims=True)
        grad[slot, 0] = dot(h2t[...], dpre[...], 1, 0).astype(BF16).reshape(shape)
        run_slot(plan, 3, (f,))
        grad[slot, 1] = dot(dmt[...], act[...], 1, 0).astype(BF16).reshape(shape)

        def keep(k):
            pltpu.make_async_copy(grad.at[k % 2], late_hbm.at[k - summed], out_sem.at[k - summed]).start()

        for k in range(summed, chunks):
            pl.when(f == k)(functools.partial(keep, k))
        return 0

    lax.fori_loop(0, chunks, chunk, 0)
    mid_copy(0).start()

    def dmid_copy(i):
        r = pl.ds(pl.multiple_of(i * block, 16), block)
        return pltpu.make_async_copy(mid_s.at[lax.rem(i, 3)], dmid_hbm.at[:, r], out_sem.at[16 + lax.rem(i, 3)])

    def second_norm_back(i, acc):
        pl.when(i >= 2)(lambda: dmid_copy(i - 2).wait())
        pl.when(i + 1 < 7)(lambda: mid_copy(i + 1).start())
        mid_copy(i).wait()
        r = pl.ds(pl.multiple_of(i * block, 16), block)
        mid = load_columns(mid_s.at[lax.rem(i, 3)], slice(None))
        xhat, rstd = normed(mid)
        h2[r, :] = (mid + mlp[r, :] + bout_ref[1:2, :]).astype(BF16)
        e = dh2[r, :]
        live = dm[r, :].astype(F32)
        d = live + norm_back(e, norm_ref[2:3, :], xhat, rstd)
        store_columns(mid_s.at[lax.rem(i, 3)], slice(None), d)
        pltpu.make_async_copy(h2.at[r], bo_hbm.at[r], out_sem.at[8 + i]).start()
        dmid_copy(i).start()
        terms = (e * xhat, e, d, live)
        return tuple(a + jnp.sum(t, axis=0, keepdims=True) for a, t in zip(acc, terms))

    zero = jnp.zeros((1, mlp.shape[1]), F32)
    acc = lax.fori_loop(0, 7, second_norm_back, (zero,) * 4)
    sums_ref[...] = jnp.zeros(sums_ref.shape, F32)
    for k in range(4):
        sums_ref[k : k + 1, :] = acc[k]
    for step in tail:
        step()

    for i in range(7):
        r = pl.ds(i * block, block)
        pltpu.make_async_copy(h2.at[r], bo_hbm.at[r], out_sem.at[8 + i]).wait()
    dmid_copy(5).wait()
    dmid_copy(6).wait()
    for k in range(summed, chunks):
        pltpu.make_async_copy(grad.at[k % 2], late_hbm.at[k - summed], out_sem.at[k - summed]).wait()


def attention_back_kernel(
    dims,
    norm_ref, sums_ref, b1g_ref, x_hbm, dmid_hbm, late_hbm, watt_hbm, qkv_hbm, ctx_hbm, p_hbm,
    gt_hbm, glate_ref, gatt_ref, small_ref,
    dattn, h1t, dh1, dqkv, watt, qkv_s, ctx_s, ctxt, p_s, grad, x_s, dmid_s, gt_s, bias_s,
    small, small_z,
    r0, r1a, r1b, r2, r3, rs_send, rs_recv, sm_send, sm_recv,
    in_sem, ctx_sem, tile_sem, dmid_sem, gt_sem,
):
    images, seq, sp, groups, chunks, held = dims
    rows = images * seq
    block = rows // 7
    model = x_s.shape[1]
    pair = 2
    tr = pair * sp
    tiles = images // pair
    at = Place()
    dmid_in = pltpu.make_async_copy(dmid_hbm, dh1, in_sem.at[0])
    watt_copy = pltpu.make_async_copy(watt_hbm, watt, in_sem.at[1])
    x_copy = pltpu.make_async_copy(x_hbm, x_s, in_sem.at[2])
    late_copies = [pltpu.make_async_copy(late_hbm.at[k], grad.at[k], in_sem.at[3 + k]) for k in range(held)]

    def dmid_copy(i):
        r = pl.ds(pl.multiple_of(i * block, 16), block)
        return pltpu.make_async_copy(dmid_hbm.at[:, r], dmid_s.at[lax.rem(i, 2)], dmid_sem.at[lax.rem(i, 2)])

    def ctx_copy(g):
        return pltpu.make_async_copy(ctx_hbm.at[g], ctx_s.at[lax.rem(g, 2)], ctx_sem.at[lax.rem(g, 2)])

    def tile_copies(g, i):
        r, im = pl.ds(pl.multiple_of(i * tr, 16), tr), pl.ds(i * pair, pair)
        return [
            pltpu.make_async_copy(qkv_hbm.at[g, r], qkv_s.at[r], tile_sem.at[0, i]),
            pltpu.make_async_copy(p_hbm.at[g, im], p_s.at[im], tile_sem.at[1, i]),
        ]

    late_copies[0].start()
    dmid_in.start()
    x_copy.start()
    watt_copy.start()
    start_all(late_copies[1:])
    ctx_copy(0).start()
    for i in range(tiles):
        start_all(tile_copies(0, i))
    scratch = (r0, r1a, r1b, r2, r3, rs_send, rs_recv)
    scatter = [
        scatter_both(at, k, (grad.at[k, 0], grad.at[k, 1]), scratch, (glate_ref.at[k, 0], glate_ref.at[k, 1]))
        for k in range(held)
    ]
    for g in range(groups):
        scatter.append(
            scatter_both(
                at, held + g, (grad.at[(held + g) % 2, 0], grad.at[(held + g) % 2, 1]), scratch, (gatt_ref.at[g, 0], gatt_ref.at[g, 1])
            )
        )
    own_z = small_z.at[at.z]
    sm = [
        remote(small.at[0], small.at[1], sm_send.at[0], sm_recv.at[0], at.sib),
        remote(small.at[2], small.at[3], sm_send.at[1], sm_recv.at[1], at.peer_x),
        remote(small.at[4], small.at[5], sm_send.at[2], sm_recv.at[2], at.peer_y),
    ]
    sm_z = [remote(own_z, own_z, sm_send.at[3 + d], sm_recv.at[3 + d], at.peers_z[d]) for d in range(NZ - 1)]
    at.barrier()
    late_copies[0].wait()
    scatter[0][0]()

    dmid_in.wait()

    def take_dattn(i, _):
        d = pad_rows(load_columns(dh1, pl.ds(i, seq, stride=images)), sp)
        dattn[pl.ds(pl.multiple_of(i * sp, 16), sp), :] = d.astype(BF16)
        return 0

    lax.fori_loop(0, images, take_dattn, 0)
    x_copy.wait()

    def first_norm(j, _):
        r = pl.ds(pl.multiple_of(j * block, 16), block)
        xhat, _r = normed(x_s[r, :].astype(F32))
        store_columns(dh1, r, xhat * norm_ref[0:1, :] + norm_ref[1:2, :])
        return 0

    lax.fori_loop(0, 7, first_norm, 0)

    def by_image(i, _):
        h = pad_rows(load_columns(dh1, pl.ds(i, seq, stride=images)), sp)
        dqkv[pl.ds(pl.multiple_of(i * sp, 16), sp), :] = h.astype(BF16)
        return 0

    lax.fori_loop(0, images, by_image, 0)

    def turn(j, _):
        r = pl.ds(pl.multiple_of(j * 128, 128), 128)
        h1t[:, r] = dqkv[r, :].T
        return 0

    lax.fori_loop(0, images * sp // 128, turn, 0)
    dh1[...] = jnp.zeros(dh1.shape, F32)
    watt_copy.wait()
    wait_all(late_copies[1:])

    entries = [(s, scatter[0][k]) for k, s in ((1, 0), (2, 2), (3, 4), (4, 7))]
    for j in range(1, held):
        entries += [(2 + s, scatter[j][k]) for k, s in enumerate((0, 2, 4, 6, 9))]
    for g in range(groups - 1):
        entries += [(6 * (g + 1) + s, scatter[held + g][k]) for k, s in enumerate((0, 1, 3, 5, 7))]
    last = scatter[held + groups - 1]
    entries.sort(key=lambda e: e[0])
    plan = planned(
        [("tile" if s % 6 < 4 else s % 6, (s // 6, s % 6) if s % 6 < 4 else (s // 6,), step)
         for s, step in entries if s < 6 * groups]
    )
    tail = [step for s, step in entries if s >= 6 * groups]

    left = left_half(sp)
    scale = HEAD_DIM ** (-0.5)

    def group(g, _):
        pl.when(g + 1 < groups)(lambda: ctx_copy(g + 1).start())
        slot = lax.rem(g, 2)
        keep = lax.rem(held + g, 2)

        def tile(i, acc):
            wait_all(tile_copies(g, i))
            run_slot(plan, "tile", (g, i))
            r = pl.ds(pl.multiple_of(i * tr, 16), tr)
            wa, wb = matrix(watt.at[g, 0]), matrix(watt.at[g, 1])
            dc = dot(dattn[r, :], out_columns(wb), 1, 0).astype(BF16)
            qkv = qkv_s[r, :]
            blocks = []
            for a in range(pair):
                part = qkv[a * sp : (a + 1) * sp]
                dqs, dks, dvs = [], [], []
                for t in range(NTP):
                    q = part[:, t * HALF : t * HALF + 128] * jnp.asarray(scale, BF16)
                    k = part[:, t * HALF + 128 : t * HALF + HALF]
                    v = part[:, 2 * HALF + t * 128 : 2 * HALF + t * 128 + 128]
                    dcx = dc[a * sp : (a + 1) * sp, t * 128 : (t + 1) * 128]
                    dp = dot(split_heads(v, left), dcx, 1, 1)
                    kt = k.T
                    dqt, ds, ps = [], [], []
                    for h in range(2):
                        low = p_s[i * pair + a, t, h][:, :sp]
                        p = low.astype(F32)
                        pd = p * dp[h * sp : (h + 1) * sp]
                        s = (pd - p * jnp.sum(pd, axis=0, keepdims=True)).astype(BF16)
                        ds.append(s)
                        ps.append(low)
                        dqt.append(dot(kt[h * HEAD_DIM : (h + 1) * HEAD_DIM], s, 1, 0))
                    dqs.append(jnp.concatenate(dqt, axis=0).T * scale)
                    dk = dot(jnp.concatenate(ds, axis=0), q, 1, 0)
                    dks.append(jnp.where(left, dk[:sp], dk[sp:]))
                    dv = dot(jnp.concatenate(ps, axis=0), dcx, 1, 0)
                    dvs.append(jnp.where(left, dv[:sp], dv[sp:]))
                blocks.append(jnp.concatenate([dqs[0], dks[0], dqs[1], dks[1], dvs[0], dvs[1]], axis=1))
            d = jnp.concatenate(blocks, axis=0).astype(BF16)
            dqkv[r, :] = d
            back = dot(d, projection(wa, wb), 1, 1)
            for a in range(pair):
                mine = pl.ds(i * pair + a, seq, stride=images)
                store_columns(dh1, mine, load_columns(dh1, mine) + back[a * sp : a * sp + seq])
            pl.when(g + 1 < groups)(lambda: start_all(tile_copies(g + 1, i)))
            return acc + jnp.sum(d.astype(F32), axis=0, keepdims=True)

        ctx_copy(g).wait()
        ctxt[...] = ctx_s[slot].T
        bias_s[g] = lax.fori_loop(0, images // pair, tile, jnp.zeros((1, model), F32))
        run_slot(plan, 4, (g,))
        shape = grad.shape[2:]
        gw = dot(h1t[...], dqkv[...], 1, 0).astype(BF16)
        grad[keep, 0] = gw[:, : 2 * HALF].reshape(shape)
        run_slot(plan, 5, (g,))
        go = dot(ctxt[...], dattn[...], 1, 0).T.astype(BF16)
        grad[keep, 1] = jnp.concatenate(
            [gw[:, 2 * HALF : 2 * HALF + 128], go[:, :128], gw[:, 2 * HALF + 128 :], go[:, 128:]], axis=1
        ).reshape(shape)
        return 0

    lax.fori_loop(0, groups, group, 0)
    last[0]()
    dmid_copy(0).start()

    def first_norm_back(i, acc):
        pl.when(i + 1 < 7)(lambda: dmid_copy(i + 1).start())
        dmid_copy(i).wait()
        r = pl.ds(pl.multiple_of(i * block, 16), block)
        xhat, rstd = normed(x_s[r, :].astype(F32))
        e = load_columns(dh1, r)
        d = load_columns(dmid_s.at[lax.rem(i, 2)], slice(None))
        gt_s[i] = d + norm_back(e, norm_ref[0:1, :], xhat, rstd)
        pltpu.make_async_copy(gt_s.at[i], gt_hbm.at[r], gt_sem.at[i]).start()
        return (acc[0] + jnp.sum(e * xhat, axis=0, keepdims=True), acc[1] + jnp.sum(e, axis=0, keepdims=True))

    zero = jnp.zeros((1, model), F32)
    acc = lax.fori_loop(0, 4, first_norm_back, (zero, zero))
    for step in tail:
        step()
    last[1]()
    acc = lax.fori_loop(4, 7, first_norm_back, acc)
    small[0] = jnp.zeros(small.shape[1:], F32)
    small[0, 0:1, :] = acc[0]
    small[0, 1:2, :] = acc[1]
    small[0, 2:6, :] = sums_ref[0:4, :]
    own_cols = groups * 128
    for g in range(groups):
        for t in range(NTP):
            cols = slice(t * own_cols + 128 * g, t * own_cols + 128 * g + 128)
            small[0, 6:7, cols] = bias_s[g, :, t * HALF : t * HALF + 128]
            small[0, 7:8, cols] = bias_s[g, :, 2 * HALF + t * 128 : 2 * HALF + t * 128 + 128]
    for f in range(chunks):
        for t in range(NTP):
            first = t * chunks * HALF + f * HALF
            row, col = 8 + first // model, first % model
            small[0, row : row + 1, col : col + HALF] = b1g_ref[f, :, t * HALF : t * HALF + HALF]
    sm[0].start()
    last[2]()
    sm[0].wait()
    small[2] = small[0] + small[1]
    sm[1].start()
    last[3]()
    sm[1].wait()
    small[4] = small[2] + small[3]
    sm[2].start()
    last[4]()
    sm[2].wait()
    small_z[at.z] = small[4] + small[5]
    start_all(sm_z)
    for i in range(7):
        r = pl.ds(i * block, block)
        pltpu.make_async_copy(gt_s.at[i], gt_hbm.at[r], gt_sem.at[i]).wait()
    wait_all(sm_z)
    total = small_z[0]
    for k in range(1, NZ):
        total = total + small_z[k]
    small_ref[...] = total


def step_kernel(dims, *refs):
    groups, chunks, held = dims
    names = ("norm", "qkv", "bqv", "out", "fc1", "bfc1", "fc2", "bout")
    gff_ref, glate_ref, gatt_ref, small_ref = refs[:4]
    n = len(names)
    ps, ms, vs = (dict(zip(names, refs[4 + k * n : 4 + (k + 1) * n])) for k in range(3))
    outs = refs[4 + 3 * n :]
    g_out, u_out, m_out, v_out = (dict(zip(names, outs[k * n : (k + 1) * n])) for k in range(4))
    late = chunks - held

    def ff(f, h):
        return gff_ref[f, h] if f < late else glate_ref[f - late, h]

    whole = {"qkv": True, "fc1": True, "fc2": True}
    decays = ("qkv", "out", "fc1", "fc2")

    def update(name, index, g):
        p = ps[name][index]
        u, m, v = adamw(p, g, ms[name][index], vs[name][index], decay_rate if name in decays else 0.0)
        g_out[name][index] = g
        u_out[name][index] = p + u if name in whole else u
        m_out[name][index] = m
        v_out[name][index] = v

    for c in range(3):
        gs = [gatt_ref[g, c // 2][:, (c % 2) * 128 : (c % 2) * 128 + 128] for g in range(groups)]
        update("qkv", c, jnp.concatenate(gs, axis=1))
    update("out", ..., jnp.concatenate([gatt_ref[g, 1][:, 128:] for g in range(groups)], axis=1))
    for f in range(chunks):
        cols = slice(f * HALF, (f + 1) * HALF)
        update("fc1", (slice(None), cols), ff(f, 0))
        update("fc2", (slice(None), cols), ff(f, 1))
    update("norm", ..., small_ref[0:4, :])
    update("bout", ..., small_ref[4:6, :])
    part = lax.axis_index("tp") * (NZ * NY * NCORE) + lax.axis_index("fsdp")
    width = ps["bqv"].shape[1]
    model = small_ref.shape[1]
    update("bqv", ..., pltpu.roll(small_ref[0:8, :], lax.rem(model - part * width, model), 1)[6:8, :width])
    width = ps["bfc1"].shape[1]
    per = model // width
    turned = pltpu.roll(small_ref[8:16, :], lax.rem(model - lax.rem(part, per) * width, model), 1)[:, :width]
    at_row = lax.broadcasted_iota(jnp.int32, turned.shape, 0)
    update("bfc1", ..., jnp.sum(jnp.where(at_row == part // per, turned, 0.0), axis=0, keepdims=True))


def sds(shape, dtype):
    return jax.ShapeDtypeStruct(shape, dtype)


def fused_device(
    tokens_in, out_grad, image_counts,
    norm_params, w_qkv, bias_qv, w_out, w_fc1, bias_fc1, w_fc2, bias_out,
    *moments,
):
    images, seq, model = tokens_in.shape
    sp = -(-seq // 16) * 16
    rows = images * sp
    own_rows, own_cols = w_qkv.shape[1], w_qkv.shape[2]
    groups = own_cols // 128
    chunks = w_fc1.shape[1] // HALF
    early, summed = 2, chunks - 2
    held = chunks - summed
    wide = NTP * HALF
    cube = (NZ, NY, NCORE, own_rows, wide)
    any_, vm, sm = pl.BlockSpec(memory_space=pl.ANY), pl.BlockSpec(memory_space=pltpu.VMEM), pl.BlockSpec(memory_space=pltpu.SMEM)
    dma = pltpu.SemaphoreType.DMA

    def params(k):
        return pltpu.CompilerParams(collective_id=k, has_side_effects=True, vmem_limit_bytes=VMEM_BYTES)

    n_ag = groups + early
    flat_rows = images * seq

    def by_token(a):
        return a.transpose(1, 0, 2).reshape(flat_rows, model)

    def by_image(a):
        return a.reshape(seq, images, model).transpose(1, 0, 2)

    x_rows, og_rows = by_token(tokens_in), by_token(out_grad)
    qkv, ctx, mid, p, watt, wff, own, bias1 = pl.pallas_call(
        functools.partial(attention_kernel, (images, seq, sp, groups, groups + chunks, early)),
        name="attention",
        in_specs=[any_] + [vm] * 8,
        out_specs=[any_] * 7 + [vm],
        out_shape=[
            sds((groups, rows, model), BF16), sds((groups, rows, HALF), BF16), sds((model // 128, flat_rows, 128), F32),
            sds((groups, images, NTP, 2, sp, LANES), BF16), sds((groups, 2) + cube, BF16), sds((early, 2) + cube, BF16),
            sds((chunks - early, 2, own_rows, HALF), BF16), sds((chunks, 1, wide), F32),
        ],
        scratch_shapes=[
            pltpu.VMEM((flat_rows, model), BF16), pltpu.VMEM((rows, model), BF16),
            pltpu.VMEM((groups, rows, model), BF16), pltpu.VMEM((groups, rows, HALF), BF16),
            pltpu.VMEM((model // 128, flat_rows, 128), F32), pltpu.VMEM((groups, images, NTP, 2, sp, LANES), BF16),
            pltpu.VMEM((groups, 2) + cube, BF16), pltpu.VMEM((groups + chunks, 2, own_rows, HALF), BF16),
            pltpu.VMEM((NTP, NZ, NY, NCORE, 8, 128), F32), pltpu.VMEM((groups, 1, model), F32),
            dma((n_ag, 2, AG_SEMS)), dma((n_ag, 2, AG_SEMS)), dma((n_ag, 2)), dma((6,)), dma((6,)),
            dma((4, groups, 8)), dma((2 + groups,)),
        ],
        compiler_params=params(0),
    )(x_rows, norm_params, bias_out, w_qkv, w_out.T, w_fc1, w_fc2.T, bias_qv, bias_fc1.reshape(1, -1))

    late = chunks - early
    bo, dmid, grad_late, sums, b1g, gff = pl.pallas_call(
        functools.partial(feed_forward_kernel, (images, seq, sp, chunks, early, summed)),
        name="feed_forward",
        in_specs=[sm, vm, vm, vm] + [any_] * 4,
        out_specs=[any_] * 3 + [vm] * 3,
        out_shape=[
            sds((flat_rows, model), BF16), sds((model // 128, flat_rows, 128), F32),
            sds((held, 2) + cube, BF16), sds((8, model), F32), sds((chunks, 1, wide), F32),
            sds((summed, 2, own_rows, HALF), F32),
        ],
        scratch_shapes=[
            pltpu.VMEM((chunks, 2) + cube, BF16), pltpu.VMEM((late, 2, own_rows, HALF), BF16),
            pltpu.VMEM((rows, model), BF16), pltpu.VMEM((model, rows), BF16),
            pltpu.VMEM((rows, model), BF16), pltpu.VMEM((model, rows), BF16),
            pltpu.VMEM((flat_rows, model), F32), pltpu.VMEM((flat_rows, model), F32),
            pltpu.VMEM((rows, wide), BF16), pltpu.VMEM((rows, wide), BF16),
            pltpu.VMEM((2, 2) + cube, BF16), pltpu.VMEM((3, model // 128, flat_rows // 7, 128), F32),
        ]
        + scatter_scratch(summed, own_rows)
        + [
            dma((late, 2, AG_SEMS)), dma((late, 2, AG_SEMS)), dma((late, 2)), dma((2 + early,)), dma((3,)),
            dma((24,)),
        ],
        compiler_params=params(1),
    )(image_counts, norm_params, bias_out, bias1, mid, og_rows, wff, own)

    gt, glate, gatt, small = pl.pallas_call(
        functools.partial(attention_back_kernel, (images, seq, sp, groups, chunks, held)),
        name="attention_back",
        in_specs=[vm] * 3 + [any_] * 7,
        out_specs=[any_] + [vm] * 3,
        out_shape=[
            sds((flat_rows, model), F32), sds((held, 2, own_rows, HALF), F32),
            sds((groups, 2, own_rows, HALF), F32), sds((16, model), F32),
        ],
        scratch_shapes=[
            pltpu.VMEM((rows, model), BF16), pltpu.VMEM((model, rows), BF16),
            pltpu.VMEM((model // 128, flat_rows, 128), F32), pltpu.VMEM((rows, model), BF16),
            pltpu.VMEM((groups, 2) + cube, BF16),
            pltpu.VMEM((rows, model), BF16), pltpu.VMEM((2, rows, HALF), BF16), pltpu.VMEM((HALF, rows), BF16),
            pltpu.VMEM((images, NTP, 2, sp, LANES), BF16), pltpu.VMEM((2, 2) + cube, BF16),
            pltpu.VMEM((flat_rows, model), BF16), pltpu.VMEM((2, model // 128, flat_rows // 7, 128), F32),
            pltpu.VMEM((7, flat_rows // 7, model), F32), pltpu.VMEM((groups, 1, model), F32),
            pltpu.VMEM((6, 16, model), F32), pltpu.VMEM((NZ, 16, model), F32),
        ]
        + scatter_scratch(held + groups, own_rows)
        + [dma((6,)), dma((6,)), dma((3 + held,)), dma((2,)), dma((2, images // 2)), dma((2,)), dma((8,))],
        compiler_params=params(2),
    )(norm_params, sums, b1g, x_rows, dmid, grad_late, watt, qkv, ctx, p)

    turned = (3, 6)

    def flat(a, k):
        return a.reshape(1, -1) if a.ndim == 1 else a.T if k in turned else a

    weights = [flat(a, k) for k, a in enumerate((norm_params, w_qkv, bias_qv, w_out, w_fc1, bias_fc1, w_fc2, bias_out))]
    moments = [flat(a, k % 8) for k, a in enumerate(moments)]
    shapes = [sds(a.shape, F32) for a in weights]
    outs = pl.pallas_call(
        functools.partial(step_kernel, (groups, chunks, held)),
        name="adamw_step",
        in_specs=[vm] * 28,
        out_specs=[vm] * 32,
        out_shape=shapes * 4,
        compiler_params=pltpu.CompilerParams(vmem_limit_bytes=VMEM_BYTES),
    )(gff, glate, gatt, small, *weights, *moments)
    outs = [o.reshape(-1) if k % 8 == 5 else o.T if k % 8 in turned else o for k, o in enumerate(outs)]
    return (by_image(bo), by_image(gt)) + tuple(outs)


def solution(mesh):
    placed = (
        P(("fsdp", "tp"), None, None),
        P(("fsdp", "tp"), None, None),
        P("fsdp"),
        P(),
        P(None, "fsdp", "tp"),
        P(None, ("tp", "fsdp")),
        P("tp", "fsdp"),
        P("fsdp", "tp"),
        P(("tp", "fsdp")),
        P("tp", "fsdp"),
        P(),
        P(),
        P(None, "fsdp", "tp"),
        P(None, ("tp", "fsdp")),
        P("tp", "fsdp"),
        P("fsdp", "tp"),
        P(("tp", "fsdp")),
        P("tp", "fsdp"),
        P(),
        P(),
        P(None, "fsdp", "tp"),
        P(None, ("tp", "fsdp")),
        P("tp", "fsdp"),
        P("fsdp", "tp"),
        P(("tp", "fsdp")),
        P("tp", "fsdp"),
        P(),
    )
    fits = mesh.shape["fsdp"] == NZ * NY * NCORE and mesh.shape["tp"] == NTP
    return jax.shard_map(
        fused_device if fits else per_device,
        mesh=mesh,
        in_specs=placed,
        out_specs=(
            P(("fsdp", "tp"), None, None),
            P(("fsdp", "tp"), None, None),
            P(),
            P(None, "fsdp", "tp"),
            P(None, ("tp", "fsdp")),
            P("tp", "fsdp"),
            P("fsdp", "tp"),
            P(("tp", "fsdp")),
            P("tp", "fsdp"),
            P(),
            P(),
            P(None, "fsdp", "tp"),
            P(None, ("tp", "fsdp")),
            P("tp", "fsdp"),
            P("fsdp", "tp"),
            P(("tp", "fsdp")),
            P("tp", "fsdp"),
            P(),
            P(),
            P(None, "fsdp", "tp"),
            P(None, ("tp", "fsdp")),
            P("tp", "fsdp"),
            P("fsdp", "tp"),
            P(("tp", "fsdp")),
            P("tp", "fsdp"),
            P(),
            P(),
            P(None, "fsdp", "tp"),
            P(None, ("tp", "fsdp")),
            P("tp", "fsdp"),
            P("fsdp", "tp"),
            P(("tp", "fsdp")),
            P("tp", "fsdp"),
            P(),
        ),
        check_vma=False,
    )
```

```python
import functools

import jax
import jax.numpy as jnp
from jax import lax
from jax.experimental import pallas as pl
from jax.experimental.pallas import tpu as pltpu
from jax.sharding import PartitionSpec as P

HEAD_DIM = 64
ADAM_STEP = 10


norm_eps = 1e-06
learn_rate = 0.02
beta_one = 0.9
beta_two = 0.999
adam_eps = 1e-08
decay_rate = 0.05


def layer_norm(rows_in, gain_vec, shift_vec):
    centre = rows_in - jnp.mean(rows_in, axis=-1, keepdims=True)
    spread = jnp.mean(centre * centre, axis=-1, keepdims=True)
    return centre * lax.rsqrt(spread + norm_eps) * gain_vec + shift_vec


def exact_gelu(rows_in):
    return jax.nn.gelu(rows_in, approximate=False)


def adamw(parameter, gradient, moment_one, moment_two, decay_on):
    one_new = beta_one * moment_one + (1.0 - beta_one) * gradient
    two_new = beta_two * moment_two + (1.0 - beta_two) * gradient * gradient
    one_hat = one_new / (1.0 - beta_one**ADAM_STEP)
    two_hat = two_new / (1.0 - beta_two**ADAM_STEP)
    update = one_hat / (jnp.sqrt(two_hat) + adam_eps) + decay_on * parameter
    return (-learn_rate * update, one_new, two_new)


def per_device(
    tokens_in,
    out_grad,
    image_counts,
    norm_params,
    w_qkv,
    bias_qv,
    w_out,
    w_fc1,
    bias_fc1,
    w_fc2,
    bias_out,
    first_norm,
    first_qkv,
    first_bias_qv,
    first_out,
    first_fc1,
    first_bias_fc1,
    first_fc2,
    first_bias_out,
    second_norm,
    second_qkv,
    second_bias_qv,
    second_out,
    second_fc1,
    second_bias_fc1,
    second_fc2,
    second_bias_out,
):
    images = tokens_in.shape[0]
    seq_len = tokens_in.shape[1]
    score_scale = HEAD_DIM ** (-0.5)
    inputs = tokens_in.astype(jnp.float32)
    slot_ids = lax.axis_index("tp") * images + jnp.arange(images)
    live_mask = (slot_ids < image_counts[0]).astype(jnp.float32)
    live_grad = out_grad.astype(jnp.float32) * live_mask[:, None, None]
    qkv_all, bqv_all, wout_all = (
        lax.all_gather(w_qkv.astype(jnp.bfloat16), "fsdp", axis=1, tiled=True),
        lax.all_gather(bias_qv.astype(jnp.bfloat16), "fsdp", axis=1, tiled=True),
        lax.all_gather(w_out.astype(jnp.bfloat16), "fsdp", axis=1, tiled=True),
    )
    fc1_all, bfc1_all, fc2_all = (
        lax.all_gather(w_fc1.astype(jnp.bfloat16), "fsdp", axis=0, tiled=True),
        lax.all_gather(bias_fc1.astype(jnp.bfloat16), "fsdp", axis=0, tiled=True),
        lax.all_gather(w_fc2.astype(jnp.bfloat16), "fsdp", axis=1, tiled=True),
    )
    hidden_one = layer_norm(inputs, norm_params[0], norm_params[1]).astype(jnp.bfloat16)
    qkv_use, bqv_use, wout_use = (
        lax.all_gather(qkv_all, "tp", axis=2, tiled=True),
        lax.all_gather(bqv_all, "tp", axis=1, tiled=True),
        lax.all_gather(wout_all, "tp", axis=0, tiled=True),
    )
    group_images = hidden_one.shape[0]
    projected = jnp.einsum("gsd,cdf->cgsf", hidden_one, qkv_use, preferred_element_type=jnp.float32)
    width_local = projected.shape[3]
    shape_heads = (group_images, seq_len, width_local // HEAD_DIM, HEAD_DIM)
    queries = (projected[0] + bqv_use[0]).astype(jnp.bfloat16).reshape(shape_heads)
    key_vecs = projected[1].astype(jnp.bfloat16).reshape(shape_heads)
    value_vecs = (projected[2] + bqv_use[1]).astype(jnp.bfloat16).reshape(shape_heads)
    scores = (
        jnp.einsum("gqhe,gkhe->ghqk", queries, key_vecs, preferred_element_type=jnp.float32)
        * score_scale
    )
    log_total = jax.nn.logsumexp(scores, axis=-1, keepdims=True)
    probs_low = jnp.exp(scores - log_total).astype(jnp.bfloat16)
    context = jnp.einsum(
        "ghqk,gkhe->gqhe", probs_low, value_vecs, preferred_element_type=jnp.float32
    )
    context = context.astype(jnp.bfloat16).reshape(group_images, seq_len, width_local)
    attn_part = jnp.einsum("gsf,fd->gsd", context, wout_use, preferred_element_type=jnp.float32)
    middle = inputs + attn_part + bias_out[0]
    hidden_two = layer_norm(middle, norm_params[2], norm_params[3]).astype(jnp.bfloat16)
    mlp_in = lax.all_gather(hidden_two, "tp", axis=0, tiled=True)
    fc1_use, bfc1_use, fc2_use = (fc1_all, bfc1_all, fc2_all)
    pre_act = (
        jnp.einsum("gsd,df->gsf", mlp_in, fc1_use, preferred_element_type=jnp.float32) + bfc1_use
    )
    activated = exact_gelu(pre_act).astype(jnp.bfloat16)
    mlp_part = jnp.einsum("gsf,fd->gsd", activated, fc2_use, preferred_element_type=jnp.float32)
    mlp_sum = lax.psum_scatter(
        mlp_part.astype(jnp.bfloat16), "tp", scatter_dimension=0, tiled=True
    ).astype(jnp.float32)
    block_out = (middle + mlp_sum + bias_out[1]).astype(jnp.bfloat16)
    grad_mlp = live_grad.astype(jnp.bfloat16)
    grad_mlp_in = lax.all_gather(grad_mlp, "tp", axis=0, tiled=True)
    grad_w2 = jnp.einsum("gsf,gsd->fd", activated, grad_mlp_in, preferred_element_type=jnp.float32)
    grad_act = jnp.einsum("gsd,fd->gsf", grad_mlp_in, fc2_use, preferred_element_type=jnp.float32)
    gelu_out, gelu_pull = jax.vjp(exact_gelu, pre_act)
    grad_pre = gelu_pull(grad_act)[0].astype(jnp.bfloat16)
    grad_b1 = jnp.sum(grad_pre.astype(jnp.float32), axis=(0, 1))
    grad_w1 = jnp.einsum("gsd,gsf->df", mlp_in, grad_pre, preferred_element_type=jnp.float32)
    grad_h2_part = jnp.einsum("gsf,df->gsd", grad_pre, fc1_use, preferred_element_type=jnp.float32)
    grad_h2 = lax.psum_scatter(
        grad_h2_part.astype(jnp.bfloat16), "tp", scatter_dimension=0, tiled=True
    ).astype(jnp.float32)
    norm_two, norm_two_pull = jax.vjp(layer_norm, middle, norm_params[2], norm_params[3])
    grad_mid_ln, grad_gain_two, grad_shift_two = norm_two_pull(grad_h2)
    grad_middle = live_grad + grad_mid_ln
    grad_attn = grad_middle.astype(jnp.bfloat16)
    grad_wo = jnp.einsum("gsf,gsd->fd", context, grad_attn, preferred_element_type=jnp.float32)
    grad_ctx = jnp.einsum("gsd,fd->gsf", grad_attn, wout_use, preferred_element_type=jnp.float32)
    grad_ctx = grad_ctx.astype(jnp.bfloat16).reshape(shape_heads)
    scores_again = (
        jnp.einsum("gqhe,gkhe->ghqk", queries, key_vecs, preferred_element_type=jnp.float32)
        * score_scale
    )
    probs_again = jnp.exp(scores_again - log_total)
    grad_probs = jnp.einsum(
        "gqhe,gkhe->ghqk", grad_ctx, value_vecs, preferred_element_type=jnp.float32
    )
    row_terms = jnp.sum(probs_again * grad_probs, axis=-1, keepdims=True)
    grad_scores = (probs_again * (grad_probs - row_terms)).astype(jnp.bfloat16)
    grad_query = (
        jnp.einsum("ghqk,gkhe->gqhe", grad_scores, key_vecs, preferred_element_type=jnp.float32)
        * score_scale
    ).astype(jnp.bfloat16)
    grad_keys = (
        jnp.einsum("ghqk,gqhe->gkhe", grad_scores, queries, preferred_element_type=jnp.float32)
        * score_scale
    ).astype(jnp.bfloat16)
    grad_values = jnp.einsum(
        "ghqk,gqhe->gkhe",
        probs_again.astype(jnp.bfloat16),
        grad_ctx,
        preferred_element_type=jnp.float32,
    ).astype(jnp.bfloat16)
    grad_proj = jnp.stack([grad_query, grad_keys, grad_values]).reshape(
        3, group_images, seq_len, width_local
    )
    grad_bqv = jnp.stack(
        [
            jnp.sum(grad_proj[0].astype(jnp.float32), axis=(0, 1)),
            jnp.sum(grad_proj[2].astype(jnp.float32), axis=(0, 1)),
        ]
    )
    grad_wqkv = jnp.einsum(
        "gsd,cgsf->cdf", hidden_one, grad_proj, preferred_element_type=jnp.float32
    )
    grad_h1_part = jnp.einsum(
        "cgsf,cdf->gsd", grad_proj, qkv_use, preferred_element_type=jnp.float32
    )
    grad_wqkv, grad_bqv, grad_wo = (
        lax.psum_scatter(
            grad_wqkv.astype(jnp.bfloat16), "tp", scatter_dimension=2, tiled=True
        ).astype(jnp.float32),
        lax.psum_scatter(
            grad_bqv.astype(jnp.bfloat16), "tp", scatter_dimension=1, tiled=True
        ).astype(jnp.float32),
        lax.psum_scatter(
            grad_wo.astype(jnp.bfloat16), "tp", scatter_dimension=0, tiled=True
        ).astype(jnp.float32),
    )
    norm_one, norm_one_pull = jax.vjp(layer_norm, inputs, norm_params[0], norm_params[1])
    grad_in_ln, grad_gain_one, grad_shift_one = norm_one_pull(grad_h1_part)
    grad_tokens = grad_middle + grad_in_ln
    g_qkv, g_bqv, g_out, g_fc1, g_bfc1, g_fc2 = (
        lax.psum_scatter(grad_wqkv, "fsdp", scatter_dimension=1, tiled=True),
        lax.psum_scatter(grad_bqv, "fsdp", scatter_dimension=1, tiled=True),
        lax.psum_scatter(grad_wo, "fsdp", scatter_dimension=1, tiled=True),
        lax.psum_scatter(grad_w1, "fsdp", scatter_dimension=0, tiled=True),
        lax.psum_scatter(grad_b1, "fsdp", scatter_dimension=0, tiled=True),
        lax.psum_scatter(grad_w2, "fsdp", scatter_dimension=1, tiled=True),
    )
    norm_terms = jnp.stack([grad_gain_one, grad_shift_one, grad_gain_two, grad_shift_two])
    bias_terms = jnp.stack([jnp.sum(grad_middle, axis=(0, 1)), jnp.sum(live_grad, axis=(0, 1))])
    g_norm, g_bout = lax.psum((norm_terms, bias_terms), ("fsdp", "tp"))
    s_norm, a_norm, b_norm = adamw(norm_params, g_norm, first_norm, second_norm, 0.0)
    s_qkv, a_qkv, b_qkv = adamw(w_qkv, g_qkv, first_qkv, second_qkv, decay_rate)
    s_bqv, a_bqv, b_bqv = adamw(bias_qv, g_bqv, first_bias_qv, second_bias_qv, 0.0)
    s_out, a_out, b_out = adamw(w_out, g_out, first_out, second_out, decay_rate)
    s_fc1, a_fc1, b_fc1 = adamw(w_fc1, g_fc1, first_fc1, second_fc1, decay_rate)
    s_bfc1, a_bfc1, b_bfc1 = adamw(bias_fc1, g_bfc1, first_bias_fc1, second_bias_fc1, 0.0)
    s_fc2, a_fc2, b_fc2 = adamw(w_fc2, g_fc2, first_fc2, second_fc2, decay_rate)
    s_bout, a_bout, b_bout = adamw(bias_out, g_bout, first_bias_out, second_bias_out, 0.0)
    return (
        block_out,
        grad_tokens,
        g_norm,
        g_qkv,
        g_bqv,
        g_out,
        g_fc1,
        g_bfc1,
        g_fc2,
        g_bout,
        s_norm,
        w_qkv + s_qkv,
        s_bqv,
        s_out,
        w_fc1 + s_fc1,
        s_bfc1,
        w_fc2 + s_fc2,
        s_bout,
        a_norm,
        a_qkv,
        a_bqv,
        a_out,
        a_fc1,
        a_bfc1,
        a_fc2,
        a_bout,
        b_norm,
        b_qkv,
        b_bqv,
        b_out,
        b_fc1,
        b_bfc1,
        b_fc2,
        b_bout,
    )


F32, BF16 = jnp.float32, jnp.bfloat16
MESH_IDS = pl.DeviceIdType.MESH
VMEM_BYTES = 62 * 2**20

NZ, NY, NCORE, NTP = 4, 2, 2, 2
HALF = 256
NEG = -1e30
LANES = 256


def dot(a, b, ca, cb):
    return lax.dot_general(a, b, (((ca,), (cb,)), ((), ())), preferred_element_type=F32)


def normed(v):
    centre = v - jnp.mean(v, axis=-1, keepdims=True)
    rstd = lax.rsqrt(jnp.mean(centre * centre, axis=-1, keepdims=True) + norm_eps)
    return centre * rstd, rstd


def norm_back(e, gain, xhat, rstd):
    eg = e * gain
    m1 = jnp.mean(eg, axis=-1, keepdims=True)
    m2 = jnp.mean(eg * xhat, axis=-1, keepdims=True)
    return rstd * (eg - m1 - xhat * m2)


def pad_rows(v, rows):
    return jnp.concatenate([v, jnp.zeros((rows - v.shape[0], v.shape[1]), v.dtype)], axis=0)


def load_columns(ref, r):
    return jnp.concatenate([ref[j, r, :] for j in range(ref.shape[0])], axis=1)


def store_columns(ref, r, v):
    for j in range(ref.shape[0]):
        ref[j, r, :] = v[:, 128 * j : 128 * j + 128]


class Place:
    def __init__(self):
        f = lax.axis_index("fsdp")
        self.x = lax.axis_index("tp")
        self.z = f // (NY * NCORE)
        self.y = lax.rem(f // NCORE, NY)
        self.c = lax.rem(f, NCORE)
        self.sib = self.at(self.z, self.y, 1 - self.c, self.x)
        self.peer_x = self.at(self.z, self.y, self.c, 1 - self.x)
        self.peer_y = self.at(self.z, 1 - self.y, self.c, self.x)
        self.other_z = [lax.rem(self.z + d, NZ) for d in range(1, NZ)]
        self.peers_z = [self.at(o, self.y, self.c, self.x) for o in self.other_z]
        self.quad = 2 * self.x + self.c
        self.quad_peers = [
            self.at(self.z, self.y, lax.rem(self.c + k, 2), lax.rem(self.x + k // 2, 2))
            for k in range(1, 4)
        ]
        self.line = self.z * NY + self.y
        self.line_peers = []
        for k in range(1, NZ * NY):
            other = lax.rem(self.line + k, NZ * NY)
            self.line_peers.append(self.at(other // NY, lax.rem(other, NY), self.c, self.x))
        self.lanes = pl.ds(pl.multiple_of(self.x * HALF, HALF), HALF)
        self.lanes_other = pl.ds(pl.multiple_of((1 - self.x) * HALF, HALF), HALF)

    def pick(self, v):
        return jnp.where(self.x == 0, v[..., :HALF], v[..., HALF:])

    def at(self, z, y, c, x):
        return {"fsdp": (z * NY + y) * NCORE + c, "tp": x}

    def barrier(self, everyone=None):
        sem = pltpu.get_barrier_semaphore()
        everyone = everyone or [self.sib, self.peer_x, self.peer_y] + self.peers_z
        for d in everyone:
            pl.semaphore_signal(sem, inc=1, device_id=d, device_id_type=MESH_IDS)
        pl.semaphore_wait(sem, len(everyone))


def remote(src, dst, send, recv, device):
    return pltpu.make_async_remote_copy(
        src_ref=src, dst_ref=dst, send_sem=send, recv_sem=recv, device_id=device, device_id_type=MESH_IDS
    )


def start_all(copies):
    for k in copies:
        k.start()


def wait_all(copies):
    for k in copies:
        k.wait()


AG_SEMS = 7


def gather_steps(at, buf, own, send, recv, local, y_first, part=slice(None)):
    x, y, z, c, lanes = at.x, at.y, at.z, at.c, at.lanes
    own = own.at[part]
    mine = buf.at[z, y, c, part, lanes]
    keep = pltpu.make_async_copy(own, mine, local)
    s0 = [remote(own, mine, send.at[d], recv.at[d], at.peers_z[d]) for d in range(NZ - 1)]
    line = buf.at[:, y, c, part, lanes]
    s1 = remote(line, line, send.at[3], recv.at[3], at.peer_y if y_first else at.peer_x)
    if y_first:
        plane, rest = buf.at[:, :, c, part, lanes], buf.at[:, :, c, part, at.lanes_other]
    else:
        plane, rest = buf.at[:, y, c, part], buf.at[:, 1 - y, c, part]
    s2 = remote(plane, plane, send.at[4], recv.at[4], at.peer_x if y_first else at.peer_y)
    sib_a = remote(plane, plane, send.at[5], recv.at[5], at.sib)
    sib_b = remote(rest, rest, send.at[6], recv.at[6], at.sib)

    def step0():
        keep.start()
        start_all(s0)

    def step1():
        keep.wait()
        wait_all(s0)
        s1.start()

    def step2():
        s1.wait()
        s2.start()
        sib_a.start()

    def step3():
        s2.wait()
        sib_b.start()

    def step4():
        sib_a.wait()
        sib_b.wait()

    return [step0, step1, step2, step3, step4]


RS_SEMS = 6


def scatter_steps(at, grad, r0, r1, r2, r3, out, send, recv, x_first):
    x, y, z, c = at.x, at.y, at.z, at.c
    s0 = remote(grad.at[:, :, 1 - c], r0, send.at[0], recv.at[0], at.sib)
    if x_first:
        s1 = remote(r0.at[:, :, :, at.lanes_other], r1, send.at[1], recv.at[1], at.peer_x)
        s2 = remote(r1.at[:, 1 - y], r2, send.at[2], recv.at[2], at.peer_y)
    else:
        s1 = remote(r0.at[:, 1 - y], r1, send.at[1], recv.at[1], at.peer_y)
        s2 = remote(r1.at[:, :, at.lanes_other], r2, send.at[2], recv.at[2], at.peer_x)
    s3 = [
        remote(r2.at[at.other_z[d]], r3.at[d], send.at[3 + d], recv.at[3 + d], at.peers_z[d])
        for d in range(NZ - 1)
    ]

    def add(a, b):
        return (a.astype(F32) + b.astype(F32)).astype(BF16)

    def step0():
        s0.start()

    def step1():
        s0.wait()

        def body(k, _):
            r0[k] = add(r0[k], grad[k, :, c])
            return 0

        lax.fori_loop(0, NZ, body, 0)
        s1.start()

    def step2():
        s1.wait()

        def body(k, _):
            r1[k] = add(r1[k], at.pick(r0[k]) if x_first else r0[k, y])
            return 0

        lax.fori_loop(0, NZ, body, 0)
        s2.start()

    def step3():
        s2.wait()

        def body(k, _):
            r2[k] = add(r2[k], r1[k, y] if x_first else at.pick(r1[k]))
            return 0

        lax.fori_loop(0, NZ, body, 0)
        start_all(s3)

    def step4():
        wait_all(s3)
        total = r2[z].astype(F32)
        for d in range(NZ - 1):
            total = total + r3[d].astype(F32)
        out[...] = total

    return [step0, step1, step2, step3, step4]


def scatter_scratch(chunks, rows):
    wide = NTP * HALF
    return [
        pltpu.VMEM((chunks, 2, NZ, NY, rows, wide), BF16),
        pltpu.VMEM((chunks, NZ, NY, rows, HALF), BF16),
        pltpu.VMEM((chunks, NZ, rows, wide), BF16),
        pltpu.VMEM((chunks, 2, NZ, rows, HALF), BF16),
        pltpu.VMEM((chunks, 2, NZ - 1, rows, HALF), BF16),
        pltpu.SemaphoreType.DMA((chunks, 2, RS_SEMS)),
        pltpu.SemaphoreType.DMA((chunks, 2, RS_SEMS)),
    ]


def scatter_both(at, k, grads, scratch, outs):
    r0, r1a, r1b, r2, r3, send, recv = scratch
    first = scatter_steps(
        at, grads[0], r0.at[k, 0], r1a.at[k], r2.at[k, 0], r3.at[k, 0], outs[0], send.at[k, 0], recv.at[k, 0], True
    )
    second = scatter_steps(
        at, grads[1], r0.at[k, 1], r1b.at[k], r2.at[k, 1], r3.at[k, 1], outs[1], send.at[k, 1], recv.at[k, 1], False
    )
    return [both(a, b) for a, b in zip(first, second)]


def both(a, b):
    def run():
        a()
        b()

    return run


def gather_both(at, buf, own, sems, part=slice(None)):
    send, recv, local = sems
    first = gather_steps(at, buf.at[0], own.at[0], send.at[0], recv.at[0], local.at[0], True, part)
    second = gather_steps(at, buf.at[1], own.at[1], send.at[1], recv.at[1], local.at[1], False, part)
    return [both(a, b) for a, b in zip(first, second)]


def run_slot(plan, key, counters):
    for want, steps in plan.get(key, {}).items():
        cond = None
        for have, value in zip(counters, want):
            test = have == value
            cond = test if cond is None else jnp.logical_and(cond, test)

        def go(steps=steps):
            for s in steps:
                s()

        pl.when(cond)(go)


def planned(entries):
    plan = {}
    for key, want, step in entries:
        plan.setdefault(key, {}).setdefault(want, []).append(step)
    return plan


def matrix(ref):
    v = ref[...]
    return v.reshape(v.shape[0] * v.shape[1] * v.shape[2] * v.shape[3], v.shape[4])


def left_half(rows):
    return lax.broadcasted_iota(jnp.int32, (rows, 2 * HEAD_DIM), 1) < HEAD_DIM


def split_heads(v, left):
    zero = jnp.zeros_like(v)
    return jnp.concatenate([jnp.where(left, v, zero), jnp.where(left, zero, v)], axis=0)


def projection(a, b):
    return jnp.concatenate([a, b[:, 0:128], b[:, HALF : HALF + 128]], axis=1)


def out_columns(b):
    return jnp.concatenate([b[:, 128:HALF], b[:, HALF + 128 :]], axis=1)


def spread(pieces, width, row, total):
    col = lax.broadcasted_iota(jnp.int32, (128, total), 1).astype(F32)
    lane = lax.broadcasted_iota(jnp.int32, (128, total), 0).astype(F32)
    owner = jnp.floor((col + 0.5) * (1.0 / width))
    pick = (col - owner * width == lane).astype(BF16)
    spreaded = dot(pieces.astype(BF16), pick, 1, 0)
    at_row = lax.broadcasted_iota(jnp.int32, spreaded.shape, 0).astype(F32)
    col = lax.broadcasted_iota(jnp.int32, spreaded.shape, 1).astype(F32)
    owner = jnp.floor((col + 0.5) * (1.0 / width))
    return jnp.sum(jnp.where(at_row == owner * 8.0 + row, spreaded, 0.0), axis=0, keepdims=True)


def attention_kernel(
    dims,
    x_hbm, norm_ref, bout_ref, wqkv_ref, wout_ref, wfc1_ref, wfc2_ref, bqv_ref, bfc1_ref,
    qkv_hbm, ctx_hbm, mid_hbm, p_hbm, watt_hbm, wff_hbm, own_hbm, bias_ref,
    x_s, h1, qkv_s, ctx_s, mid_s, p_s, watt, own, pieces, bias_s,
    ag_send, ag_recv, ag_local, sm_send, sm_recv, out_sem, in_sem,
):
    images, seq, sp, groups, chunks, early = dims
    at = Place()
    x_copy = pltpu.make_async_copy(x_hbm, x_s, in_sem.at[0])
    x_copy.start()
    own_rows = wqkv_ref.shape[2]
    rows = images * seq
    for g in range(groups):
        cols = slice(128 * g, 128 * g + 128)
        own[g, 0] = jnp.concatenate([wqkv_ref[0, :, cols], wqkv_ref[1, :, cols]], axis=1).astype(BF16)
        own[g, 1] = jnp.concatenate([wqkv_ref[2, :, cols], wout_ref[:, cols]], axis=1).astype(BF16)
    pieces[at.x, at.z, at.y, at.c] = jnp.zeros((8, 128), F32)
    pieces[at.x, at.z, at.y, at.c, 0:1, 0 : bfc1_ref.shape[1]] = bfc1_ref[...]
    pieces[at.x, at.z, at.y, at.c, 1:3, 0 : bqv_ref.shape[1]] = bqv_ref[...]

    def sems(k):
        return ag_send.at[k], ag_recv.at[k], ag_local.at[k]

    third = own.shape[2] // 3
    head = [
        gather_both(at, watt.at[0], own.at[0], sems(k), pl.ds(j * third, third))
        for j, k in enumerate((0, groups + early, groups + early + 1))
    ]
    steps = [[None] * 5] + [gather_both(at, watt.at[g], own.at[g], sems(g)) for g in range(1, groups)]
    steps += [gather_both(at, wff_hbm.at[f], own.at[groups + f], sems(groups + f)) for f in range(early)]
    here = pieces.at[at.x, at.z, at.y, at.c]
    line = pieces.at[at.x, :, at.y, at.c]
    plane = pieces.at[at.x, :, :, at.c]
    cube = pieces.at[:, :, :, at.c]
    bias_steps = [[remote(here, here, sm_send.at[d], sm_recv.at[d], at.peers_z[d]) for d in range(NZ - 1)]]
    bias_steps += [
        [remote(r, r, sm_send.at[3 + k], sm_recv.at[3 + k], d)]
        for k, (r, d) in enumerate([(line, at.peer_y), (plane, at.peer_x), (cube, at.sib)])
    ]

    def head_step(k):
        for part in head:
            part[k]()

    at.barrier()
    head_step(0)
    start_all(bias_steps[0])
    steps[1][0]()
    for f in range(chunks - groups):
        cols = slice(HALF * f, HALF * f + HALF)
        own[groups + f, 0] = wfc1_ref[:, cols].astype(BF16)
        own[groups + f, 1] = wfc2_ref[:, cols].astype(BF16)
    late = pltpu.make_async_copy(own.at[pl.ds(groups + early, chunks - groups - early)], own_hbm, in_sem.at[1])
    late.start()
    x_copy.wait()

    block = rows // 7

    def first_norm(j, _):
        r = pl.ds(pl.multiple_of(j * block, 16), block)
        xhat, _r = normed(x_s[r, :].astype(F32))
        store_columns(mid_s, r, xhat * norm_ref[0:1, :] + norm_ref[1:2, :])
        return 0

    def by_image(i, _):
        h = pad_rows(load_columns(mid_s, pl.ds(i, seq, stride=images)), sp)
        h1[pl.ds(pl.multiple_of(i * sp, 16), sp), :] = h.astype(BF16)
        return 0

    head_step(1)
    wait_all(bias_steps[0])
    start_all(bias_steps[1])
    steps[2][0]()
    lax.fori_loop(0, 7, first_norm, 0)
    head_step(2)
    wait_all(bias_steps[1])
    start_all(bias_steps[2])
    lax.fori_loop(0, images, by_image, 0)
    steps[1][1]()
    head_step(3)
    wait_all(bias_steps[2])
    start_all(bias_steps[3])
    wait_all(bias_steps[3])
    flat = pieces[...].reshape(NTP * NZ * NY * NCORE * 8, 128)
    width = bqv_ref.shape[1]
    model = width * NTP * NZ * NY * NCORE
    bias_q = spread(flat, width, 1.0, model)
    bias_v = spread(flat, width, 2.0, model)
    for g in range(groups):
        parts = []
        for t in range(NTP):
            parts += [bias_q[:, t * own_rows + 128 * g : t * own_rows + 128 * g + 128], jnp.zeros((1, 128), F32)]
        for t in range(NTP):
            parts.append(bias_v[:, t * own_rows + 128 * g : t * own_rows + 128 * g + 128])
        bias_s[g] = jnp.concatenate(parts, axis=1)
    width = bfc1_ref.shape[1]
    bias_ff = spread(flat, width, 0.0, width * NTP * NZ * NY * NCORE)
    per = bias_ff.shape[1] // NTP
    for f in range(chunks - groups):
        bias_ref[f] = jnp.concatenate(
            [bias_ff[:, t * per + f * HALF : t * per + f * HALF + HALF] for t in range(NTP)], axis=1
        )
    head_step(4)

    when = {1: [None, None, 2, 4, 4], 2: [None, 2, 4, 8, 8]}
    when.update({groups + f: ns for f, ns in enumerate([[0, 4, 7, 10, 13], [4, 8, 11, 14, 14]])})
    entries = sorted((n, k, k_step) for k, ns in when.items() for k_step, n in enumerate(ns) if n is not None)
    last = 4 * groups + 2
    plan = planned(
        [("out", (n - 4 * groups,), steps[k][j]) if n >= 4 * groups else (n % 2, (n // 4, n % 4 // 2), steps[k][j])
         for n, k, j in entries if n < last]
    )
    remains = [steps[k][j] for n, k, j in entries if n >= last]

    quad = 4
    tr = quad * sp
    left = left_half(sp)
    full = seq // 16 * 16
    live_key = lax.broadcasted_iota(jnp.int32, (sp - full, LANES), 0) < seq - full
    tiles = images // quad
    units = [(a, t) for a in range(quad) for t in range(NTP)]

    def soften(s):
        s = jnp.concatenate([s[:full], jnp.where(live_key, s[full:], NEG)], axis=0)
        e = jnp.exp(s - jnp.max(s, axis=0, keepdims=True))
        return (e * (1.0 / jnp.sum(e, axis=0, keepdims=True))).astype(BF16)

    def group(g, _):
        def tile(i, _):
            run_slot(plan, 0, (g, i))
            r = pl.ds(pl.multiple_of(i * tr, 16), tr)
            w = projection(matrix(watt.at[g, 0]), matrix(watt.at[g, 1]))
            qkv_s[g, r, :] = (dot(h1[r, :], w, 1, 0) + bias_s[g]).astype(BF16)
            run_slot(plan, 1, (g, i))
            qkv = qkv_s[g, r, :]

            def cut(a, first):
                return qkv[a * sp : (a + 1) * sp, first : first + 128]

            scores = []
            for a, t in units:
                q = pad_rows(cut(a, t * HALF) * jnp.asarray(HEAD_DIM ** (-0.5), BF16), LANES)
                scores.append(dot(split_heads(cut(a, t * HALF + 128), left), q, 1, 1))
            probs = []
            for (a, t), s in zip(units, scores):
                probs.append([soften(s[h * sp : (h + 1) * sp]) for h in range(2)])
                for h in range(2):
                    p_s[g, i * quad + a, t, h] = probs[-1][h]
            for (a, t), p in zip(units, probs):
                vt = cut(a, 2 * HALF + t * 128).T
                cs = [dot(vt[h * HEAD_DIM : (h + 1) * HEAD_DIM], p[h], 1, 0) for h in range(2)]
                mine = pl.ds(pl.multiple_of(i * tr + a * sp, 16), sp)
                ctx_s[g, mine, t * 128 : (t + 1) * 128] = jnp.concatenate(cs, axis=0).T[:sp].astype(BF16)
            pltpu.make_async_copy(qkv_s.at[g, r], qkv_hbm.at[g, r], out_sem.at[0, g, i]).start()
            pltpu.make_async_copy(ctx_s.at[g, r], ctx_hbm.at[g, r], out_sem.at[1, g, i]).start()
            im = pl.ds(i * quad, quad)
            pltpu.make_async_copy(p_s.at[g, im], p_hbm.at[g, im], out_sem.at[2, g, i]).start()
            return 0

        lax.fori_loop(0, tiles, tile, 0)
        pltpu.make_async_copy(watt.at[g], watt_hbm.at[g], in_sem.at[2 + g]).start()
        return 0

    lax.fori_loop(0, groups, group, 0)

    def project_out(i, _):
        run_slot(plan, "out", (i,))
        r = pl.ds(pl.multiple_of(i * tr, 16), tr)
        w = jnp.concatenate([out_columns(matrix(watt.at[g, 1])) for g in range(groups)], axis=1)
        c = jnp.concatenate([ctx_s[g, r, :] for g in range(groups)], axis=1)
        attn = dot(c, w, 1, 1)
        for a in range(quad):
            store_columns(mid_s, pl.ds(i * quad + a, seq, stride=images), attn[a * sp : a * sp + seq])
        return 0

    lax.fori_loop(0, tiles, project_out, 0)

    def residual(j, _):
        r = pl.ds(pl.multiple_of(j * block, 16), block)
        store_columns(mid_s, r, load_columns(mid_s, r) + x_s[r, :].astype(F32) + bout_ref[0:1, :])
        pltpu.make_async_copy(mid_s.at[:, r], mid_hbm.at[:, r], out_sem.at[3, 0, j]).start()
        return 0

    lax.fori_loop(0, 7, residual, 0)
    for step in remains:
        step()

    def drain(k, _):
        g, i = k // tiles, lax.rem(k, tiles)
        r = pl.ds(pl.multiple_of(i * tr, 16), tr)
        pltpu.make_async_copy(qkv_s.at[g, r], qkv_hbm.at[g, r], out_sem.at[0, g, i]).wait()
        pltpu.make_async_copy(ctx_s.at[g, r], ctx_hbm.at[g, r], out_sem.at[1, g, i]).wait()
        im = pl.ds(i * quad, quad)
        pltpu.make_async_copy(p_s.at[g, im], p_hbm.at[g, im], out_sem.at[2, g, i]).wait()
        return 0

    lax.fori_loop(0, groups * tiles, drain, 0)
    for g in range(groups):
        pltpu.make_async_copy(watt.at[g], watt_hbm.at[g], in_sem.at[2 + g]).wait()
    for j in range(7):
        r = pl.ds(j * block, block)
        pltpu.make_async_copy(mid_s.at[:, r], mid_hbm.at[:, r], out_sem.at[3, 0, j]).wait()
    late.wait()


def feed_forward_kernel(
    dims,
    counts_ref, norm_ref, bout_ref, bias_ref, mid_hbm, og_hbm, wff_hbm, own_hbm,
    bo_hbm, dmid_hbm, late_hbm, sums_ref, b1g_ref, gff_ref,
    wff, own, h2, h2t, dm, dmt, mlp, dh2, act, dpre, grad, mid_s,
    r0, r1a, r1b, r2, r3, rs_send, rs_recv,
    ag_send, ag_recv, ag_local, in_sem, mid_sem, out_sem,
):
    images, seq, sp, chunks, early, summed = dims
    rows = images * seq
    padded = h2.shape[0]
    block = rows // 7
    at = Place()
    og_copy = pltpu.make_async_copy(og_hbm, dm.at[pl.ds(0, rows)], in_sem.at[0])
    own_copy = pltpu.make_async_copy(own_hbm, own, in_sem.at[1])
    w_copies = [pltpu.make_async_copy(wff_hbm.at[f], wff.at[f], in_sem.at[2 + f]) for f in range(early)]
    own_copy.start()
    og_copy.start()

    def mid_copy(i):
        r = pl.ds(pl.multiple_of(i * block, 16), block)
        return pltpu.make_async_copy(mid_hbm.at[:, r], mid_s.at[lax.rem(i, 3)], mid_sem.at[lax.rem(i, 3)])

    mid_copy(0).start()
    start_all(w_copies)
    late = chunks - early
    gather = {
        early + k: gather_both(
            at, wff.at[early + k], own.at[k], (ag_send.at[k], ag_recv.at[k], ag_local.at[k])
        )
        for k in range(late)
    }
    scratch = (r0, r1a, r1b, r2, r3, rs_send, rs_recv)
    scatter = [
        scatter_both(
            at, k, (grad.at[k % 2, 0], grad.at[k % 2, 1]), scratch, (gff_ref.at[k, 0], gff_ref.at[k, 1])
        )
        for k in range(summed)
    ]
    at.barrier()
    own_copy.wait()
    for k in range(late):
        gather[early + k][0]()
    og_copy.wait()
    count = counts_ref[0]

    first = at.x * images
    image = lax.rem(lax.broadcasted_iota(jnp.int32, (block, 1), 0), images) + first
    live = jnp.where(image < count, 1.0, 0.0).astype(F32)

    def second_norm(i, _):
        pl.when(i + 1 < 7)(lambda: mid_copy(i + 1).start())
        mid_copy(i).wait()
        r = pl.ds(pl.multiple_of(i * block, 16), block)
        xhat, _r = normed(load_columns(mid_s.at[lax.rem(i, 3)], slice(None)))
        h2[r, :] = (xhat * norm_ref[2:3, :] + norm_ref[3:4, :]).astype(BF16)
        dm[r, :] = (dm[r, :].astype(F32) * live).astype(BF16)
        mlp[r, :] = jnp.zeros((block, mlp.shape[1]), F32)
        dh2[r, :] = jnp.zeros((block, mlp.shape[1]), F32)
        return 0

    rest = pl.ds(rows, padded - rows)
    for ref in (h2, dm, act, dpre):
        ref[rest, :] = jnp.zeros((padded - rows, ref.shape[1]), BF16)
    lax.fori_loop(0, 7, second_norm, 0)

    def turn(j, _):
        r = pl.ds(pl.multiple_of(j * 128, 128), 128)
        h2t[:, r] = h2[r, :].T
        dmt[:, r] = dm[r, :].T
        return 0

    lax.fori_loop(0, padded // 128, turn, 0)
    wait_all(w_copies)

    entries = []
    for k, slots in enumerate(
        ((None, 0, 2, 6, 8), (None, 2, 6, 10, 12), (None, 4, 7, 12, 16), (None, 6, 10, 14, 20))
    ):
        entries += [(n, gather[early + k][j]) for j, n in enumerate(slots) if n is not None]
    for k, slots in enumerate(((8, 10, 16, 18, 21), (12, 14, 17, 19, 23), (16, 18, 21, 23, 24))):
        entries += [(n, scatter[k][j]) for j, n in enumerate(slots)]
    entries.sort(key=lambda e: e[0])
    plan = planned([(slot % 4, (slot // 4,), step) for slot, step in entries if slot < 4 * chunks])
    tail = [step for slot, step in entries if slot >= 4 * chunks]

    def late_copy(k):
        return pltpu.make_async_copy(grad.at[k % 2], late_hbm.at[k - summed], out_sem.at[k - summed])

    def chunk(f, _):
        b1 = bias_ref[f]
        for i in range(2):
            run_slot(plan, i, (f,))
            r = pl.ds(i * (rows // 2), rows // 2)
            w1, w2 = matrix(wff.at[f, 0]), matrix(wff.at[f, 1])
            pre = dot(h2[r, :], w1, 1, 0) + b1
            phi = 0.5 + 0.5 * lax.erf(pre * 0.7071067811865476)
            a = (pre * phi).astype(BF16)
            slope = phi + pre * (jnp.exp(-0.5 * pre * pre) * 0.3989422804014327)
            d = (dot(dm[r, :], w2, 1, 0) * slope).astype(BF16)
            act[r, :] = a
            dpre[r, :] = d
            mlp[r, :] += dot(a, w2, 1, 1)
            dh2[r, :] += dot(d, w1, 1, 1)
        slot = lax.rem(f, 2)
        shape = grad.shape[2:]
        run_slot(plan, 2, (f,))
        for k in range(summed, chunks - 2):
            pl.when(f == k + 2)(late_copy(k).wait)
        b1g_ref[f] = jnp.sum(dpre[...].astype(F32), axis=0, keepdims=True)
        grad[slot, 0] = dot(h2t[...], dpre[...], 1, 0).astype(BF16).reshape(shape)
        run_slot(plan, 3, (f,))
        grad[slot, 1] = dot(dmt[...], act[...], 1, 0).astype(BF16).reshape(shape)

        for k in range(summed, chunks):
            pl.when(f == k)(late_copy(k).start)
        return 0

    lax.fori_loop(0, chunks, chunk, 0)
    mid_copy(0).start()

    def dmid_copy(i):
        r = pl.ds(pl.multiple_of(i * block, 16), block)
        return pltpu.make_async_copy(mid_s.at[lax.rem(i, 3)], dmid_hbm.at[:, r], out_sem.at[16 + lax.rem(i, 3)])

    def second_norm_back(i, acc):
        pl.when(i >= 2)(lambda: dmid_copy(i - 2).wait())
        pl.when(i + 1 < 7)(lambda: mid_copy(i + 1).start())
        mid_copy(i).wait()
        r = pl.ds(pl.multiple_of(i * block, 16), block)
        mid = load_columns(mid_s.at[lax.rem(i, 3)], slice(None))
        xhat, rstd = normed(mid)
        h2[r, :] = (mid + mlp[r, :] + bout_ref[1:2, :]).astype(BF16)
        e = dh2[r, :]
        live = dm[r, :].astype(F32)
        d = live + norm_back(e, norm_ref[2:3, :], xhat, rstd)
        store_columns(mid_s.at[lax.rem(i, 3)], slice(None), d)
        pltpu.make_async_copy(h2.at[r], bo_hbm.at[r], out_sem.at[8 + i]).start()
        dmid_copy(i).start()
        terms = (e * xhat, e, d, live)
        return tuple(a + jnp.sum(t, axis=0, keepdims=True) for a, t in zip(acc, terms))

    zero = jnp.zeros((1, mlp.shape[1]), F32)
    acc = lax.fori_loop(0, 7, second_norm_back, (zero,) * 4)
    sums_ref[...] = jnp.zeros(sums_ref.shape, F32)
    for k in range(4):
        sums_ref[k : k + 1, :] = acc[k]
    for step in tail:
        step()

    for i in range(7):
        r = pl.ds(i * block, block)
        pltpu.make_async_copy(h2.at[r], bo_hbm.at[r], out_sem.at[8 + i]).wait()
    dmid_copy(5).wait()
    dmid_copy(6).wait()
    for k in range(chunks - 2, chunks):
        late_copy(k).wait()


def attention_back_kernel(
    dims,
    norm_ref, sums_ref, b1g_ref, x_hbm, dmid_hbm, late_hbm, watt_hbm, qkv_hbm, ctx_hbm, p_hbm,
    gt_hbm, glate_ref, gatt_ref, small_ref,
    dattn, h1t, dh1, dqkv, watt, qkv_s, dc_s, ctx_s, ctxt, p_s, grad, x_s, dmid_s, gt_s, bias_s,
    small, small_line,
    r0, r1a, r1b, r2, r3, rs_send, rs_recv, sm_send, sm_recv,
    in_sem, ctx_sem, tile_sem, dmid_sem, gt_sem,
):
    images, seq, sp, groups, chunks, held = dims
    rows = images * seq
    block = rows // 7
    model = x_s.shape[1]
    quad = 4
    tr = quad * sp
    tiles = images // quad
    at = Place()
    dmid_in = pltpu.make_async_copy(dmid_hbm, dh1, in_sem.at[0])
    watt_copy = pltpu.make_async_copy(watt_hbm, watt, in_sem.at[1])
    x_copy = pltpu.make_async_copy(x_hbm, x_s, in_sem.at[2])
    late_copies = [pltpu.make_async_copy(late_hbm.at[k], grad.at[k], in_sem.at[3 + k]) for k in range(held)]

    def dmid_copy(i):
        r = pl.ds(pl.multiple_of(i * block, 16), block)
        return pltpu.make_async_copy(dmid_hbm.at[:, r], dmid_s.at[lax.rem(i, 2)], dmid_sem.at[lax.rem(i, 2)])

    def ctx_copy(g):
        return pltpu.make_async_copy(ctx_hbm.at[g], ctx_s, ctx_sem.at[0])

    def tile_copies(g, i):
        r, im = pl.ds(pl.multiple_of(i * tr, 16), tr), pl.ds(i * quad, quad)
        return [
            pltpu.make_async_copy(qkv_hbm.at[g, r], qkv_s.at[r], tile_sem.at[0, i]),
            pltpu.make_async_copy(p_hbm.at[g, im], p_s.at[im], tile_sem.at[1, i]),
        ]

    late_copies[0].start()
    dmid_in.start()
    x_copy.start()
    watt_copy.start()
    start_all(late_copies[1:])
    ctx_copy(0).start()
    for i in range(tiles):
        start_all(tile_copies(0, i))
    scratch = (r0, r1a, r1b, r2, r3, rs_send, rs_recv)
    scatter = [
        scatter_both(at, k, (grad.at[k, 0], grad.at[k, 1]), scratch, (glate_ref.at[k, 0], glate_ref.at[k, 1]))
        for k in range(held)
    ]
    for g in range(groups):
        scatter.append(
            scatter_both(
                at, held + g, (grad.at[g % held, 0], grad.at[g % held, 1]), scratch, (gatt_ref.at[g, 0], gatt_ref.at[g, 1])
            )
        )
    own_quad, own_line = small.at[at.quad], small_line.at[at.line]
    sm_quad = [remote(own_quad, own_quad, sm_send.at[k], sm_recv.at[k], d) for k, d in enumerate(at.quad_peers)]
    sm_line = [
        remote(own_line, own_line, sm_send.at[3 + k], sm_recv.at[3 + k], d) for k, d in enumerate(at.line_peers)
    ]
    at.barrier(at.quad_peers + at.line_peers)
    for k in range(held):
        late_copies[k].wait()
        scatter[k][0]()

    dmid_in.wait()

    def take_dattn(i, _):
        d = pad_rows(load_columns(dh1, pl.ds(i, seq, stride=images)), sp)
        dattn[pl.ds(pl.multiple_of(i * sp, 16), sp), :] = d.astype(BF16)
        return 0

    lax.fori_loop(0, images, take_dattn, 0)
    x_copy.wait()

    def first_norm(j, _):
        r = pl.ds(pl.multiple_of(j * block, 16), block)
        xhat, _r = normed(x_s[r, :].astype(F32))
        store_columns(dh1, r, xhat * norm_ref[0:1, :] + norm_ref[1:2, :])
        return 0

    lax.fori_loop(0, 7, first_norm, 0)

    def by_image(i, _):
        h = pad_rows(load_columns(dh1, pl.ds(i, seq, stride=images)), sp)
        dqkv[0, pl.ds(pl.multiple_of(i * sp, 16), sp), :] = h.astype(BF16)
        return 0

    lax.fori_loop(0, images, by_image, 0)

    for k in range(held):
        scatter[k][1]()

    def turn(j, _):
        r = pl.ds(pl.multiple_of(j * 128, 128), 128)
        h1t[:, r] = dqkv[0, r, :].T
        return 0

    lax.fori_loop(0, images * sp // 128, turn, 0)
    watt_copy.wait()

    entries = []
    for k, slots in enumerate(((2, 8, 12), (4, 10, 14), (8, 11, 16))):
        entries += [(n, scatter[k][2 + j]) for j, n in enumerate(slots)]
    for g, slots in enumerate(((12, 15, 18, 21, 27), (14, 16, 20, 22, 30), (18, 20, 26, 30, 31))):
        entries += [(n, scatter[held + g][j]) for j, n in enumerate(slots)]
    entries.sort(key=lambda e: e[0])

    def spot(n):
        return (n % 2, (n // 6, n % 6 // 2)) if n % 6 < 4 else (n % 6, (n // 6,))

    tail_at = 6 * groups
    plan = planned(
        [spot(n) + (step,) for n, step in entries if n < tail_at]
        + [("through", (n - tail_at,), step) for n, step in entries if tail_at <= n < tail_at + 4]
        + [("norm", (n - tail_at - 4,), step) for n, step in entries if tail_at + 4 <= n < tail_at + 11]
    )
    tail = [[step for n, step in entries if n == at_end] for at_end in (tail_at + 12, tail_at + 13)]

    left = left_half(sp)
    scale = HEAD_DIM ** (-0.5)

    units = [(a, t) for a in range(quad) for t in range(NTP)]

    def group(g, _):
        keep = lax.rem(g, grad.shape[0])
        ctx_copy(g).wait()
        ctxt[...] = ctx_s[...].T
        pl.when(g + 1 < groups)(lambda: ctx_copy(g + 1).start())

        def tile(i, acc):
            wait_all(tile_copies(g, i))
            run_slot(plan, 0, (g, i))
            r = pl.ds(pl.multiple_of(i * tr, 16), tr)
            dc_s[...] = dot(dattn[r, :], out_columns(matrix(watt.at[g, 1])), 1, 0).astype(BF16)
            run_slot(plan, 1, (g, i))
            qkv, dc = qkv_s[r, :], dc_s[...]

            def cut(a, first):
                return qkv[a * sp : (a + 1) * sp, first : first + 128]

            def wide(v):
                return pad_rows(v, LANES)

            def grads_in(a, t):
                return wide(dc[a * sp : (a + 1) * sp, t * 128 : (t + 1) * 128])

            dps = [dot(split_heads(cut(a, 2 * HALF + t * 128), left), grads_in(a, t), 1, 1) for a, t in units]
            dss = []
            for (a, t), dp in zip(units, dps):
                ds = []
                for h in range(2):
                    p = p_s[i * quad + a, t, h].astype(F32)
                    pd = p * dp[h * sp : (h + 1) * sp]
                    ds.append((pd - p * jnp.sum(pd, axis=0, keepdims=True)).astype(BF16))
                dss.append(ds)
            parts = []
            for (a, t), ds in zip(units, dss):
                q = wide(cut(a, t * HALF) * jnp.asarray(scale, BF16))
                kt = cut(a, t * HALF + 128).T
                dqt = [dot(kt[h * HEAD_DIM : (h + 1) * HEAD_DIM], ds[h], 1, 0) for h in range(2)]
                dk = dot(jnp.concatenate(ds, axis=0), q, 1, 0)
                ps = jnp.concatenate([p_s[i * quad + a, t, h] for h in range(2)], axis=0)
                dv = dot(ps, grads_in(a, t), 1, 0)
                parts.append((
                    jnp.concatenate(dqt, axis=0).T[:sp] * scale,
                    jnp.where(left, dk[:sp], dk[sp:]),
                    jnp.where(left, dv[:sp], dv[sp:]),
                ))
            for a in range(quad):
                (q0, k0, v0), (q1, k1, v1) = parts[NTP * a], parts[NTP * a + 1]
                d = jnp.concatenate([q0, k0, q1, k1, v0, v1], axis=1).astype(BF16)
                dqkv[g, pl.ds(pl.multiple_of(i * tr + a * sp, 16), sp), :] = d
                acc = acc + jnp.sum(d.astype(F32), axis=0, keepdims=True)
            pl.when(g + 1 < groups)(lambda: start_all(tile_copies(g + 1, i)))
            return acc

        bias_s[g] = lax.fori_loop(0, tiles, tile, jnp.zeros((1, model), F32))
        run_slot(plan, 4, (g,))
        shape = grad.shape[2:]
        gw = dot(h1t[...], dqkv[g], 1, 0).astype(BF16)
        grad[keep, 0] = gw[:, : 2 * HALF].reshape(shape)
        run_slot(plan, 5, (g,))
        go = dot(ctxt[...], dattn[...], 1, 0).T.astype(BF16)
        grad[keep, 1] = jnp.concatenate(
            [gw[:, 2 * HALF : 2 * HALF + 128], go[:, :128], gw[:, 2 * HALF + 128 :], go[:, 128:]], axis=1
        ).reshape(shape)
        return 0

    lax.fori_loop(0, groups, group, 0)
    dmid_copy(0).start()
    small_tr = 2 * sp

    def through(i, _):
        run_slot(plan, "through", (i,))
        r = pl.ds(pl.multiple_of(i * small_tr, 16), small_tr)
        d = jnp.concatenate([dqkv[g, r, :] for g in range(groups)], axis=1)
        w = jnp.concatenate(
            [projection(matrix(watt.at[g, 0]), matrix(watt.at[g, 1])) for g in range(groups)], axis=1
        )
        back = dot(d, w, 1, 1)
        for a in range(2):
            store_columns(dh1, pl.ds(i * 2 + a, seq, stride=images), back[a * sp : a * sp + seq])
        return 0

    lax.fori_loop(0, images // 2, through, 0)

    def gt_copy(i):
        r = pl.ds(pl.multiple_of(i * block, 16), block)
        return pltpu.make_async_copy(gt_s.at[lax.rem(i, 2)], gt_hbm.at[r], gt_sem.at[lax.rem(i, 2)])

    def first_norm_back(i, acc):
        run_slot(plan, "norm", (i,))
        pl.when(i >= 2)(lambda: gt_copy(i - 2).wait())
        pl.when(i + 1 < 7)(lambda: dmid_copy(i + 1).start())
        dmid_copy(i).wait()
        r = pl.ds(pl.multiple_of(i * block, 16), block)
        xhat, rstd = normed(x_s[r, :].astype(F32))
        e = load_columns(dh1, r)
        d = load_columns(dmid_s.at[lax.rem(i, 2)], slice(None))
        gt_s[lax.rem(i, 2)] = d + norm_back(e, norm_ref[0:1, :], xhat, rstd)
        gt_copy(i).start()
        return (acc[0] + jnp.sum(e * xhat, axis=0, keepdims=True), acc[1] + jnp.sum(e, axis=0, keepdims=True))

    zero = jnp.zeros((1, model), F32)
    acc = lax.fori_loop(0, 7, first_norm_back, (zero, zero))
    own_quad[...] = jnp.zeros(own_quad.shape, F32)
    own_quad[0:1, :] = acc[0]
    own_quad[1:2, :] = acc[1]
    own_quad[2:6, :] = sums_ref[0:4, :]
    own_cols = groups * 128
    for g in range(groups):
        for t in range(NTP):
            cols = slice(t * own_cols + 128 * g, t * own_cols + 128 * g + 128)
            own_quad[6:7, cols] = bias_s[g, :, t * HALF : t * HALF + 128]
            own_quad[7:8, cols] = bias_s[g, :, 2 * HALF + t * 128 : 2 * HALF + t * 128 + 128]
    for f in range(chunks):
        for t in range(NTP):
            first = t * chunks * HALF + f * HALF
            row, col = 8 + first // model, first % model
            own_quad[row : row + 1, col : col + HALF] = b1g_ref[f, :, t * HALF : t * HALF + HALF]
    start_all(sm_quad)
    for step in tail[0]:
        step()
    wait_all(sm_quad)
    own_line[...] = (small[0] + small[1]) + (small[2] + small[3])
    start_all(sm_line)
    for step in tail[1]:
        step()
    gt_copy(5).wait()
    gt_copy(6).wait()
    wait_all(sm_line)
    total = small_line[0]
    for k in range(1, NZ * NY):
        total = total + small_line[k]
    small_ref[...] = total


def step_kernel(dims, *refs):
    groups, chunks, held = dims
    names = ("norm", "qkv", "bqv", "out", "fc1", "bfc1", "fc2", "bout")
    gff_ref, glate_ref, gatt_ref, small_ref = refs[:4]
    n = len(names)
    ps, ms, vs = (dict(zip(names, refs[4 + k * n : 4 + (k + 1) * n])) for k in range(3))
    outs = refs[4 + 3 * n :]
    g_out, u_out, m_out, v_out = (dict(zip(names, outs[k * n : (k + 1) * n])) for k in range(4))
    late = chunks - held

    def ff(f, h):
        return gff_ref[f, h] if f < late else glate_ref[f - late, h]

    whole = {"qkv": True, "fc1": True, "fc2": True}
    decays = ("qkv", "out", "fc1", "fc2")

    def update(name, index, g):
        p = ps[name][index]
        u, m, v = adamw(p, g, ms[name][index], vs[name][index], decay_rate if name in decays else 0.0)
        g_out[name][index] = g
        u_out[name][index] = p + u if name in whole else u
        m_out[name][index] = m
        v_out[name][index] = v

    for c in range(3):
        gs = [gatt_ref[g, c // 2][:, (c % 2) * 128 : (c % 2) * 128 + 128] for g in range(groups)]
        update("qkv", c, jnp.concatenate(gs, axis=1))
    update("out", ..., jnp.concatenate([gatt_ref[g, 1][:, 128:] for g in range(groups)], axis=1))
    for f in range(chunks):
        cols = slice(f * HALF, (f + 1) * HALF)
        update("fc1", (slice(None), cols), ff(f, 0))
        update("fc2", (slice(None), cols), ff(f, 1))
    update("norm", ..., small_ref[0:4, :])
    update("bout", ..., small_ref[4:6, :])
    part = lax.axis_index("tp") * (NZ * NY * NCORE) + lax.axis_index("fsdp")
    width = ps["bqv"].shape[1]
    model = small_ref.shape[1]
    update("bqv", ..., pltpu.roll(small_ref[0:8, :], lax.rem(model - part * width, model), 1)[6:8, :width])
    width = ps["bfc1"].shape[1]
    per = model // width
    turned = pltpu.roll(small_ref[8:16, :], lax.rem(model - lax.rem(part, per) * width, model), 1)[:, :width]
    at_row = lax.broadcasted_iota(jnp.int32, turned.shape, 0)
    update("bfc1", ..., jnp.sum(jnp.where(at_row == part // per, turned, 0.0), axis=0, keepdims=True))


def sds(shape, dtype):
    return jax.ShapeDtypeStruct(shape, dtype)


def fused_device(
    tokens_in, out_grad, image_counts,
    norm_params, w_qkv, bias_qv, w_out, w_fc1, bias_fc1, w_fc2, bias_out,
    *moments,
):
    images, seq, model = tokens_in.shape
    sp = -(-seq // 16) * 16
    rows = images * sp
    own_rows, own_cols = w_qkv.shape[1], w_qkv.shape[2]
    groups = own_cols // 128
    chunks = w_fc1.shape[1] // HALF
    early, summed = 2, chunks - 3
    held = chunks - summed
    wide = NTP * HALF
    cube = (NZ, NY, NCORE, own_rows, wide)
    any_, vm, sm = pl.BlockSpec(memory_space=pl.ANY), pl.BlockSpec(memory_space=pltpu.VMEM), pl.BlockSpec(memory_space=pltpu.SMEM)
    dma = pltpu.SemaphoreType.DMA

    def params(k):
        return pltpu.CompilerParams(collective_id=k, has_side_effects=True, vmem_limit_bytes=VMEM_BYTES)

    n_ag = groups + early + 2
    flat_rows = images * seq

    def by_token(a):
        return a.transpose(1, 0, 2).reshape(flat_rows, model)

    def by_image(a):
        return a.reshape(seq, images, model).transpose(1, 0, 2)

    x_rows, og_rows = by_token(tokens_in), by_token(out_grad)
    qkv, ctx, mid, p, watt, wff, own, bias1 = pl.pallas_call(
        functools.partial(attention_kernel, (images, seq, sp, groups, groups + chunks, early)),
        name="attention",
        in_specs=[any_] + [vm] * 8,
        out_specs=[any_] * 7 + [vm],
        out_shape=[
            sds((groups, rows, model), BF16), sds((groups, rows, HALF), BF16), sds((model // 128, flat_rows, 128), F32),
            sds((groups, images, NTP, 2, sp, LANES), BF16), sds((groups, 2) + cube, BF16), sds((early, 2) + cube, BF16),
            sds((chunks - early, 2, own_rows, HALF), BF16), sds((chunks, 1, wide), F32),
        ],
        scratch_shapes=[
            pltpu.VMEM((flat_rows, model), BF16), pltpu.VMEM((rows, model), BF16),
            pltpu.VMEM((groups, rows, model), BF16), pltpu.VMEM((groups, rows, HALF), BF16),
            pltpu.VMEM((model // 128, flat_rows, 128), F32), pltpu.VMEM((groups, images, NTP, 2, sp, LANES), BF16),
            pltpu.VMEM((groups, 2) + cube, BF16), pltpu.VMEM((groups + chunks, 2, own_rows, HALF), BF16),
            pltpu.VMEM((NTP, NZ, NY, NCORE, 8, 128), F32), pltpu.VMEM((groups, 1, model), F32),
            dma((n_ag, 2, AG_SEMS)), dma((n_ag, 2, AG_SEMS)), dma((n_ag, 2)), dma((6,)), dma((6,)),
            dma((4, groups, 8)), dma((2 + groups,)),
        ],
        compiler_params=params(0),
    )(x_rows, norm_params, bias_out, w_qkv, w_out.T, w_fc1, w_fc2.T, bias_qv, bias_fc1.reshape(1, -1))

    late = chunks - early
    bo, dmid, grad_late, sums, b1g, gff = pl.pallas_call(
        functools.partial(feed_forward_kernel, (images, seq, sp, chunks, early, summed)),
        name="feed_forward",
        in_specs=[sm, vm, vm, vm] + [any_] * 4,
        out_specs=[any_] * 3 + [vm] * 3,
        out_shape=[
            sds((flat_rows, model), BF16), sds((model // 128, flat_rows, 128), F32),
            sds((held, 2) + cube, BF16), sds((8, model), F32), sds((chunks, 1, wide), F32),
            sds((summed, 2, own_rows, HALF), F32),
        ],
        scratch_shapes=[
            pltpu.VMEM((chunks, 2) + cube, BF16), pltpu.VMEM((late, 2, own_rows, HALF), BF16),
            pltpu.VMEM((rows, model), BF16), pltpu.VMEM((model, rows), BF16),
            pltpu.VMEM((rows, model), BF16), pltpu.VMEM((model, rows), BF16),
            pltpu.VMEM((flat_rows, model), F32), pltpu.VMEM((flat_rows, model), F32),
            pltpu.VMEM((rows, wide), BF16), pltpu.VMEM((rows, wide), BF16),
            pltpu.VMEM((2, 2) + cube, BF16), pltpu.VMEM((3, model // 128, flat_rows // 7, 128), F32),
        ]
        + scatter_scratch(summed, own_rows)
        + [
            dma((late, 2, AG_SEMS)), dma((late, 2, AG_SEMS)), dma((late, 2)), dma((2 + early,)), dma((3,)),
            dma((24,)),
        ],
        compiler_params=params(1),
    )(image_counts, norm_params, bias_out, bias1, mid, og_rows, wff, own)

    gt, glate, gatt, small = pl.pallas_call(
        functools.partial(attention_back_kernel, (images, seq, sp, groups, chunks, held)),
        name="attention_back",
        in_specs=[vm] * 3 + [any_] * 7,
        out_specs=[any_] + [vm] * 3,
        out_shape=[
            sds((flat_rows, model), F32), sds((held, 2, own_rows, HALF), F32),
            sds((groups, 2, own_rows, HALF), F32), sds((16, model), F32),
        ],
        scratch_shapes=[
            pltpu.VMEM((rows, model), BF16), pltpu.VMEM((model, rows), BF16),
            pltpu.VMEM((model // 128, flat_rows, 128), F32), pltpu.VMEM((groups, rows, model), BF16),
            pltpu.VMEM((groups, 2) + cube, BF16),
            pltpu.VMEM((rows, model), BF16), pltpu.VMEM((4 * sp, HALF), BF16),
            pltpu.VMEM((rows, HALF), BF16), pltpu.VMEM((HALF, rows), BF16),
            pltpu.VMEM((images, NTP, 2, sp, LANES), BF16), pltpu.VMEM((held, 2) + cube, BF16),
            pltpu.VMEM((flat_rows, model), BF16), pltpu.VMEM((2, model // 128, flat_rows // 7, 128), F32),
            pltpu.VMEM((2, flat_rows // 7, model), F32), pltpu.VMEM((groups, 1, model), F32),
            pltpu.VMEM((4, 16, model), F32), pltpu.VMEM((NZ * NY, 16, model), F32),
        ]
        + scatter_scratch(held + groups, own_rows)
        + [dma((10,)), dma((10,)), dma((3 + held,)), dma((1,)), dma((2, 2)), dma((2,)), dma((2,))],
        compiler_params=params(2),
    )(norm_params, sums, b1g, x_rows, dmid, grad_late, watt, qkv, ctx, p)

    turned = (3, 6)

    def flat(a, k):
        return a.reshape(1, -1) if a.ndim == 1 else a.T if k in turned else a

    weights = [flat(a, k) for k, a in enumerate((norm_params, w_qkv, bias_qv, w_out, w_fc1, bias_fc1, w_fc2, bias_out))]
    moments = [flat(a, k % 8) for k, a in enumerate(moments)]
    shapes = [sds(a.shape, F32) for a in weights]
    outs = pl.pallas_call(
        functools.partial(step_kernel, (groups, chunks, held)),
        name="adamw_step",
        in_specs=[vm] * 28,
        out_specs=[vm] * 32,
        out_shape=shapes * 4,
        compiler_params=pltpu.CompilerParams(vmem_limit_bytes=VMEM_BYTES),
    )(gff, glate, gatt, small, *weights, *moments)
    outs = [o.reshape(-1) if k % 8 == 5 else o.T if k % 8 in turned else o for k, o in enumerate(outs)]
    return (by_image(bo), by_image(gt)) + tuple(outs)


def solution(mesh):
    placed = (
        P(("fsdp", "tp"), None, None),
        P(("fsdp", "tp"), None, None),
        P("fsdp"),
        P(),
        P(None, "fsdp", "tp"),
        P(None, ("tp", "fsdp")),
        P("tp", "fsdp"),
        P("fsdp", "tp"),
        P(("tp", "fsdp")),
        P("tp", "fsdp"),
        P(),
        P(),
        P(None, "fsdp", "tp"),
        P(None, ("tp", "fsdp")),
        P("tp", "fsdp"),
        P("fsdp", "tp"),
        P(("tp", "fsdp")),
        P("tp", "fsdp"),
        P(),
        P(),
        P(None, "fsdp", "tp"),
        P(None, ("tp", "fsdp")),
        P("tp", "fsdp"),
        P("fsdp", "tp"),
        P(("tp", "fsdp")),
        P("tp", "fsdp"),
        P(),
    )
    fits = mesh.shape["fsdp"] == NZ * NY * NCORE and mesh.shape["tp"] == NTP
    return jax.shard_map(
        fused_device if fits else per_device,
        mesh=mesh,
        in_specs=placed,
        out_specs=(
            P(("fsdp", "tp"), None, None),
            P(("fsdp", "tp"), None, None),
            P(),
            P(None, "fsdp", "tp"),
            P(None, ("tp", "fsdp")),
            P("tp", "fsdp"),
            P("fsdp", "tp"),
            P(("tp", "fsdp")),
            P("tp", "fsdp"),
            P(),
            P(),
            P(None, "fsdp", "tp"),
            P(None, ("tp", "fsdp")),
            P("tp", "fsdp"),
            P("fsdp", "tp"),
            P(("tp", "fsdp")),
            P("tp", "fsdp"),
            P(),
            P(),
            P(None, "fsdp", "tp"),
            P(None, ("tp", "fsdp")),
            P("tp", "fsdp"),
            P("fsdp", "tp"),
            P(("tp", "fsdp")),
            P("tp", "fsdp"),
            P(),
            P(),
            P(None, "fsdp", "tp"),
            P(None, ("tp", "fsdp")),
            P("tp", "fsdp"),
            P("fsdp", "tp"),
            P(("tp", "fsdp")),
            P("tp", "fsdp"),
            P(),
        ),
        check_vma=False,
    )
```

```python
import functools

import jax
import jax.numpy as jnp
from jax import lax
from jax.experimental import pallas as pl
from jax.experimental.pallas import tpu as pltpu
from jax.sharding import PartitionSpec as P

HEAD_DIM = 64
ADAM_STEP = 10


norm_eps = 1e-06
learn_rate = 0.02
beta_one = 0.9
beta_two = 0.999
adam_eps = 1e-08
decay_rate = 0.05


def layer_norm(rows_in, gain_vec, shift_vec):
    centre = rows_in - jnp.mean(rows_in, axis=-1, keepdims=True)
    spread = jnp.mean(centre * centre, axis=-1, keepdims=True)
    return centre * lax.rsqrt(spread + norm_eps) * gain_vec + shift_vec


def exact_gelu(rows_in):
    return jax.nn.gelu(rows_in, approximate=False)


def adamw(parameter, gradient, moment_one, moment_two, decay_on):
    one_new = beta_one * moment_one + (1.0 - beta_one) * gradient
    two_new = beta_two * moment_two + (1.0 - beta_two) * gradient * gradient
    one_hat = one_new / (1.0 - beta_one**ADAM_STEP)
    two_hat = two_new / (1.0 - beta_two**ADAM_STEP)
    update = one_hat / (jnp.sqrt(two_hat) + adam_eps) + decay_on * parameter
    return (-learn_rate * update, one_new, two_new)


def per_device(
    tokens_in,
    out_grad,
    image_counts,
    norm_params,
    w_qkv,
    bias_qv,
    w_out,
    w_fc1,
    bias_fc1,
    w_fc2,
    bias_out,
    first_norm,
    first_qkv,
    first_bias_qv,
    first_out,
    first_fc1,
    first_bias_fc1,
    first_fc2,
    first_bias_out,
    second_norm,
    second_qkv,
    second_bias_qv,
    second_out,
    second_fc1,
    second_bias_fc1,
    second_fc2,
    second_bias_out,
):
    images = tokens_in.shape[0]
    seq_len = tokens_in.shape[1]
    score_scale = HEAD_DIM ** (-0.5)
    inputs = tokens_in.astype(jnp.float32)
    slot_ids = lax.axis_index("tp") * images + jnp.arange(images)
    live_mask = (slot_ids < image_counts[0]).astype(jnp.float32)
    live_grad = out_grad.astype(jnp.float32) * live_mask[:, None, None]
    qkv_all, bqv_all, wout_all = (
        lax.all_gather(w_qkv.astype(jnp.bfloat16), "fsdp", axis=1, tiled=True),
        lax.all_gather(bias_qv.astype(jnp.bfloat16), "fsdp", axis=1, tiled=True),
        lax.all_gather(w_out.astype(jnp.bfloat16), "fsdp", axis=1, tiled=True),
    )
    fc1_all, bfc1_all, fc2_all = (
        lax.all_gather(w_fc1.astype(jnp.bfloat16), "fsdp", axis=0, tiled=True),
        lax.all_gather(bias_fc1.astype(jnp.bfloat16), "fsdp", axis=0, tiled=True),
        lax.all_gather(w_fc2.astype(jnp.bfloat16), "fsdp", axis=1, tiled=True),
    )
    hidden_one = layer_norm(inputs, norm_params[0], norm_params[1]).astype(jnp.bfloat16)
    qkv_use, bqv_use, wout_use = (
        lax.all_gather(qkv_all, "tp", axis=2, tiled=True),
        lax.all_gather(bqv_all, "tp", axis=1, tiled=True),
        lax.all_gather(wout_all, "tp", axis=0, tiled=True),
    )
    group_images = hidden_one.shape[0]
    projected = jnp.einsum("gsd,cdf->cgsf", hidden_one, qkv_use, preferred_element_type=jnp.float32)
    width_local = projected.shape[3]
    shape_heads = (group_images, seq_len, width_local // HEAD_DIM, HEAD_DIM)
    queries = (projected[0] + bqv_use[0]).astype(jnp.bfloat16).reshape(shape_heads)
    key_vecs = projected[1].astype(jnp.bfloat16).reshape(shape_heads)
    value_vecs = (projected[2] + bqv_use[1]).astype(jnp.bfloat16).reshape(shape_heads)
    scores = (
        jnp.einsum("gqhe,gkhe->ghqk", queries, key_vecs, preferred_element_type=jnp.float32)
        * score_scale
    )
    log_total = jax.nn.logsumexp(scores, axis=-1, keepdims=True)
    probs_low = jnp.exp(scores - log_total).astype(jnp.bfloat16)
    context = jnp.einsum(
        "ghqk,gkhe->gqhe", probs_low, value_vecs, preferred_element_type=jnp.float32
    )
    context = context.astype(jnp.bfloat16).reshape(group_images, seq_len, width_local)
    attn_part = jnp.einsum("gsf,fd->gsd", context, wout_use, preferred_element_type=jnp.float32)
    middle = inputs + attn_part + bias_out[0]
    hidden_two = layer_norm(middle, norm_params[2], norm_params[3]).astype(jnp.bfloat16)
    mlp_in = lax.all_gather(hidden_two, "tp", axis=0, tiled=True)
    fc1_use, bfc1_use, fc2_use = (fc1_all, bfc1_all, fc2_all)
    pre_act = (
        jnp.einsum("gsd,df->gsf", mlp_in, fc1_use, preferred_element_type=jnp.float32) + bfc1_use
    )
    activated = exact_gelu(pre_act).astype(jnp.bfloat16)
    mlp_part = jnp.einsum("gsf,fd->gsd", activated, fc2_use, preferred_element_type=jnp.float32)
    mlp_sum = lax.psum_scatter(
        mlp_part.astype(jnp.bfloat16), "tp", scatter_dimension=0, tiled=True
    ).astype(jnp.float32)
    block_out = (middle + mlp_sum + bias_out[1]).astype(jnp.bfloat16)
    grad_mlp = live_grad.astype(jnp.bfloat16)
    grad_mlp_in = lax.all_gather(grad_mlp, "tp", axis=0, tiled=True)
    grad_w2 = jnp.einsum("gsf,gsd->fd", activated, grad_mlp_in, preferred_element_type=jnp.float32)
    grad_act = jnp.einsum("gsd,fd->gsf", grad_mlp_in, fc2_use, preferred_element_type=jnp.float32)
    gelu_out, gelu_pull = jax.vjp(exact_gelu, pre_act)
    grad_pre = gelu_pull(grad_act)[0].astype(jnp.bfloat16)
    grad_b1 = jnp.sum(grad_pre.astype(jnp.float32), axis=(0, 1))
    grad_w1 = jnp.einsum("gsd,gsf->df", mlp_in, grad_pre, preferred_element_type=jnp.float32)
    grad_h2_part = jnp.einsum("gsf,df->gsd", grad_pre, fc1_use, preferred_element_type=jnp.float32)
    grad_h2 = lax.psum_scatter(
        grad_h2_part.astype(jnp.bfloat16), "tp", scatter_dimension=0, tiled=True
    ).astype(jnp.float32)
    norm_two, norm_two_pull = jax.vjp(layer_norm, middle, norm_params[2], norm_params[3])
    grad_mid_ln, grad_gain_two, grad_shift_two = norm_two_pull(grad_h2)
    grad_middle = live_grad + grad_mid_ln
    grad_attn = grad_middle.astype(jnp.bfloat16)
    grad_wo = jnp.einsum("gsf,gsd->fd", context, grad_attn, preferred_element_type=jnp.float32)
    grad_ctx = jnp.einsum("gsd,fd->gsf", grad_attn, wout_use, preferred_element_type=jnp.float32)
    grad_ctx = grad_ctx.astype(jnp.bfloat16).reshape(shape_heads)
    scores_again = (
        jnp.einsum("gqhe,gkhe->ghqk", queries, key_vecs, preferred_element_type=jnp.float32)
        * score_scale
    )
    probs_again = jnp.exp(scores_again - log_total)
    grad_probs = jnp.einsum(
        "gqhe,gkhe->ghqk", grad_ctx, value_vecs, preferred_element_type=jnp.float32
    )
    row_terms = jnp.sum(probs_again * grad_probs, axis=-1, keepdims=True)
    grad_scores = (probs_again * (grad_probs - row_terms)).astype(jnp.bfloat16)
    grad_query = (
        jnp.einsum("ghqk,gkhe->gqhe", grad_scores, key_vecs, preferred_element_type=jnp.float32)
        * score_scale
    ).astype(jnp.bfloat16)
    grad_keys = (
        jnp.einsum("ghqk,gqhe->gkhe", grad_scores, queries, preferred_element_type=jnp.float32)
        * score_scale
    ).astype(jnp.bfloat16)
    grad_values = jnp.einsum(
        "ghqk,gqhe->gkhe",
        probs_again.astype(jnp.bfloat16),
        grad_ctx,
        preferred_element_type=jnp.float32,
    ).astype(jnp.bfloat16)
    grad_proj = jnp.stack([grad_query, grad_keys, grad_values]).reshape(
        3, group_images, seq_len, width_local
    )
    grad_bqv = jnp.stack(
        [
            jnp.sum(grad_proj[0].astype(jnp.float32), axis=(0, 1)),
            jnp.sum(grad_proj[2].astype(jnp.float32), axis=(0, 1)),
        ]
    )
    grad_wqkv = jnp.einsum(
        "gsd,cgsf->cdf", hidden_one, grad_proj, preferred_element_type=jnp.float32
    )
    grad_h1_part = jnp.einsum(
        "cgsf,cdf->gsd", grad_proj, qkv_use, preferred_element_type=jnp.float32
    )
    grad_wqkv, grad_bqv, grad_wo = (
        lax.psum_scatter(
            grad_wqkv.astype(jnp.bfloat16), "tp", scatter_dimension=2, tiled=True
        ).astype(jnp.float32),
        lax.psum_scatter(
            grad_bqv.astype(jnp.bfloat16), "tp", scatter_dimension=1, tiled=True
        ).astype(jnp.float32),
        lax.psum_scatter(
            grad_wo.astype(jnp.bfloat16), "tp", scatter_dimension=0, tiled=True
        ).astype(jnp.float32),
    )
    norm_one, norm_one_pull = jax.vjp(layer_norm, inputs, norm_params[0], norm_params[1])
    grad_in_ln, grad_gain_one, grad_shift_one = norm_one_pull(grad_h1_part)
    grad_tokens = grad_middle + grad_in_ln
    g_qkv, g_bqv, g_out, g_fc1, g_bfc1, g_fc2 = (
        lax.psum_scatter(grad_wqkv, "fsdp", scatter_dimension=1, tiled=True),
        lax.psum_scatter(grad_bqv, "fsdp", scatter_dimension=1, tiled=True),
        lax.psum_scatter(grad_wo, "fsdp", scatter_dimension=1, tiled=True),
        lax.psum_scatter(grad_w1, "fsdp", scatter_dimension=0, tiled=True),
        lax.psum_scatter(grad_b1, "fsdp", scatter_dimension=0, tiled=True),
        lax.psum_scatter(grad_w2, "fsdp", scatter_dimension=1, tiled=True),
    )
    norm_terms = jnp.stack([grad_gain_one, grad_shift_one, grad_gain_two, grad_shift_two])
    bias_terms = jnp.stack([jnp.sum(grad_middle, axis=(0, 1)), jnp.sum(live_grad, axis=(0, 1))])
    g_norm, g_bout = lax.psum((norm_terms, bias_terms), ("fsdp", "tp"))
    s_norm, a_norm, b_norm = adamw(norm_params, g_norm, first_norm, second_norm, 0.0)
    s_qkv, a_qkv, b_qkv = adamw(w_qkv, g_qkv, first_qkv, second_qkv, decay_rate)
    s_bqv, a_bqv, b_bqv = adamw(bias_qv, g_bqv, first_bias_qv, second_bias_qv, 0.0)
    s_out, a_out, b_out = adamw(w_out, g_out, first_out, second_out, decay_rate)
    s_fc1, a_fc1, b_fc1 = adamw(w_fc1, g_fc1, first_fc1, second_fc1, decay_rate)
    s_bfc1, a_bfc1, b_bfc1 = adamw(bias_fc1, g_bfc1, first_bias_fc1, second_bias_fc1, 0.0)
    s_fc2, a_fc2, b_fc2 = adamw(w_fc2, g_fc2, first_fc2, second_fc2, decay_rate)
    s_bout, a_bout, b_bout = adamw(bias_out, g_bout, first_bias_out, second_bias_out, 0.0)
    return (
        block_out,
        grad_tokens,
        g_norm,
        g_qkv,
        g_bqv,
        g_out,
        g_fc1,
        g_bfc1,
        g_fc2,
        g_bout,
        s_norm,
        w_qkv + s_qkv,
        s_bqv,
        s_out,
        w_fc1 + s_fc1,
        s_bfc1,
        w_fc2 + s_fc2,
        s_bout,
        a_norm,
        a_qkv,
        a_bqv,
        a_out,
        a_fc1,
        a_bfc1,
        a_fc2,
        a_bout,
        b_norm,
        b_qkv,
        b_bqv,
        b_out,
        b_fc1,
        b_bfc1,
        b_fc2,
        b_bout,
    )


F32, BF16 = jnp.float32, jnp.bfloat16
MESH_IDS = pl.DeviceIdType.MESH
VMEM_BYTES = 62 * 2**20

NZ, NY, NCORE, NTP = 4, 2, 2, 2
HALF = 256
NEG = -1e30
LANES = 256


def dot(a, b, ca, cb):
    return lax.dot_general(a, b, (((ca,), (cb,)), ((), ())), preferred_element_type=F32)


def normed(v):
    centre = v - jnp.mean(v, axis=-1, keepdims=True)
    rstd = lax.rsqrt(jnp.mean(centre * centre, axis=-1, keepdims=True) + norm_eps)
    return centre * rstd, rstd


def norm_back(e, gain, xhat, rstd):
    eg = e * gain
    m1 = jnp.mean(eg, axis=-1, keepdims=True)
    m2 = jnp.mean(eg * xhat, axis=-1, keepdims=True)
    return rstd * (eg - m1 - xhat * m2)


def pad_rows(v, rows):
    return jnp.concatenate([v, jnp.zeros((rows - v.shape[0], v.shape[1]), v.dtype)], axis=0)


def load_columns(ref, r):
    return jnp.concatenate([ref[j, r, :] for j in range(ref.shape[0])], axis=1)


def store_columns(ref, r, v):
    for j in range(ref.shape[0]):
        ref[j, r, :] = v[:, 128 * j : 128 * j + 128]


class Place:
    def __init__(self):
        f = lax.axis_index("fsdp")
        self.x = lax.axis_index("tp")
        self.z = f // (NY * NCORE)
        self.y = lax.rem(f // NCORE, NY)
        self.c = lax.rem(f, NCORE)
        self.sib = self.at(self.z, self.y, 1 - self.c, self.x)
        self.peer_x = self.at(self.z, self.y, self.c, 1 - self.x)
        self.peer_y = self.at(self.z, 1 - self.y, self.c, self.x)
        self.other_z = [lax.rem(self.z + d, NZ) for d in range(1, NZ)]
        self.peers_z = [self.at(o, self.y, self.c, self.x) for o in self.other_z]
        self.quad = 2 * self.x + self.c
        self.quad_peers = [
            self.at(self.z, self.y, lax.rem(self.c + k, 2), lax.rem(self.x + k // 2, 2))
            for k in range(1, 4)
        ]
        self.line = self.z * NY + self.y
        self.line_peers = []
        for k in range(1, NZ * NY):
            other = lax.rem(self.line + k, NZ * NY)
            self.line_peers.append(self.at(other // NY, lax.rem(other, NY), self.c, self.x))
        self.lanes = pl.ds(pl.multiple_of(self.x * HALF, HALF), HALF)
        self.lanes_other = pl.ds(pl.multiple_of((1 - self.x) * HALF, HALF), HALF)

    def pick(self, v):
        return jnp.where(self.x == 0, v[..., :HALF], v[..., HALF:])

    def at(self, z, y, c, x):
        return {"fsdp": (z * NY + y) * NCORE + c, "tp": x}

    def barrier(self, everyone=None):
        sem = pltpu.get_barrier_semaphore()
        everyone = everyone or [self.sib, self.peer_x, self.peer_y] + self.peers_z
        for d in everyone:
            pl.semaphore_signal(sem, inc=1, device_id=d, device_id_type=MESH_IDS)
        pl.semaphore_wait(sem, len(everyone))


def remote(src, dst, send, recv, device):
    return pltpu.make_async_remote_copy(
        src_ref=src, dst_ref=dst, send_sem=send, recv_sem=recv, device_id=device, device_id_type=MESH_IDS
    )


def start_all(copies):
    for k in copies:
        k.start()


def wait_all(copies):
    for k in copies:
        k.wait()


AG_SEMS = 7


def gather_steps(at, buf, own, send, recv, local, y_first, part=slice(None)):
    x, y, z, c, lanes = at.x, at.y, at.z, at.c, at.lanes
    own = own.at[part]
    mine = buf.at[z, y, c, part, lanes]
    keep = pltpu.make_async_copy(own, mine, local)
    s0 = [remote(own, mine, send.at[d], recv.at[d], at.peers_z[d]) for d in range(NZ - 1)]
    line = buf.at[:, y, c, part, lanes]
    s1 = remote(line, line, send.at[3], recv.at[3], at.peer_y if y_first else at.peer_x)
    if y_first:
        plane, rest = buf.at[:, :, c, part, lanes], buf.at[:, :, c, part, at.lanes_other]
    else:
        plane, rest = buf.at[:, y, c, part], buf.at[:, 1 - y, c, part]
    s2 = remote(plane, plane, send.at[4], recv.at[4], at.peer_x if y_first else at.peer_y)
    sib_a = remote(plane, plane, send.at[5], recv.at[5], at.sib)
    sib_b = remote(rest, rest, send.at[6], recv.at[6], at.sib)

    def step0():
        keep.start()
        start_all(s0)

    def step1():
        keep.wait()
        wait_all(s0)
        s1.start()

    def step2():
        s1.wait()
        s2.start()
        sib_a.start()

    def step3():
        s2.wait()
        sib_b.start()

    def step4():
        sib_a.wait()
        sib_b.wait()

    return [step0, step1, step2, step3, step4]


RS_SEMS = 6


def scatter_steps(at, grad, r0, r1, r2, r3, out, send, recv, x_first):
    x, y, z, c = at.x, at.y, at.z, at.c
    s0 = remote(grad.at[:, :, 1 - c], r0, send.at[0], recv.at[0], at.sib)
    if x_first:
        s1 = remote(r0.at[:, :, :, at.lanes_other], r1, send.at[1], recv.at[1], at.peer_x)
        s2 = remote(r1.at[:, 1 - y], r2, send.at[2], recv.at[2], at.peer_y)
    else:
        s1 = remote(r0.at[:, 1 - y], r1, send.at[1], recv.at[1], at.peer_y)
        s2 = remote(r1.at[:, :, at.lanes_other], r2, send.at[2], recv.at[2], at.peer_x)
    s3 = [
        remote(r2.at[at.other_z[d]], r3.at[d], send.at[3 + d], recv.at[3 + d], at.peers_z[d])
        for d in range(NZ - 1)
    ]

    def add(a, b):
        return (a.astype(F32) + b.astype(F32)).astype(BF16)

    def step0():
        s0.start()

    def step1():
        s0.wait()

        def body(k, _):
            r0[k] = add(r0[k], grad[k, :, c])
            return 0

        lax.fori_loop(0, NZ, body, 0)
        s1.start()

    def step2():
        s1.wait()

        def body(k, _):
            r1[k] = add(r1[k], at.pick(r0[k]) if x_first else r0[k, y])
            return 0

        lax.fori_loop(0, NZ, body, 0)
        s2.start()

    def step3():
        s2.wait()

        def body(k, _):
            r2[k] = add(r2[k], r1[k, y] if x_first else at.pick(r1[k]))
            return 0

        lax.fori_loop(0, NZ, body, 0)
        start_all(s3)

    def step4():
        wait_all(s3)
        total = r2[z].astype(F32)
        for d in range(NZ - 1):
            total = total + r3[d].astype(F32)
        out[...] = total

    return [step0, step1, step2, step3, step4]


def scatter_scratch(chunks, rows):
    wide = NTP * HALF
    return [
        pltpu.VMEM((chunks, 2, NZ, NY, rows, wide), BF16),
        pltpu.VMEM((chunks, NZ, NY, rows, HALF), BF16),
        pltpu.VMEM((chunks, NZ, rows, wide), BF16),
        pltpu.VMEM((chunks, 2, NZ, rows, HALF), BF16),
        pltpu.VMEM((chunks, 2, NZ - 1, rows, HALF), BF16),
        pltpu.SemaphoreType.DMA((chunks, 2, RS_SEMS)),
        pltpu.SemaphoreType.DMA((chunks, 2, RS_SEMS)),
    ]


def scatter_both(at, k, grads, scratch, outs):
    r0, r1a, r1b, r2, r3, send, recv = scratch
    first = scatter_steps(
        at, grads[0], r0.at[k, 0], r1a.at[k], r2.at[k, 0], r3.at[k, 0], outs[0], send.at[k, 0], recv.at[k, 0], True
    )
    second = scatter_steps(
        at, grads[1], r0.at[k, 1], r1b.at[k], r2.at[k, 1], r3.at[k, 1], outs[1], send.at[k, 1], recv.at[k, 1], False
    )
    return [both(a, b) for a, b in zip(first, second)]


def both(a, b):
    def run():
        a()
        b()

    return run


def gather_both(at, buf, own, sems, part=slice(None)):
    send, recv, local = sems
    first = gather_steps(at, buf.at[0], own.at[0], send.at[0], recv.at[0], local.at[0], True, part)
    second = gather_steps(at, buf.at[1], own.at[1], send.at[1], recv.at[1], local.at[1], False, part)
    return [both(a, b) for a, b in zip(first, second)]


def run_slot(plan, key, counters):
    for want, steps in plan.get(key, {}).items():
        cond = None
        for have, value in zip(counters, want):
            test = have == value
            cond = test if cond is None else jnp.logical_and(cond, test)

        def go(steps=steps):
            for s in steps:
                s()

        pl.when(cond)(go)


def planned(entries):
    plan = {}
    for key, want, step in entries:
        plan.setdefault(key, {}).setdefault(want, []).append(step)
    return plan


def matrix(ref):
    v = ref[...]
    return v.reshape(v.shape[0] * v.shape[1] * v.shape[2] * v.shape[3], v.shape[4])


def left_half(rows):
    return lax.broadcasted_iota(jnp.int32, (rows, 2 * HEAD_DIM), 1) < HEAD_DIM


def split_heads(v, left):
    zero = jnp.zeros_like(v)
    return jnp.concatenate([jnp.where(left, v, zero), jnp.where(left, zero, v)], axis=0)


def projection(a, b):
    return jnp.concatenate([a, b[:, 0:128], b[:, HALF : HALF + 128]], axis=1)


def out_columns(b):
    return jnp.concatenate([b[:, 128:HALF], b[:, HALF + 128 :]], axis=1)


def spread(pieces, width, row, total):
    col = lax.broadcasted_iota(jnp.int32, (128, total), 1).astype(F32)
    lane = lax.broadcasted_iota(jnp.int32, (128, total), 0).astype(F32)
    owner = jnp.floor((col + 0.5) * (1.0 / width))
    pick = (col - owner * width == lane).astype(BF16)
    spreaded = dot(pieces.astype(BF16), pick, 1, 0)
    at_row = lax.broadcasted_iota(jnp.int32, spreaded.shape, 0).astype(F32)
    col = lax.broadcasted_iota(jnp.int32, spreaded.shape, 1).astype(F32)
    owner = jnp.floor((col + 0.5) * (1.0 / width))
    return jnp.sum(jnp.where(at_row == owner * 8.0 + row, spreaded, 0.0), axis=0, keepdims=True)


def attention_kernel(
    dims,
    x_hbm, norm_ref, bout_ref, wqkv_ref, wout_ref, wfc1_ref, wfc2_ref, bqv_ref, bfc1_ref,
    qkv_hbm, ctx_hbm, mid_hbm, p_hbm, watt_hbm, wff_hbm, own_hbm, bias_ref,
    x_s, h1, qkv_s, ctx_s, mid_s, p_s, watt, own, pieces, bias_s,
    ag_send, ag_recv, ag_local, sm_send, sm_recv, out_sem, in_sem,
):
    images, seq, sp, groups, chunks, early = dims
    at = Place()
    x_copy = pltpu.make_async_copy(x_hbm, x_s, in_sem.at[0])
    x_copy.start()
    own_rows = wqkv_ref.shape[2]
    rows = images * seq
    for g in range(groups):
        cols = slice(128 * g, 128 * g + 128)
        own[g, 0] = jnp.concatenate([wqkv_ref[0, :, cols], wqkv_ref[1, :, cols]], axis=1).astype(BF16)
        own[g, 1] = jnp.concatenate([wqkv_ref[2, :, cols], wout_ref[:, cols]], axis=1).astype(BF16)
    pieces[at.x, at.z, at.y, at.c] = jnp.zeros((8, 128), F32)
    pieces[at.x, at.z, at.y, at.c, 0:1, 0 : bfc1_ref.shape[1]] = bfc1_ref[...]
    pieces[at.x, at.z, at.y, at.c, 1:3, 0 : bqv_ref.shape[1]] = bqv_ref[...]

    def sems(k):
        return ag_send.at[k], ag_recv.at[k], ag_local.at[k]

    third = own.shape[2] // 3
    head = [
        gather_both(at, watt.at[0], own.at[0], sems(k), pl.ds(j * third, third))
        for j, k in enumerate((0, groups + early, groups + early + 1))
    ]
    steps = [[None] * 5] + [gather_both(at, watt.at[g], own.at[g], sems(g)) for g in range(1, groups)]
    steps += [gather_both(at, wff_hbm.at[f], own.at[groups + f], sems(groups + f)) for f in range(early)]
    here = pieces.at[at.x, at.z, at.y, at.c]
    line = pieces.at[at.x, :, at.y, at.c]
    plane = pieces.at[at.x, :, :, at.c]
    cube = pieces.at[:, :, :, at.c]
    bias_steps = [[remote(here, here, sm_send.at[d], sm_recv.at[d], at.peers_z[d]) for d in range(NZ - 1)]]
    bias_steps += [
        [remote(r, r, sm_send.at[3 + k], sm_recv.at[3 + k], d)]
        for k, (r, d) in enumerate([(line, at.peer_y), (plane, at.peer_x), (cube, at.sib)])
    ]

    def head_step(k):
        for part in head:
            part[k]()

    at.barrier()
    head_step(0)
    start_all(bias_steps[0])
    steps[1][0]()
    steps[2][0]()
    for f in range(chunks - groups):
        cols = slice(HALF * f, HALF * f + HALF)
        own[groups + f, 0] = wfc1_ref[:, cols].astype(BF16)
        own[groups + f, 1] = wfc2_ref[:, cols].astype(BF16)
    late = pltpu.make_async_copy(own.at[pl.ds(groups + early, chunks - groups - early)], own_hbm, in_sem.at[1])
    late.start()
    x_copy.wait()

    block = rows // 7

    def first_norm(j, _):
        r = pl.ds(pl.multiple_of(j * block, 16), block)
        xhat, _r = normed(x_s[r, :].astype(F32))
        store_columns(mid_s, r, xhat * norm_ref[0:1, :] + norm_ref[1:2, :])
        return 0

    def by_image(i, _):
        h = pad_rows(load_columns(mid_s, pl.ds(i, seq, stride=images)), sp)
        h1[pl.ds(pl.multiple_of(i * sp, 16), sp), :] = h.astype(BF16)
        return 0

    head_step(1)
    wait_all(bias_steps[0])
    start_all(bias_steps[1])
    lax.fori_loop(0, 7, first_norm, 0)
    head_step(2)
    wait_all(bias_steps[1])
    start_all(bias_steps[2])
    lax.fori_loop(0, images, by_image, 0)
    steps[1][1]()
    head_step(3)
    wait_all(bias_steps[2])
    start_all(bias_steps[3])
    wait_all(bias_steps[3])
    flat = pieces[...].reshape(NTP * NZ * NY * NCORE * 8, 128)
    width = bqv_ref.shape[1]
    model = width * NTP * NZ * NY * NCORE
    bias_q = spread(flat, width, 1.0, model)
    bias_v = spread(flat, width, 2.0, model)
    for g in range(groups):
        parts = []
        for t in range(NTP):
            parts += [bias_q[:, t * own_rows + 128 * g : t * own_rows + 128 * g + 128], jnp.zeros((1, 128), F32)]
        for t in range(NTP):
            parts.append(bias_v[:, t * own_rows + 128 * g : t * own_rows + 128 * g + 128])
        bias_s[g] = jnp.concatenate(parts, axis=1)
    width = bfc1_ref.shape[1]
    bias_ff = spread(flat, width, 0.0, width * NTP * NZ * NY * NCORE)
    per = bias_ff.shape[1] // NTP
    for f in range(chunks - groups):
        bias_ref[f] = jnp.concatenate(
            [bias_ff[:, t * per + f * HALF : t * per + f * HALF + HALF] for t in range(NTP)], axis=1
        )
    head_step(4)

    when = {1: [None, None, 1, 4.1, 4.2], 2: [None, 2, 4, 7, 8]}
    when.update({groups + f: ns for f, ns in enumerate([[1.5, 5, 8.5, 11, 14], [5, 9, 12, 14.1, 14.2]])})
    entries = sorted((n, k, j) for k, ns in when.items() for j, n in enumerate(ns) if n is not None)
    entries = [(int(n), k, j) for n, k, j in entries]
    last = 4 * groups + 2
    plan = planned(
        [("out", (n - 4 * groups,), steps[k][j]) if n >= 4 * groups else (n % 2, (n // 4, n % 4 // 2), steps[k][j])
         for n, k, j in entries if n < last]
    )
    remains = [steps[k][j] for n, k, j in entries if n >= last]

    quad = 4
    tr = quad * sp
    left = left_half(sp)
    full = seq // 16 * 16
    live_key = lax.broadcasted_iota(jnp.int32, (sp - full, LANES), 0) < seq - full
    tiles = images // quad
    units = [(a, t) for a in range(quad) for t in range(NTP)]

    def soften(s):
        s = jnp.concatenate([s[:full], jnp.where(live_key, s[full:], NEG)], axis=0)
        e = jnp.exp(s - jnp.max(s, axis=0, keepdims=True))
        return (e * (1.0 / jnp.sum(e, axis=0, keepdims=True))).astype(BF16)

    def group(g, _):
        def tile(i, _):
            run_slot(plan, 0, (g, i))
            r = pl.ds(pl.multiple_of(i * tr, 16), tr)
            w = projection(matrix(watt.at[g, 0]), matrix(watt.at[g, 1]))
            qkv_s[g, r, :] = (dot(h1[r, :], w, 1, 0) + bias_s[g]).astype(BF16)
            run_slot(plan, 1, (g, i))
            qkv = qkv_s[g, r, :]

            def cut(a, first):
                return qkv[a * sp : (a + 1) * sp, first : first + 128]

            scores = []
            for a, t in units:
                q = pad_rows(cut(a, t * HALF) * jnp.asarray(HEAD_DIM ** (-0.5), BF16), LANES)
                scores.append(dot(split_heads(cut(a, t * HALF + 128), left), q, 1, 1))
            probs = []
            for (a, t), s in zip(units, scores):
                probs.append([soften(s[h * sp : (h + 1) * sp]) for h in range(2)])
                for h in range(2):
                    p_s[g, i * quad + a, t, h] = probs[-1][h]
            for (a, t), p in zip(units, probs):
                vt = cut(a, 2 * HALF + t * 128).T
                cs = [dot(vt[h * HEAD_DIM : (h + 1) * HEAD_DIM], p[h], 1, 0) for h in range(2)]
                mine = pl.ds(pl.multiple_of(i * tr + a * sp, 16), sp)
                ctx_s[g, mine, t * 128 : (t + 1) * 128] = jnp.concatenate(cs, axis=0).T[:sp].astype(BF16)
            pltpu.make_async_copy(qkv_s.at[g, r], qkv_hbm.at[g, r], out_sem.at[0, g, i]).start()
            pltpu.make_async_copy(ctx_s.at[g, r], ctx_hbm.at[g, r], out_sem.at[1, g, i]).start()
            im = pl.ds(i * quad, quad)
            pltpu.make_async_copy(p_s.at[g, im], p_hbm.at[g, im], out_sem.at[2, g, i]).start()
            return 0

        lax.fori_loop(0, tiles, tile, 0)
        pltpu.make_async_copy(watt.at[g], watt_hbm.at[g], in_sem.at[2 + g]).start()
        return 0

    lax.fori_loop(0, groups, group, 0)

    def project_out(i, _):
        run_slot(plan, "out", (i,))
        r = pl.ds(pl.multiple_of(i * tr, 16), tr)
        w = jnp.concatenate([out_columns(matrix(watt.at[g, 1])) for g in range(groups)], axis=1)
        c = jnp.concatenate([ctx_s[g, r, :] for g in range(groups)], axis=1)
        attn = dot(c, w, 1, 1)
        for a in range(quad):
            store_columns(mid_s, pl.ds(i * quad + a, seq, stride=images), attn[a * sp : a * sp + seq])
        return 0

    lax.fori_loop(0, tiles, project_out, 0)

    def residual(j, _):
        r = pl.ds(pl.multiple_of(j * block, 16), block)
        store_columns(mid_s, r, load_columns(mid_s, r) + x_s[r, :].astype(F32) + bout_ref[0:1, :])
        pltpu.make_async_copy(mid_s.at[:, r], mid_hbm.at[:, r], out_sem.at[3, 0, j]).start()
        return 0

    lax.fori_loop(0, 7, residual, 0)
    for step in remains:
        step()

    def drain(k, _):
        g, i = k // tiles, lax.rem(k, tiles)
        r = pl.ds(pl.multiple_of(i * tr, 16), tr)
        pltpu.make_async_copy(qkv_s.at[g, r], qkv_hbm.at[g, r], out_sem.at[0, g, i]).wait()
        pltpu.make_async_copy(ctx_s.at[g, r], ctx_hbm.at[g, r], out_sem.at[1, g, i]).wait()
        im = pl.ds(i * quad, quad)
        pltpu.make_async_copy(p_s.at[g, im], p_hbm.at[g, im], out_sem.at[2, g, i]).wait()
        return 0

    lax.fori_loop(0, groups * tiles, drain, 0)
    for g in range(groups):
        pltpu.make_async_copy(watt.at[g], watt_hbm.at[g], in_sem.at[2 + g]).wait()
    for j in range(7):
        r = pl.ds(j * block, block)
        pltpu.make_async_copy(mid_s.at[:, r], mid_hbm.at[:, r], out_sem.at[3, 0, j]).wait()
    late.wait()


def feed_forward_kernel(
    dims,
    counts_ref, norm_ref, bout_ref, bias_ref, mid_hbm, og_hbm, wff_hbm, own_hbm,
    bo_hbm, dmid_hbm, late_hbm, sums_ref, b1g_ref, gff_ref,
    wff, own, h2, h2t, dm, dmt, mlp, dh2, act, dpre, grad, mid_s,
    r0, r1a, r1b, r2, r3, rs_send, rs_recv,
    ag_send, ag_recv, ag_local, in_sem, mid_sem, out_sem,
):
    images, seq, sp, chunks, early, summed = dims
    rows = images * seq
    padded = h2.shape[0]
    block = rows // 7
    at = Place()
    og_copy = pltpu.make_async_copy(og_hbm, dm.at[pl.ds(0, rows)], in_sem.at[0])
    own_copy = pltpu.make_async_copy(own_hbm, own, in_sem.at[1])
    w_copies = [pltpu.make_async_copy(wff_hbm.at[f], wff.at[f], in_sem.at[2 + f]) for f in range(early)]
    own_copy.start()
    og_copy.start()

    def mid_copy(i):
        r = pl.ds(pl.multiple_of(i * block, 16), block)
        return pltpu.make_async_copy(mid_hbm.at[:, r], mid_s.at[lax.rem(i, 4)], mid_sem.at[lax.rem(i, 4)])

    mid_copy(0).start()
    mid_copy(1).start()
    start_all(w_copies)
    late = chunks - early
    gather = {
        early + k: gather_both(
            at, wff.at[early + k], own.at[k], (ag_send.at[k], ag_recv.at[k], ag_local.at[k])
        )
        for k in range(late)
    }
    scratch = (r0, r1a, r1b, r2, r3, rs_send, rs_recv)
    scatter = [
        scatter_both(
            at, k, (grad.at[k % 2, 0], grad.at[k % 2, 1]), scratch, (gff_ref.at[k, 0], gff_ref.at[k, 1])
        )
        for k in range(summed)
    ]
    at.barrier()
    own_copy.wait()
    for k in range(late):
        gather[early + k][0]()
    og_copy.wait()
    count = counts_ref[0]

    first = at.x * images
    image = lax.rem(lax.broadcasted_iota(jnp.int32, (block, 1), 0), images) + first
    live = jnp.where(image < count, 1.0, 0.0).astype(F32)

    def second_norm(i, _):
        pl.when(i + 2 < 7)(lambda: mid_copy(i + 2).start())
        mid_copy(i).wait()
        r = pl.ds(pl.multiple_of(i * block, 16), block)
        xhat, _r = normed(load_columns(mid_s.at[lax.rem(i, 4)], slice(None)))
        h2[r, :] = (xhat * norm_ref[2:3, :] + norm_ref[3:4, :]).astype(BF16)
        dm[r, :] = (dm[r, :].astype(F32) * live).astype(BF16)
        mlp[r, :] = jnp.zeros((block, mlp.shape[1]), F32)
        dh2[r, :] = jnp.zeros((block, mlp.shape[1]), F32)
        return 0

    rest = pl.ds(rows, padded - rows)
    for ref in (h2, dm, act, dpre):
        ref[rest, :] = jnp.zeros((padded - rows, ref.shape[1]), BF16)
    lax.fori_loop(0, 7, second_norm, 0)

    def turn(j, _):
        r = pl.ds(pl.multiple_of(j * 128, 128), 128)
        h2t[:, r] = h2[r, :].T
        dmt[:, r] = dm[r, :].T
        return 0

    lax.fori_loop(0, padded // 128, turn, 0)
    wait_all(w_copies)

    entries = []
    for k, slots in enumerate(
        ((None, 0, 2, 6, 8), (None, 2, 6, 10, 12), (None, 4, 7, 12, 16), (None, 6, 10, 14, 20))
    ):
        entries += [(n, gather[early + k][j]) for j, n in enumerate(slots) if n is not None]
    for k, slots in enumerate(((8, 10, 16, 18, 21), (12, 14, 17, 19, 23), (16, 18, 21, 23, 24))):
        entries += [(n, scatter[k][j]) for j, n in enumerate(slots)]
    entries.sort(key=lambda e: e[0])
    plan = planned([(slot % 4, (slot // 4,), step) for slot, step in entries if slot < 4 * chunks])
    tail = [step for slot, step in entries if slot >= 4 * chunks]

    def late_copy(k):
        return pltpu.make_async_copy(grad.at[k % 2], late_hbm.at[k - summed], out_sem.at[k - summed])

    def chunk(f, _):
        b1 = bias_ref[f]
        for i in range(2):
            run_slot(plan, i, (f,))
            r = pl.ds(i * (rows // 2), rows // 2)
            w1, w2 = matrix(wff.at[f, 0]), matrix(wff.at[f, 1])
            pre = dot(h2[r, :], w1, 1, 0) + b1
            phi = 0.5 + 0.5 * lax.erf(pre * 0.7071067811865476)
            a = (pre * phi).astype(BF16)
            slope = phi + pre * (jnp.exp(-0.5 * pre * pre) * 0.3989422804014327)
            d = (dot(dm[r, :], w2, 1, 0) * slope).astype(BF16)
            act[r, :] = a
            dpre[r, :] = d
            mlp[r, :] += dot(a, w2, 1, 1)
            dh2[r, :] += dot(d, w1, 1, 1)
        slot = lax.rem(f, 2)
        shape = grad.shape[2:]
        run_slot(plan, 2, (f,))
        for k in range(summed, chunks - 2):
            pl.when(f == k + 2)(late_copy(k).wait)
        b1g_ref[f] = jnp.sum(dpre[...].astype(F32), axis=0, keepdims=True)
        grad[slot, 0] = dot(h2t[...], dpre[...], 1, 0).astype(BF16).reshape(shape)
        run_slot(plan, 3, (f,))
        grad[slot, 1] = dot(dmt[...], act[...], 1, 0).astype(BF16).reshape(shape)

        for k in range(summed, chunks):
            pl.when(f == k)(late_copy(k).start)
        return 0

    mid_copy(0).start()
    mid_copy(1).start()
    lax.fori_loop(0, chunks, chunk, 0)

    def dmid_copy(i):
        r = pl.ds(pl.multiple_of(i * block, 16), block)
        return pltpu.make_async_copy(mid_s.at[lax.rem(i, 4)], dmid_hbm.at[:, r], out_sem.at[16 + lax.rem(i, 4)])

    def second_norm_back(i, acc):
        pl.when(i >= 2)(lambda: dmid_copy(i - 2).wait())
        pl.when(i + 2 < 7)(lambda: mid_copy(i + 2).start())
        mid_copy(i).wait()
        r = pl.ds(pl.multiple_of(i * block, 16), block)
        mid = load_columns(mid_s.at[lax.rem(i, 4)], slice(None))
        xhat, rstd = normed(mid)
        h2[r, :] = (mid + mlp[r, :] + bout_ref[1:2, :]).astype(BF16)
        e = dh2[r, :]
        live = dm[r, :].astype(F32)
        d = live + norm_back(e, norm_ref[2:3, :], xhat, rstd)
        store_columns(mid_s.at[lax.rem(i, 4)], slice(None), d)
        pltpu.make_async_copy(h2.at[r], bo_hbm.at[r], out_sem.at[8 + i]).start()
        dmid_copy(i).start()
        terms = (e * xhat, e, d, live)
        return tuple(a + jnp.sum(t, axis=0, keepdims=True) for a, t in zip(acc, terms))

    zero = jnp.zeros((1, mlp.shape[1]), F32)
    acc = lax.fori_loop(0, 7, second_norm_back, (zero,) * 4)
    sums_ref[...] = jnp.zeros(sums_ref.shape, F32)
    for k in range(4):
        sums_ref[k : k + 1, :] = acc[k]
    for step in tail:
        step()

    for i in range(7):
        r = pl.ds(i * block, block)
        pltpu.make_async_copy(h2.at[r], bo_hbm.at[r], out_sem.at[8 + i]).wait()
    dmid_copy(5).wait()
    dmid_copy(6).wait()
    for k in range(chunks - 2, chunks):
        late_copy(k).wait()


def attention_back_kernel(
    dims,
    norm_ref, sums_ref, b1g_ref, x_hbm, dmid_hbm, late_hbm, watt_hbm, qkv_hbm, ctx_hbm, p_hbm,
    gt_hbm, glate_ref, gatt_ref, small_ref,
    dattn, h1t, dh1, dqkv, watt, qkv_s, dc_s, ctx_s, ctxt, p_s, grad, x_s, dmid_s, gt_s, bias_s,
    small, small_line,
    r0, r1a, r1b, r2, r3, rs_send, rs_recv, sm_send, sm_recv,
    in_sem, ctx_sem, tile_sem, dmid_sem, gt_sem,
):
    images, seq, sp, groups, chunks, held = dims
    rows = images * seq
    block = rows // 7
    model = x_s.shape[1]
    quad = 4
    tr = quad * sp
    tiles = images // quad
    at = Place()
    dmid_in = pltpu.make_async_copy(dmid_hbm, dh1, in_sem.at[0])
    watt_copy = pltpu.make_async_copy(watt_hbm, watt, in_sem.at[1])
    x_copy = pltpu.make_async_copy(x_hbm, x_s, in_sem.at[2])
    late_copies = [pltpu.make_async_copy(late_hbm.at[k], grad.at[k], in_sem.at[3 + k]) for k in range(held)]

    def dmid_copy(i):
        r = pl.ds(pl.multiple_of(i * block, 16), block)
        return pltpu.make_async_copy(dmid_hbm.at[:, r], dmid_s.at[lax.rem(i, 3)], dmid_sem.at[lax.rem(i, 3)])

    def ctx_copy(g):
        return pltpu.make_async_copy(ctx_hbm.at[g], ctx_s, ctx_sem.at[0])

    def tile_copies(g, i):
        r, im = pl.ds(pl.multiple_of(i * tr, 16), tr), pl.ds(i * quad, quad)
        return [
            pltpu.make_async_copy(qkv_hbm.at[g, r], qkv_s.at[r], tile_sem.at[0, i]),
            pltpu.make_async_copy(p_hbm.at[g, im], p_s.at[im], tile_sem.at[1, i]),
        ]

    late_copies[0].start()
    dmid_in.start()
    x_copy.start()
    watt_copy.start()
    start_all(late_copies[1:])
    ctx_copy(0).start()
    for i in range(tiles):
        start_all(tile_copies(0, i))
    scratch = (r0, r1a, r1b, r2, r3, rs_send, rs_recv)
    scatter = [
        scatter_both(at, k, (grad.at[k, 0], grad.at[k, 1]), scratch, (glate_ref.at[k, 0], glate_ref.at[k, 1]))
        for k in range(held)
    ]
    for g in range(groups):
        scatter.append(
            scatter_both(
                at, held + g, (grad.at[g % held, 0], grad.at[g % held, 1]), scratch, (gatt_ref.at[g, 0], gatt_ref.at[g, 1])
            )
        )
    own_quad, own_line = small.at[at.quad], small_line.at[at.line]
    sm_quad = [remote(own_quad, own_quad, sm_send.at[k], sm_recv.at[k], d) for k, d in enumerate(at.quad_peers)]
    sm_line = [
        remote(own_line, own_line, sm_send.at[3 + k], sm_recv.at[3 + k], d) for k, d in enumerate(at.line_peers)
    ]
    at.barrier(at.quad_peers + at.line_peers)
    for k in range(held):
        late_copies[k].wait()
        scatter[k][0]()

    dmid_in.wait()

    def take_dattn(i, _):
        d = pad_rows(load_columns(dh1, pl.ds(i, seq, stride=images)), sp)
        dattn[pl.ds(pl.multiple_of(i * sp, 16), sp), :] = d.astype(BF16)
        return 0

    lax.fori_loop(0, images, take_dattn, 0)
    x_copy.wait()

    def first_norm(j, _):
        r = pl.ds(pl.multiple_of(j * block, 16), block)
        xhat, _r = normed(x_s[r, :].astype(F32))
        store_columns(dh1, r, xhat * norm_ref[0:1, :] + norm_ref[1:2, :])
        return 0

    lax.fori_loop(0, 7, first_norm, 0)

    def by_image(i, _):
        h = pad_rows(load_columns(dh1, pl.ds(i, seq, stride=images)), sp)
        dqkv[0, pl.ds(pl.multiple_of(i * sp, 16), sp), :] = h.astype(BF16)
        return 0

    lax.fori_loop(0, images, by_image, 0)

    scatter[0][1]()

    def turn(j, _):
        r = pl.ds(pl.multiple_of(j * 128, 128), 128)
        h1t[:, r] = dqkv[0, r, :].T
        return 0

    lax.fori_loop(0, images * sp // 128, turn, 0)
    watt_copy.wait()

    entries = []
    for k, slots in enumerate(((2, 8, 12), (2, 6, 10, 14), (5, 9, 12, 16))):
        entries += [(n, scatter[k][5 - len(slots) + j]) for j, n in enumerate(slots)]
    for g, slots in enumerate(((12, 15, 18, 21, 27), (14, 16, 20, 22, 30), (18, 20, 26, 30, 31))):
        entries += [(n, scatter[held + g][j]) for j, n in enumerate(slots)]
    entries.sort(key=lambda e: e[0])

    def spot(n):
        return (n % 2, (n // 6, n % 6 // 2)) if n % 6 < 4 else (n % 6, (n // 6,))

    tail_at = 6 * groups
    plan = planned(
        [spot(n) + (step,) for n, step in entries if n < tail_at]
        + [("through", (n - tail_at,), step) for n, step in entries if tail_at <= n < tail_at + 4]
        + [("norm", (n - tail_at - 4,), step) for n, step in entries if tail_at + 4 <= n < tail_at + 11]
    )
    tail = [[step for n, step in entries if n == at_end] for at_end in (tail_at + 12, tail_at + 13)]

    left = left_half(sp)
    scale = HEAD_DIM ** (-0.5)

    units = [(a, t) for a in range(quad) for t in range(NTP)]

    def group(g, _):
        keep = lax.rem(g, grad.shape[0])
        ctx_copy(g).wait()
        ctxt[...] = ctx_s[...].T
        pl.when(g + 1 < groups)(lambda: ctx_copy(g + 1).start())

        def tile(i, acc):
            wait_all(tile_copies(g, i))
            run_slot(plan, 0, (g, i))
            r = pl.ds(pl.multiple_of(i * tr, 16), tr)
            dc_s[...] = dot(dattn[r, :], out_columns(matrix(watt.at[g, 1])), 1, 0).astype(BF16)
            run_slot(plan, 1, (g, i))
            qkv, dc = qkv_s[r, :], dc_s[...]

            def cut(a, first):
                return qkv[a * sp : (a + 1) * sp, first : first + 128]

            def wide(v):
                return pad_rows(v, LANES)

            def grads_in(a, t):
                return wide(dc[a * sp : (a + 1) * sp, t * 128 : (t + 1) * 128])

            dps = [dot(split_heads(cut(a, 2 * HALF + t * 128), left), grads_in(a, t), 1, 1) for a, t in units]
            dss = []
            for (a, t), dp in zip(units, dps):
                ds = []
                for h in range(2):
                    p = p_s[i * quad + a, t, h].astype(F32)
                    pd = p * dp[h * sp : (h + 1) * sp]
                    ds.append((pd - p * jnp.sum(pd, axis=0, keepdims=True)).astype(BF16))
                dss.append(ds)
            parts = []
            for (a, t), ds in zip(units, dss):
                q = wide(cut(a, t * HALF) * jnp.asarray(scale, BF16))
                kt = cut(a, t * HALF + 128).T
                dqt = [dot(kt[h * HEAD_DIM : (h + 1) * HEAD_DIM], ds[h], 1, 0) for h in range(2)]
                dk = dot(jnp.concatenate(ds, axis=0), q, 1, 0)
                ps = jnp.concatenate([p_s[i * quad + a, t, h] for h in range(2)], axis=0)
                dv = dot(ps, grads_in(a, t), 1, 0)
                parts.append((
                    jnp.concatenate(dqt, axis=0).T[:sp] * scale,
                    jnp.where(left, dk[:sp], dk[sp:]),
                    jnp.where(left, dv[:sp], dv[sp:]),
                ))
            for a in range(quad):
                (q0, k0, v0), (q1, k1, v1) = parts[NTP * a], parts[NTP * a + 1]
                d = jnp.concatenate([q0, k0, q1, k1, v0, v1], axis=1).astype(BF16)
                dqkv[g, pl.ds(pl.multiple_of(i * tr + a * sp, 16), sp), :] = d
                acc = acc + jnp.sum(d.astype(F32), axis=0, keepdims=True)
            pl.when(g + 1 < groups)(lambda: start_all(tile_copies(g + 1, i)))
            return acc

        bias_s[g] = lax.fori_loop(0, tiles, tile, jnp.zeros((1, model), F32))
        run_slot(plan, 4, (g,))
        shape = grad.shape[2:]
        gw = dot(h1t[...], dqkv[g], 1, 0).astype(BF16)
        grad[keep, 0] = gw[:, : 2 * HALF].reshape(shape)
        run_slot(plan, 5, (g,))
        go = dot(ctxt[...], dattn[...], 1, 0).T.astype(BF16)
        grad[keep, 1] = jnp.concatenate(
            [gw[:, 2 * HALF : 2 * HALF + 128], go[:, :128], gw[:, 2 * HALF + 128 :], go[:, 128:]], axis=1
        ).reshape(shape)
        return 0

    dmid_copy(0).start()
    dmid_copy(1).start()
    lax.fori_loop(0, groups, group, 0)
    small_tr = 2 * sp

    def through(i, _):
        run_slot(plan, "through", (i,))
        r = pl.ds(pl.multiple_of(i * small_tr, 16), small_tr)
        d = jnp.concatenate([dqkv[g, r, :] for g in range(groups)], axis=1)
        w = jnp.concatenate(
            [projection(matrix(watt.at[g, 0]), matrix(watt.at[g, 1])) for g in range(groups)], axis=1
        )
        back = dot(d, w, 1, 1)
        for a in range(2):
            store_columns(dh1, pl.ds(i * 2 + a, seq, stride=images), back[a * sp : a * sp + seq])
        return 0

    lax.fori_loop(0, images // 2, through, 0)

    def gt_copy(i):
        r = pl.ds(pl.multiple_of(i * block, 16), block)
        return pltpu.make_async_copy(gt_s.at[lax.rem(i, 2)], gt_hbm.at[r], gt_sem.at[lax.rem(i, 2)])

    def first_norm_back(i, acc):
        run_slot(plan, "norm", (i,))
        pl.when(i >= 2)(lambda: gt_copy(i - 2).wait())
        pl.when(i + 2 < 7)(lambda: dmid_copy(i + 2).start())
        dmid_copy(i).wait()
        r = pl.ds(pl.multiple_of(i * block, 16), block)
        xhat, rstd = normed(x_s[r, :].astype(F32))
        e = load_columns(dh1, r)
        d = load_columns(dmid_s.at[lax.rem(i, 3)], slice(None))
        gt_s[lax.rem(i, 2)] = d + norm_back(e, norm_ref[0:1, :], xhat, rstd)
        gt_copy(i).start()
        return (acc[0] + jnp.sum(e * xhat, axis=0, keepdims=True), acc[1] + jnp.sum(e, axis=0, keepdims=True))

    zero = jnp.zeros((1, model), F32)
    acc = lax.fori_loop(0, 7, first_norm_back, (zero, zero))
    own_quad[...] = jnp.zeros(own_quad.shape, F32)
    own_quad[0:1, :] = acc[0]
    own_quad[1:2, :] = acc[1]
    own_quad[2:6, :] = sums_ref[0:4, :]
    own_cols = groups * 128
    for g in range(groups):
        for t in range(NTP):
            cols = slice(t * own_cols + 128 * g, t * own_cols + 128 * g + 128)
            own_quad[6:7, cols] = bias_s[g, :, t * HALF : t * HALF + 128]
            own_quad[7:8, cols] = bias_s[g, :, 2 * HALF + t * 128 : 2 * HALF + t * 128 + 128]
    for f in range(chunks):
        for t in range(NTP):
            first = t * chunks * HALF + f * HALF
            row, col = 8 + first // model, first % model
            own_quad[row : row + 1, col : col + HALF] = b1g_ref[f, :, t * HALF : t * HALF + HALF]
    start_all(sm_quad)
    for step in tail[0]:
        step()
    wait_all(sm_quad)
    own_line[...] = (small[0] + small[1]) + (small[2] + small[3])
    start_all(sm_line)
    for step in tail[1]:
        step()
    gt_copy(5).wait()
    gt_copy(6).wait()
    wait_all(sm_line)
    total = small_line[0]
    for k in range(1, NZ * NY):
        total = total + small_line[k]
    small_ref[...] = total


def step_kernel(dims, *refs):
    groups, chunks, held = dims
    names = ("norm", "qkv", "bqv", "out", "fc1", "bfc1", "fc2", "bout")
    bo_hbm, gt_hbm, gff_ref, glate_ref, gatt_ref, small_ref = refs[:6]
    n = len(names)
    ps, ms, vs = (dict(zip(names, refs[6 + k * n : 6 + (k + 1) * n])) for k in range(3))
    outs = refs[6 + 3 * n :]
    bo_out, gt_out = outs[:2]
    g_out, u_out, m_out, v_out = (dict(zip(names, outs[2 + k * n : 2 + (k + 1) * n])) for k in range(4))
    bo_s, gt_s, sem = outs[2 + 4 * n :]
    pieces = 7
    block = bo_s.shape[0] // pieces
    moves = []
    for j in range(pieces):
        r = pl.ds(j * block, block)
        for k, (src, mid, dst) in enumerate(((gt_hbm, gt_s, gt_out), (bo_hbm, bo_s, bo_out))):
            moves.append((
                pltpu.make_async_copy(src.at[r], mid.at[r], sem.at[0, k, j]),
                pltpu.make_async_copy(mid.at[r], dst.at[r], sem.at[1, k, j]),
            ))
    for first, _second in moves:
        first.start()
    for first, second in moves:
        first.wait()
        second.start()
    late = chunks - held

    def ff(f, h):
        return gff_ref[f, h] if f < late else glate_ref[f - late, h]

    whole = {"qkv": True, "fc1": True, "fc2": True}
    decays = ("qkv", "out", "fc1", "fc2")

    def update(name, index, g):
        p = ps[name][index]
        u, m, v = adamw(p, g, ms[name][index], vs[name][index], decay_rate if name in decays else 0.0)
        g_out[name][index] = g
        u_out[name][index] = p + u if name in whole else u
        m_out[name][index] = m
        v_out[name][index] = v

    for c in range(3):
        gs = [gatt_ref[g, c // 2][:, (c % 2) * 128 : (c % 2) * 128 + 128] for g in range(groups)]
        update("qkv", c, jnp.concatenate(gs, axis=1))
    update("out", ..., jnp.concatenate([gatt_ref[g, 1][:, 128:] for g in range(groups)], axis=1))
    for f in range(chunks):
        cols = slice(f * HALF, (f + 1) * HALF)
        update("fc1", (slice(None), cols), ff(f, 0))
        update("fc2", (slice(None), cols), ff(f, 1))
    update("norm", ..., small_ref[0:4, :])
    update("bout", ..., small_ref[4:6, :])
    part = lax.axis_index("tp") * (NZ * NY * NCORE) + lax.axis_index("fsdp")
    width = ps["bqv"].shape[1]
    model = small_ref.shape[1]
    update("bqv", ..., pltpu.roll(small_ref[0:8, :], lax.rem(model - part * width, model), 1)[6:8, :width])
    width = ps["bfc1"].shape[1]
    per = model // width
    turned = pltpu.roll(small_ref[8:16, :], lax.rem(model - lax.rem(part, per) * width, model), 1)[:, :width]
    at_row = lax.broadcasted_iota(jnp.int32, turned.shape, 0)
    update("bfc1", ..., jnp.sum(jnp.where(at_row == part // per, turned, 0.0), axis=0, keepdims=True))
    for _first, second in moves:
        second.wait()


def sds(shape, dtype):
    return jax.ShapeDtypeStruct(shape, dtype)


def fused_device(
    tokens_in, out_grad, image_counts,
    norm_params, w_qkv, bias_qv, w_out, w_fc1, bias_fc1, w_fc2, bias_out,
    *moments,
):
    images, seq, model = tokens_in.shape
    sp = -(-seq // 16) * 16
    rows = images * sp
    own_rows, own_cols = w_qkv.shape[1], w_qkv.shape[2]
    groups = own_cols // 128
    chunks = w_fc1.shape[1] // HALF
    early, summed = 2, chunks - 3
    held = chunks - summed
    wide = NTP * HALF
    cube = (NZ, NY, NCORE, own_rows, wide)
    any_, vm, sm = pl.BlockSpec(memory_space=pl.ANY), pl.BlockSpec(memory_space=pltpu.VMEM), pl.BlockSpec(memory_space=pltpu.SMEM)
    dma = pltpu.SemaphoreType.DMA

    def params(k):
        return pltpu.CompilerParams(collective_id=k, has_side_effects=True, vmem_limit_bytes=VMEM_BYTES)

    n_ag = groups + early + 2
    flat_rows = images * seq

    def by_token(a):
        return a.transpose(1, 0, 2).reshape(flat_rows, model)

    def by_image(a):
        return a.reshape(seq, images, model).transpose(1, 0, 2)

    x_rows, og_rows = by_token(tokens_in), by_token(out_grad)
    qkv, ctx, mid, p, watt, wff, own, bias1 = pl.pallas_call(
        functools.partial(attention_kernel, (images, seq, sp, groups, groups + chunks, early)),
        name="attention",
        in_specs=[any_] + [vm] * 8,
        out_specs=[any_] * 7 + [vm],
        out_shape=[
            sds((groups, rows, model), BF16), sds((groups, rows, HALF), BF16), sds((model // 128, flat_rows, 128), F32),
            sds((groups, images, NTP, 2, sp, LANES), BF16), sds((groups, 2) + cube, BF16), sds((early, 2) + cube, BF16),
            sds((chunks - early, 2, own_rows, HALF), BF16), sds((chunks, 1, wide), F32),
        ],
        scratch_shapes=[
            pltpu.VMEM((flat_rows, model), BF16), pltpu.VMEM((rows, model), BF16),
            pltpu.VMEM((groups, rows, model), BF16), pltpu.VMEM((groups, rows, HALF), BF16),
            pltpu.VMEM((model // 128, flat_rows, 128), F32), pltpu.VMEM((groups, images, NTP, 2, sp, LANES), BF16),
            pltpu.VMEM((groups, 2) + cube, BF16), pltpu.VMEM((groups + chunks, 2, own_rows, HALF), BF16),
            pltpu.VMEM((NTP, NZ, NY, NCORE, 8, 128), F32), pltpu.VMEM((groups, 1, model), F32),
            dma((n_ag, 2, AG_SEMS)), dma((n_ag, 2, AG_SEMS)), dma((n_ag, 2)), dma((6,)), dma((6,)),
            dma((4, groups, 8)), dma((2 + groups,)),
        ],
        compiler_params=params(0),
    )(x_rows, norm_params, bias_out, w_qkv, w_out.T, w_fc1, w_fc2.T, bias_qv, bias_fc1.reshape(1, -1))

    late = chunks - early
    bo, dmid, grad_late, sums, b1g, gff = pl.pallas_call(
        functools.partial(feed_forward_kernel, (images, seq, sp, chunks, early, summed)),
        name="feed_forward",
        in_specs=[sm, vm, vm, vm] + [any_] * 4,
        out_specs=[any_] * 3 + [vm] * 3,
        out_shape=[
            sds((flat_rows, model), BF16), sds((model // 128, flat_rows, 128), F32),
            sds((held, 2) + cube, BF16), sds((8, model), F32), sds((chunks, 1, wide), F32),
            sds((summed, 2, own_rows, HALF), F32),
        ],
        scratch_shapes=[
            pltpu.VMEM((chunks, 2) + cube, BF16), pltpu.VMEM((late, 2, own_rows, HALF), BF16),
            pltpu.VMEM((rows, model), BF16), pltpu.VMEM((model, rows), BF16),
            pltpu.VMEM((rows, model), BF16), pltpu.VMEM((model, rows), BF16),
            pltpu.VMEM((flat_rows, model), F32), pltpu.VMEM((flat_rows, model), F32),
            pltpu.VMEM((rows, wide), BF16), pltpu.VMEM((rows, wide), BF16),
            pltpu.VMEM((2, 2) + cube, BF16), pltpu.VMEM((4, model // 128, flat_rows // 7, 128), F32),
        ]
        + scatter_scratch(summed, own_rows)
        + [
            dma((late, 2, AG_SEMS)), dma((late, 2, AG_SEMS)), dma((late, 2)), dma((2 + early,)), dma((4,)),
            dma((24,)),
        ],
        compiler_params=params(1),
    )(image_counts, norm_params, bias_out, bias1, mid, og_rows, wff, own)

    gt, glate, gatt, small = pl.pallas_call(
        functools.partial(attention_back_kernel, (images, seq, sp, groups, chunks, held)),
        name="attention_back",
        in_specs=[vm] * 3 + [any_] * 7,
        out_specs=[any_] + [vm] * 3,
        out_shape=[
            sds((flat_rows, model), F32), sds((held, 2, own_rows, HALF), F32),
            sds((groups, 2, own_rows, HALF), F32), sds((16, model), F32),
        ],
        scratch_shapes=[
            pltpu.VMEM((rows, model), BF16), pltpu.VMEM((model, rows), BF16),
            pltpu.VMEM((model // 128, flat_rows, 128), F32), pltpu.VMEM((groups, rows, model), BF16),
            pltpu.VMEM((groups, 2) + cube, BF16),
            pltpu.VMEM((rows, model), BF16), pltpu.VMEM((4 * sp, HALF), BF16),
            pltpu.VMEM((rows, HALF), BF16), pltpu.VMEM((HALF, rows), BF16),
            pltpu.VMEM((images, NTP, 2, sp, LANES), BF16), pltpu.VMEM((held, 2) + cube, BF16),
            pltpu.VMEM((flat_rows, model), BF16), pltpu.VMEM((3, model // 128, flat_rows // 7, 128), F32),
            pltpu.VMEM((2, flat_rows // 7, model), F32), pltpu.VMEM((groups, 1, model), F32),
            pltpu.VMEM((4, 16, model), F32), pltpu.VMEM((NZ * NY, 16, model), F32),
        ]
        + scatter_scratch(held + groups, own_rows)
        + [dma((10,)), dma((10,)), dma((3 + held,)), dma((1,)), dma((2, 2)), dma((3,)), dma((2,))],
        compiler_params=params(2),
    )(norm_params, sums, b1g, x_rows, dmid, grad_late, watt, qkv, ctx, p)

    turned = (3, 6)

    def flat(a, k):
        return a.reshape(1, -1) if a.ndim == 1 else a.T if k in turned else a

    weights = [flat(a, k) for k, a in enumerate((norm_params, w_qkv, bias_qv, w_out, w_fc1, bias_fc1, w_fc2, bias_out))]
    moments = [flat(a, k % 8) for k, a in enumerate(moments)]
    shapes = [sds(a.shape, F32) for a in weights]
    outs = pl.pallas_call(
        functools.partial(step_kernel, (groups, chunks, held)),
        name="adamw_step",
        in_specs=[any_] * 2 + [vm] * 28,
        out_specs=[any_] * 2 + [vm] * 32,
        out_shape=[sds(bo.shape, BF16), sds(gt.shape, F32)] + shapes * 4,
        scratch_shapes=[pltpu.VMEM(bo.shape, BF16), pltpu.VMEM(gt.shape, F32), dma((2, 2, 7))],
        compiler_params=pltpu.CompilerParams(vmem_limit_bytes=VMEM_BYTES),
    )(bo, gt, gff, glate, gatt, small, *weights, *moments)
    bo, gt, *outs = outs
    outs = [o.reshape(-1) if k % 8 == 5 else o.T if k % 8 in turned else o for k, o in enumerate(outs)]
    return (by_image(bo), by_image(gt)) + tuple(outs)


def solution(mesh):
    placed = (
        P(("fsdp", "tp"), None, None),
        P(("fsdp", "tp"), None, None),
        P("fsdp"),
        P(),
        P(None, "fsdp", "tp"),
        P(None, ("tp", "fsdp")),
        P("tp", "fsdp"),
        P("fsdp", "tp"),
        P(("tp", "fsdp")),
        P("tp", "fsdp"),
        P(),
        P(),
        P(None, "fsdp", "tp"),
        P(None, ("tp", "fsdp")),
        P("tp", "fsdp"),
        P("fsdp", "tp"),
        P(("tp", "fsdp")),
        P("tp", "fsdp"),
        P(),
        P(),
        P(None, "fsdp", "tp"),
        P(None, ("tp", "fsdp")),
        P("tp", "fsdp"),
        P("fsdp", "tp"),
        P(("tp", "fsdp")),
        P("tp", "fsdp"),
        P(),
    )
    fits = mesh.shape["fsdp"] == NZ * NY * NCORE and mesh.shape["tp"] == NTP
    return jax.shard_map(
        fused_device if fits else per_device,
        mesh=mesh,
        in_specs=placed,
        out_specs=(
            P(("fsdp", "tp"), None, None),
            P(("fsdp", "tp"), None, None),
            P(),
            P(None, "fsdp", "tp"),
            P(None, ("tp", "fsdp")),
            P("tp", "fsdp"),
            P("fsdp", "tp"),
            P(("tp", "fsdp")),
            P("tp", "fsdp"),
            P(),
            P(),
            P(None, "fsdp", "tp"),
            P(None, ("tp", "fsdp")),
            P("tp", "fsdp"),
            P("fsdp", "tp"),
            P(("tp", "fsdp")),
            P("tp", "fsdp"),
            P(),
            P(),
            P(None, "fsdp", "tp"),
            P(None, ("tp", "fsdp")),
            P("tp", "fsdp"),
            P("fsdp", "tp"),
            P(("tp", "fsdp")),
            P("tp", "fsdp"),
            P(),
            P(),
            P(None, "fsdp", "tp"),
            P(None, ("tp", "fsdp")),
            P("tp", "fsdp"),
            P("fsdp", "tp"),
            P(("tp", "fsdp")),
            P("tp", "fsdp"),
            P(),
        ),
        check_vma=False,
    )
```

```python
import functools

import jax
import jax.numpy as jnp
from jax import lax
from jax.experimental import pallas as pl
from jax.experimental.pallas import tpu as pltpu
from jax.sharding import PartitionSpec as P

HEAD_DIM = 64
ADAM_STEP = 10


norm_eps = 1e-06
learn_rate = 0.02
beta_one = 0.9
beta_two = 0.999
adam_eps = 1e-08
decay_rate = 0.05


def layer_norm(rows_in, gain_vec, shift_vec):
    centre = rows_in - jnp.mean(rows_in, axis=-1, keepdims=True)
    spread = jnp.mean(centre * centre, axis=-1, keepdims=True)
    return centre * lax.rsqrt(spread + norm_eps) * gain_vec + shift_vec


def exact_gelu(rows_in):
    return jax.nn.gelu(rows_in, approximate=False)


def adamw(parameter, gradient, moment_one, moment_two, decay_on):
    one_new = beta_one * moment_one + (1.0 - beta_one) * gradient
    two_new = beta_two * moment_two + (1.0 - beta_two) * gradient * gradient
    one_hat = one_new / (1.0 - beta_one**ADAM_STEP)
    two_hat = two_new / (1.0 - beta_two**ADAM_STEP)
    update = one_hat / (jnp.sqrt(two_hat) + adam_eps) + decay_on * parameter
    return (-learn_rate * update, one_new, two_new)


def per_device(
    tokens_in,
    out_grad,
    image_counts,
    norm_params,
    w_qkv,
    bias_qv,
    w_out,
    w_fc1,
    bias_fc1,
    w_fc2,
    bias_out,
    first_norm,
    first_qkv,
    first_bias_qv,
    first_out,
    first_fc1,
    first_bias_fc1,
    first_fc2,
    first_bias_out,
    second_norm,
    second_qkv,
    second_bias_qv,
    second_out,
    second_fc1,
    second_bias_fc1,
    second_fc2,
    second_bias_out,
):
    images = tokens_in.shape[0]
    seq_len = tokens_in.shape[1]
    score_scale = HEAD_DIM ** (-0.5)
    inputs = tokens_in.astype(jnp.float32)
    slot_ids = lax.axis_index("tp") * images + jnp.arange(images)
    live_mask = (slot_ids < image_counts[0]).astype(jnp.float32)
    live_grad = out_grad.astype(jnp.float32) * live_mask[:, None, None]
    qkv_all, bqv_all, wout_all = (
        lax.all_gather(w_qkv.astype(jnp.bfloat16), "fsdp", axis=1, tiled=True),
        lax.all_gather(bias_qv.astype(jnp.bfloat16), "fsdp", axis=1, tiled=True),
        lax.all_gather(w_out.astype(jnp.bfloat16), "fsdp", axis=1, tiled=True),
    )
    fc1_all, bfc1_all, fc2_all = (
        lax.all_gather(w_fc1.astype(jnp.bfloat16), "fsdp", axis=0, tiled=True),
        lax.all_gather(bias_fc1.astype(jnp.bfloat16), "fsdp", axis=0, tiled=True),
        lax.all_gather(w_fc2.astype(jnp.bfloat16), "fsdp", axis=1, tiled=True),
    )
    hidden_one = layer_norm(inputs, norm_params[0], norm_params[1]).astype(jnp.bfloat16)
    qkv_use, bqv_use, wout_use = (
        lax.all_gather(qkv_all, "tp", axis=2, tiled=True),
        lax.all_gather(bqv_all, "tp", axis=1, tiled=True),
        lax.all_gather(wout_all, "tp", axis=0, tiled=True),
    )
    group_images = hidden_one.shape[0]
    projected = jnp.einsum("gsd,cdf->cgsf", hidden_one, qkv_use, preferred_element_type=jnp.float32)
    width_local = projected.shape[3]
    shape_heads = (group_images, seq_len, width_local // HEAD_DIM, HEAD_DIM)
    queries = (projected[0] + bqv_use[0]).astype(jnp.bfloat16).reshape(shape_heads)
    key_vecs = projected[1].astype(jnp.bfloat16).reshape(shape_heads)
    value_vecs = (projected[2] + bqv_use[1]).astype(jnp.bfloat16).reshape(shape_heads)
    scores = (
        jnp.einsum("gqhe,gkhe->ghqk", queries, key_vecs, preferred_element_type=jnp.float32)
        * score_scale
    )
    log_total = jax.nn.logsumexp(scores, axis=-1, keepdims=True)
    probs_low = jnp.exp(scores - log_total).astype(jnp.bfloat16)
    context = jnp.einsum(
        "ghqk,gkhe->gqhe", probs_low, value_vecs, preferred_element_type=jnp.float32
    )
    context = context.astype(jnp.bfloat16).reshape(group_images, seq_len, width_local)
    attn_part = jnp.einsum("gsf,fd->gsd", context, wout_use, preferred_element_type=jnp.float32)
    middle = inputs + attn_part + bias_out[0]
    hidden_two = layer_norm(middle, norm_params[2], norm_params[3]).astype(jnp.bfloat16)
    mlp_in = lax.all_gather(hidden_two, "tp", axis=0, tiled=True)
    fc1_use, bfc1_use, fc2_use = (fc1_all, bfc1_all, fc2_all)
    pre_act = (
        jnp.einsum("gsd,df->gsf", mlp_in, fc1_use, preferred_element_type=jnp.float32) + bfc1_use
    )
    activated = exact_gelu(pre_act).astype(jnp.bfloat16)
    mlp_part = jnp.einsum("gsf,fd->gsd", activated, fc2_use, preferred_element_type=jnp.float32)
    mlp_sum = lax.psum_scatter(
        mlp_part.astype(jnp.bfloat16), "tp", scatter_dimension=0, tiled=True
    ).astype(jnp.float32)
    block_out = (middle + mlp_sum + bias_out[1]).astype(jnp.bfloat16)
    grad_mlp = live_grad.astype(jnp.bfloat16)
    grad_mlp_in = lax.all_gather(grad_mlp, "tp", axis=0, tiled=True)
    grad_w2 = jnp.einsum("gsf,gsd->fd", activated, grad_mlp_in, preferred_element_type=jnp.float32)
    grad_act = jnp.einsum("gsd,fd->gsf", grad_mlp_in, fc2_use, preferred_element_type=jnp.float32)
    gelu_out, gelu_pull = jax.vjp(exact_gelu, pre_act)
    grad_pre = gelu_pull(grad_act)[0].astype(jnp.bfloat16)
    grad_b1 = jnp.sum(grad_pre.astype(jnp.float32), axis=(0, 1))
    grad_w1 = jnp.einsum("gsd,gsf->df", mlp_in, grad_pre, preferred_element_type=jnp.float32)
    grad_h2_part = jnp.einsum("gsf,df->gsd", grad_pre, fc1_use, preferred_element_type=jnp.float32)
    grad_h2 = lax.psum_scatter(
        grad_h2_part.astype(jnp.bfloat16), "tp", scatter_dimension=0, tiled=True
    ).astype(jnp.float32)
    norm_two, norm_two_pull = jax.vjp(layer_norm, middle, norm_params[2], norm_params[3])
    grad_mid_ln, grad_gain_two, grad_shift_two = norm_two_pull(grad_h2)
    grad_middle = live_grad + grad_mid_ln
    grad_attn = grad_middle.astype(jnp.bfloat16)
    grad_wo = jnp.einsum("gsf,gsd->fd", context, grad_attn, preferred_element_type=jnp.float32)
    grad_ctx = jnp.einsum("gsd,fd->gsf", grad_attn, wout_use, preferred_element_type=jnp.float32)
    grad_ctx = grad_ctx.astype(jnp.bfloat16).reshape(shape_heads)
    scores_again = (
        jnp.einsum("gqhe,gkhe->ghqk", queries, key_vecs, preferred_element_type=jnp.float32)
        * score_scale
    )
    probs_again = jnp.exp(scores_again - log_total)
    grad_probs = jnp.einsum(
        "gqhe,gkhe->ghqk", grad_ctx, value_vecs, preferred_element_type=jnp.float32
    )
    row_terms = jnp.sum(probs_again * grad_probs, axis=-1, keepdims=True)
    grad_scores = (probs_again * (grad_probs - row_terms)).astype(jnp.bfloat16)
    grad_query = (
        jnp.einsum("ghqk,gkhe->gqhe", grad_scores, key_vecs, preferred_element_type=jnp.float32)
        * score_scale
    ).astype(jnp.bfloat16)
    grad_keys = (
        jnp.einsum("ghqk,gqhe->gkhe", grad_scores, queries, preferred_element_type=jnp.float32)
        * score_scale
    ).astype(jnp.bfloat16)
    grad_values = jnp.einsum(
        "ghqk,gqhe->gkhe",
        probs_again.astype(jnp.bfloat16),
        grad_ctx,
        preferred_element_type=jnp.float32,
    ).astype(jnp.bfloat16)
    grad_proj = jnp.stack([grad_query, grad_keys, grad_values]).reshape(
        3, group_images, seq_len, width_local
    )
    grad_bqv = jnp.stack(
        [
            jnp.sum(grad_proj[0].astype(jnp.float32), axis=(0, 1)),
            jnp.sum(grad_proj[2].astype(jnp.float32), axis=(0, 1)),
        ]
    )
    grad_wqkv = jnp.einsum(
        "gsd,cgsf->cdf", hidden_one, grad_proj, preferred_element_type=jnp.float32
    )
    grad_h1_part = jnp.einsum(
        "cgsf,cdf->gsd", grad_proj, qkv_use, preferred_element_type=jnp.float32
    )
    grad_wqkv, grad_bqv, grad_wo = (
        lax.psum_scatter(
            grad_wqkv.astype(jnp.bfloat16), "tp", scatter_dimension=2, tiled=True
        ).astype(jnp.float32),
        lax.psum_scatter(
            grad_bqv.astype(jnp.bfloat16), "tp", scatter_dimension=1, tiled=True
        ).astype(jnp.float32),
        lax.psum_scatter(
            grad_wo.astype(jnp.bfloat16), "tp", scatter_dimension=0, tiled=True
        ).astype(jnp.float32),
    )
    norm_one, norm_one_pull = jax.vjp(layer_norm, inputs, norm_params[0], norm_params[1])
    grad_in_ln, grad_gain_one, grad_shift_one = norm_one_pull(grad_h1_part)
    grad_tokens = grad_middle + grad_in_ln
    g_qkv, g_bqv, g_out, g_fc1, g_bfc1, g_fc2 = (
        lax.psum_scatter(grad_wqkv, "fsdp", scatter_dimension=1, tiled=True),
        lax.psum_scatter(grad_bqv, "fsdp", scatter_dimension=1, tiled=True),
        lax.psum_scatter(grad_wo, "fsdp", scatter_dimension=1, tiled=True),
        lax.psum_scatter(grad_w1, "fsdp", scatter_dimension=0, tiled=True),
        lax.psum_scatter(grad_b1, "fsdp", scatter_dimension=0, tiled=True),
        lax.psum_scatter(grad_w2, "fsdp", scatter_dimension=1, tiled=True),
    )
    norm_terms = jnp.stack([grad_gain_one, grad_shift_one, grad_gain_two, grad_shift_two])
    bias_terms = jnp.stack([jnp.sum(grad_middle, axis=(0, 1)), jnp.sum(live_grad, axis=(0, 1))])
    g_norm, g_bout = lax.psum((norm_terms, bias_terms), ("fsdp", "tp"))
    s_norm, a_norm, b_norm = adamw(norm_params, g_norm, first_norm, second_norm, 0.0)
    s_qkv, a_qkv, b_qkv = adamw(w_qkv, g_qkv, first_qkv, second_qkv, decay_rate)
    s_bqv, a_bqv, b_bqv = adamw(bias_qv, g_bqv, first_bias_qv, second_bias_qv, 0.0)
    s_out, a_out, b_out = adamw(w_out, g_out, first_out, second_out, decay_rate)
    s_fc1, a_fc1, b_fc1 = adamw(w_fc1, g_fc1, first_fc1, second_fc1, decay_rate)
    s_bfc1, a_bfc1, b_bfc1 = adamw(bias_fc1, g_bfc1, first_bias_fc1, second_bias_fc1, 0.0)
    s_fc2, a_fc2, b_fc2 = adamw(w_fc2, g_fc2, first_fc2, second_fc2, decay_rate)
    s_bout, a_bout, b_bout = adamw(bias_out, g_bout, first_bias_out, second_bias_out, 0.0)
    return (
        block_out,
        grad_tokens,
        g_norm,
        g_qkv,
        g_bqv,
        g_out,
        g_fc1,
        g_bfc1,
        g_fc2,
        g_bout,
        s_norm,
        w_qkv + s_qkv,
        s_bqv,
        s_out,
        w_fc1 + s_fc1,
        s_bfc1,
        w_fc2 + s_fc2,
        s_bout,
        a_norm,
        a_qkv,
        a_bqv,
        a_out,
        a_fc1,
        a_bfc1,
        a_fc2,
        a_bout,
        b_norm,
        b_qkv,
        b_bqv,
        b_out,
        b_fc1,
        b_bfc1,
        b_fc2,
        b_bout,
    )


F32, BF16 = jnp.float32, jnp.bfloat16
MESH_IDS = pl.DeviceIdType.MESH
VMEM_BYTES = 62 * 2**20

NZ, NY, NCORE, NTP = 4, 2, 2, 2
HALF = 256
NEG = -1e30
LANES = 256


def dot(a, b, ca, cb):
    return lax.dot_general(a, b, (((ca,), (cb,)), ((), ())), preferred_element_type=F32)


def normed(v):
    centre = v - jnp.mean(v, axis=-1, keepdims=True)
    rstd = lax.rsqrt(jnp.mean(centre * centre, axis=-1, keepdims=True) + norm_eps)
    return centre * rstd, rstd


def norm_back(e, gain, xhat, rstd):
    eg = e * gain
    m1 = jnp.mean(eg, axis=-1, keepdims=True)
    m2 = jnp.mean(eg * xhat, axis=-1, keepdims=True)
    return rstd * (eg - m1 - xhat * m2)


def pad_rows(v, rows):
    return jnp.concatenate([v, jnp.zeros((rows - v.shape[0], v.shape[1]), v.dtype)], axis=0)


def load_columns(ref, r):
    return jnp.concatenate([ref[j, r, :] for j in range(ref.shape[0])], axis=1)


def store_columns(ref, r, v):
    for j in range(ref.shape[0]):
        ref[j, r, :] = v[:, 128 * j : 128 * j + 128]


class Place:
    def __init__(self):
        f = lax.axis_index("fsdp")
        self.x = lax.axis_index("tp")
        self.z = f // (NY * NCORE)
        self.y = lax.rem(f // NCORE, NY)
        self.c = lax.rem(f, NCORE)
        self.sib = self.at(self.z, self.y, 1 - self.c, self.x)
        self.peer_x = self.at(self.z, self.y, self.c, 1 - self.x)
        self.peer_y = self.at(self.z, 1 - self.y, self.c, self.x)
        self.other_z = [lax.rem(self.z + d, NZ) for d in range(1, NZ)]
        self.peers_z = [self.at(o, self.y, self.c, self.x) for o in self.other_z]
        self.quad = 2 * self.x + self.c
        self.quad_peers = [
            self.at(self.z, self.y, lax.rem(self.c + k, 2), lax.rem(self.x + k // 2, 2))
            for k in range(1, 4)
        ]
        self.line = self.z * NY + self.y
        self.line_peers = []
        for k in range(1, NZ * NY):
            other = lax.rem(self.line + k, NZ * NY)
            self.line_peers.append(self.at(other // NY, lax.rem(other, NY), self.c, self.x))
        self.lanes = pl.ds(pl.multiple_of(self.x * HALF, HALF), HALF)
        self.lanes_other = pl.ds(pl.multiple_of((1 - self.x) * HALF, HALF), HALF)

    def pick(self, v):
        return jnp.where(self.x == 0, v[..., :HALF], v[..., HALF:])

    def at(self, z, y, c, x):
        return {"fsdp": (z * NY + y) * NCORE + c, "tp": x}

    def barrier(self, everyone=None):
        sem = pltpu.get_barrier_semaphore()
        everyone = everyone or [self.sib, self.peer_x, self.peer_y] + self.peers_z
        for d in everyone:
            pl.semaphore_signal(sem, inc=1, device_id=d, device_id_type=MESH_IDS)
        pl.semaphore_wait(sem, len(everyone))


def remote(src, dst, send, recv, device):
    return pltpu.make_async_remote_copy(
        src_ref=src, dst_ref=dst, send_sem=send, recv_sem=recv, device_id=device, device_id_type=MESH_IDS
    )


def start_all(copies):
    for k in copies:
        k.start()


def wait_all(copies):
    for k in copies:
        k.wait()


AG_SEMS = 7


def gather_steps(at, buf, own, send, recv, local, y_first, part=slice(None)):
    x, y, z, c, lanes = at.x, at.y, at.z, at.c, at.lanes
    own = own.at[part]
    mine = buf.at[z, y, c, part, lanes]
    keep = pltpu.make_async_copy(own, mine, local)
    s0 = [remote(own, mine, send.at[d], recv.at[d], at.peers_z[d]) for d in range(NZ - 1)]
    line = buf.at[:, y, c, part, lanes]
    s1 = remote(line, line, send.at[3], recv.at[3], at.peer_y if y_first else at.peer_x)
    if y_first:
        plane, rest = buf.at[:, :, c, part, lanes], buf.at[:, :, c, part, at.lanes_other]
    else:
        plane, rest = buf.at[:, y, c, part], buf.at[:, 1 - y, c, part]
    s2 = remote(plane, plane, send.at[4], recv.at[4], at.peer_x if y_first else at.peer_y)
    sib_a = remote(plane, plane, send.at[5], recv.at[5], at.sib)
    sib_b = remote(rest, rest, send.at[6], recv.at[6], at.sib)

    def step0():
        keep.start()
        start_all(s0)

    def step1():
        keep.wait()
        wait_all(s0)
        s1.start()

    def step2():
        s1.wait()
        s2.start()
        sib_a.start()

    def step3():
        s2.wait()
        sib_b.start()

    def step4():
        sib_a.wait()
        sib_b.wait()

    return [step0, step1, step2, step3, step4]


RS_SEMS = 6


def scatter_steps(at, grad, r0, r1, r2, r3, out, send, recv, x_first):
    x, y, z, c = at.x, at.y, at.z, at.c
    s0 = remote(grad.at[:, :, 1 - c], r0, send.at[0], recv.at[0], at.sib)
    if x_first:
        s1 = remote(r0.at[:, :, :, at.lanes_other], r1, send.at[1], recv.at[1], at.peer_x)
        s2 = remote(r1.at[:, 1 - y], r2, send.at[2], recv.at[2], at.peer_y)
    else:
        s1 = remote(r0.at[:, 1 - y], r1, send.at[1], recv.at[1], at.peer_y)
        s2 = remote(r1.at[:, :, at.lanes_other], r2, send.at[2], recv.at[2], at.peer_x)
    s3 = [
        remote(r2.at[at.other_z[d]], r3.at[d], send.at[3 + d], recv.at[3 + d], at.peers_z[d])
        for d in range(NZ - 1)
    ]

    def add(a, b):
        return (a.astype(F32) + b.astype(F32)).astype(BF16)

    def step0():
        s0.start()

    def step1():
        s0.wait()

        def body(k, _):
            r0[k] = add(r0[k], grad[k, :, c])
            return 0

        lax.fori_loop(0, NZ, body, 0)
        s1.start()

    def step2():
        s1.wait()

        def body(k, _):
            r1[k] = add(r1[k], at.pick(r0[k]) if x_first else r0[k, y])
            return 0

        lax.fori_loop(0, NZ, body, 0)
        s2.start()

    def step3():
        s2.wait()

        def body(k, _):
            r2[k] = add(r2[k], r1[k, y] if x_first else at.pick(r1[k]))
            return 0

        lax.fori_loop(0, NZ, body, 0)
        start_all(s3)

    def step4():
        wait_all(s3)
        total = r2[z].astype(F32)
        for d in range(NZ - 1):
            total = total + r3[d].astype(F32)
        out[...] = total

    return [step0, step1, step2, step3, step4]


def scatter_scratch(chunks, rows):
    wide = NTP * HALF
    return [
        pltpu.VMEM((chunks, 2, NZ, NY, rows, wide), BF16),
        pltpu.VMEM((chunks, NZ, NY, rows, HALF), BF16),
        pltpu.VMEM((chunks, NZ, rows, wide), BF16),
        pltpu.VMEM((chunks, 2, NZ, rows, HALF), BF16),
        pltpu.VMEM((chunks, 2, NZ - 1, rows, HALF), BF16),
        pltpu.SemaphoreType.DMA((chunks, 2, RS_SEMS)),
        pltpu.SemaphoreType.DMA((chunks, 2, RS_SEMS)),
    ]


def scatter_both(at, k, grads, scratch, outs):
    r0, r1a, r1b, r2, r3, send, recv = scratch
    first = scatter_steps(
        at, grads[0], r0.at[k, 0], r1a.at[k], r2.at[k, 0], r3.at[k, 0], outs[0], send.at[k, 0], recv.at[k, 0], True
    )
    second = scatter_steps(
        at, grads[1], r0.at[k, 1], r1b.at[k], r2.at[k, 1], r3.at[k, 1], outs[1], send.at[k, 1], recv.at[k, 1], False
    )
    return [both(a, b) for a, b in zip(first, second)]


def both(a, b):
    def run():
        a()
        b()

    return run


def gather_both(at, buf, own, sems, part=slice(None)):
    send, recv, local = sems
    first = gather_steps(at, buf.at[0], own.at[0], send.at[0], recv.at[0], local.at[0], True, part)
    second = gather_steps(at, buf.at[1], own.at[1], send.at[1], recv.at[1], local.at[1], False, part)
    return [both(a, b) for a, b in zip(first, second)]


def run_slot(plan, key, counters):
    for want, steps in plan.get(key, {}).items():
        cond = None
        for have, value in zip(counters, want):
            test = have == value
            cond = test if cond is None else jnp.logical_and(cond, test)

        def go(steps=steps):
            for s in steps:
                s()

        pl.when(cond)(go)


def planned(entries):
    plan = {}
    for key, want, step in entries:
        plan.setdefault(key, {}).setdefault(want, []).append(step)
    return plan


def matrix(ref):
    v = ref[...]
    return v.reshape(v.shape[0] * v.shape[1] * v.shape[2] * v.shape[3], v.shape[4])


def left_half(rows):
    return lax.broadcasted_iota(jnp.int32, (rows, 2 * HEAD_DIM), 1) < HEAD_DIM


def split_heads(v, left):
    zero = jnp.zeros_like(v)
    return jnp.concatenate([jnp.where(left, v, zero), jnp.where(left, zero, v)], axis=0)


def projection(a, b):
    return jnp.concatenate([a, b[:, 0:128], b[:, HALF : HALF + 128]], axis=1)


def out_columns(b):
    return jnp.concatenate([b[:, 128:HALF], b[:, HALF + 128 :]], axis=1)


def spread(pieces, width, row, total):
    col = lax.broadcasted_iota(jnp.int32, (128, total), 1).astype(F32)
    lane = lax.broadcasted_iota(jnp.int32, (128, total), 0).astype(F32)
    owner = jnp.floor((col + 0.5) * (1.0 / width))
    pick = (col - owner * width == lane).astype(BF16)
    spreaded = dot(pieces.astype(BF16), pick, 1, 0)
    at_row = lax.broadcasted_iota(jnp.int32, spreaded.shape, 0).astype(F32)
    col = lax.broadcasted_iota(jnp.int32, spreaded.shape, 1).astype(F32)
    owner = jnp.floor((col + 0.5) * (1.0 / width))
    return jnp.sum(jnp.where(at_row == owner * 8.0 + row, spreaded, 0.0), axis=0, keepdims=True)


def attention_kernel(
    dims,
    x_hbm, norm_ref, bout_ref, wqkv_ref, wout_ref, wfc1_ref, wfc2_ref, bqv_ref, bfc1_ref,
    qkv_hbm, ctx_hbm, mid_hbm, p_hbm, watt_hbm, wff_hbm, own_hbm, bias_ref,
    x_s, h1, qkv_s, ctx_s, mid_s, p_s, watt, own, pieces, bias_s,
    ag_send, ag_recv, ag_local, sm_send, sm_recv, out_sem, in_sem,
):
    images, seq, sp, groups, chunks, early = dims
    at = Place()
    x_copy = pltpu.make_async_copy(x_hbm, x_s, in_sem.at[0])
    x_copy.start()
    own_rows = wqkv_ref.shape[2]
    rows = images * seq
    for g in range(groups):
        cols = slice(128 * g, 128 * g + 128)
        own[g, 0] = jnp.concatenate([wqkv_ref[0, :, cols], wqkv_ref[1, :, cols]], axis=1).astype(BF16)
        own[g, 1] = jnp.concatenate([wqkv_ref[2, :, cols], wout_ref[:, cols]], axis=1).astype(BF16)
    pieces[at.x, at.z, at.y, at.c] = jnp.zeros((8, 128), F32)
    pieces[at.x, at.z, at.y, at.c, 0:1, 0 : bfc1_ref.shape[1]] = bfc1_ref[...]
    pieces[at.x, at.z, at.y, at.c, 1:3, 0 : bqv_ref.shape[1]] = bqv_ref[...]

    def sems(k):
        return ag_send.at[k], ag_recv.at[k], ag_local.at[k]

    third = own.shape[2] // 3
    head = [
        gather_both(at, watt.at[0], own.at[0], sems(k), pl.ds(j * third, third))
        for j, k in enumerate((0, groups + early, groups + early + 1))
    ]
    steps = [[None] * 5] + [gather_both(at, watt.at[g], own.at[g], sems(g)) for g in range(1, groups)]
    steps += [gather_both(at, wff_hbm.at[f], own.at[groups + f], sems(groups + f)) for f in range(early)]
    here = pieces.at[at.x, at.z, at.y, at.c]
    line = pieces.at[at.x, :, at.y, at.c]
    plane = pieces.at[at.x, :, :, at.c]
    cube = pieces.at[:, :, :, at.c]
    bias_steps = [[remote(here, here, sm_send.at[d], sm_recv.at[d], at.peers_z[d]) for d in range(NZ - 1)]]
    bias_steps += [
        [remote(r, r, sm_send.at[3 + k], sm_recv.at[3 + k], d)]
        for k, (r, d) in enumerate([(line, at.peer_y), (plane, at.peer_x), (cube, at.sib)])
    ]

    def head_step(k):
        for part in head:
            part[k]()

    at.barrier()
    head_step(0)
    start_all(bias_steps[0])
    steps[1][0]()
    steps[2][0]()
    for f in range(chunks - groups):
        cols = slice(HALF * f, HALF * f + HALF)
        own[groups + f, 0] = wfc1_ref[:, cols].astype(BF16)
        own[groups + f, 1] = wfc2_ref[:, cols].astype(BF16)
    late = pltpu.make_async_copy(own.at[pl.ds(groups + early, chunks - groups - early)], own_hbm, in_sem.at[1])
    late.start()
    x_copy.wait()

    block = rows // 7

    def first_norm(j, _):
        r = pl.ds(pl.multiple_of(j * block, 16), block)
        xhat, _r = normed(x_s[r, :].astype(F32))
        store_columns(mid_s, r, xhat * norm_ref[0:1, :] + norm_ref[1:2, :])
        return 0

    def by_image(i, _):
        h = pad_rows(load_columns(mid_s, pl.ds(i, seq, stride=images)), sp)
        h1[pl.ds(pl.multiple_of(i * sp, 16), sp), :] = h.astype(BF16)
        return 0

    head_step(1)
    wait_all(bias_steps[0])
    start_all(bias_steps[1])
    lax.fori_loop(0, 7, first_norm, 0)
    head_step(2)
    wait_all(bias_steps[1])
    start_all(bias_steps[2])
    lax.fori_loop(0, images, by_image, 0)
    steps[1][1]()
    head_step(3)
    wait_all(bias_steps[2])
    start_all(bias_steps[3])
    wait_all(bias_steps[3])
    flat = pieces[...].reshape(NTP * NZ * NY * NCORE * 8, 128)
    width = bqv_ref.shape[1]
    model = width * NTP * NZ * NY * NCORE
    bias_q = spread(flat, width, 1.0, model)
    bias_v = spread(flat, width, 2.0, model)
    for g in range(groups):
        parts = []
        for t in range(NTP):
            parts += [bias_q[:, t * own_rows + 128 * g : t * own_rows + 128 * g + 128], jnp.zeros((1, 128), F32)]
        for t in range(NTP):
            parts.append(bias_v[:, t * own_rows + 128 * g : t * own_rows + 128 * g + 128])
        bias_s[g] = jnp.concatenate(parts, axis=1)
    width = bfc1_ref.shape[1]
    bias_ff = spread(flat, width, 0.0, width * NTP * NZ * NY * NCORE)
    per = bias_ff.shape[1] // NTP
    for f in range(chunks - groups):
        bias_ref[f] = jnp.concatenate(
            [bias_ff[:, t * per + f * HALF : t * per + f * HALF + HALF] for t in range(NTP)], axis=1
        )
    head_step(4)

    when = {1: [None, None, 1, 4.1, 4.2], 2: [None, 2, 4, 7, 8]}
    when.update({groups + f: ns for f, ns in enumerate([[1.5, 5, 8.5, 11, 14], [5, 9, 12, 14.1, 14.2]])})
    entries = sorted((n, k, j) for k, ns in when.items() for j, n in enumerate(ns) if n is not None)
    entries = [(int(n), k, j) for n, k, j in entries]
    last = 4 * groups + 2
    plan = planned(
        [("out", (n - 4 * groups,), steps[k][j]) if n >= 4 * groups else (n % 2, (n // 4, n % 4 // 2), steps[k][j])
         for n, k, j in entries if n < last]
    )
    remains = [steps[k][j] for n, k, j in entries if n >= last]

    quad = 4
    tr = quad * sp
    left = left_half(sp)
    full = seq // 16 * 16
    live_key = lax.broadcasted_iota(jnp.int32, (sp - full, LANES), 0) < seq - full
    tiles = images // quad
    units = [(a, t) for a in range(quad) for t in range(NTP)]

    def soften(s):
        s = jnp.concatenate([s[:full], jnp.where(live_key, s[full:], NEG)], axis=0)
        e = jnp.exp(s - jnp.max(s, axis=0, keepdims=True))
        return (e * (1.0 / jnp.sum(e, axis=0, keepdims=True))).astype(BF16)

    def group(g, _):
        def tile(i, _):
            run_slot(plan, 0, (g, i))
            r = pl.ds(pl.multiple_of(i * tr, 16), tr)
            w = projection(matrix(watt.at[g, 0]), matrix(watt.at[g, 1]))
            qkv_s[g, r, :] = (dot(h1[r, :], w, 1, 0) + bias_s[g]).astype(BF16)
            run_slot(plan, 1, (g, i))
            qkv = qkv_s[g, r, :]

            def cut(a, first):
                return qkv[a * sp : (a + 1) * sp, first : first + 128]

            scores = []
            for a, t in units:
                q = pad_rows(cut(a, t * HALF) * jnp.asarray(HEAD_DIM ** (-0.5), BF16), LANES)
                scores.append(dot(split_heads(cut(a, t * HALF + 128), left), q, 1, 1))
            probs = []
            for (a, t), s in zip(units, scores):
                probs.append([soften(s[h * sp : (h + 1) * sp]) for h in range(2)])
                for h in range(2):
                    p_s[g, i * quad + a, t, h] = probs[-1][h]
            for (a, t), p in zip(units, probs):
                vt = cut(a, 2 * HALF + t * 128).T
                cs = [dot(vt[h * HEAD_DIM : (h + 1) * HEAD_DIM], p[h], 1, 0) for h in range(2)]
                mine = pl.ds(pl.multiple_of(i * tr + a * sp, 16), sp)
                ctx_s[g, mine, t * 128 : (t + 1) * 128] = jnp.concatenate(cs, axis=0).T[:sp].astype(BF16)
            pltpu.make_async_copy(qkv_s.at[g, r], qkv_hbm.at[g, r], out_sem.at[0, g, i]).start()
            pltpu.make_async_copy(ctx_s.at[g, r], ctx_hbm.at[g, r], out_sem.at[1, g, i]).start()
            im = pl.ds(i * quad, quad)
            pltpu.make_async_copy(p_s.at[g, im], p_hbm.at[g, im], out_sem.at[2, g, i]).start()
            return 0

        lax.fori_loop(0, tiles, tile, 0)
        pltpu.make_async_copy(watt.at[g], watt_hbm.at[g], in_sem.at[2 + g]).start()
        return 0

    lax.fori_loop(0, groups, group, 0)

    def project_out(i, _):
        run_slot(plan, "out", (i,))
        r = pl.ds(pl.multiple_of(i * tr, 16), tr)
        w = jnp.concatenate([out_columns(matrix(watt.at[g, 1])) for g in range(groups)], axis=1)
        c = jnp.concatenate([ctx_s[g, r, :] for g in range(groups)], axis=1)
        attn = dot(c, w, 1, 1)
        for a in range(quad):
            store_columns(mid_s, pl.ds(i * quad + a, seq, stride=images), attn[a * sp : a * sp + seq])
        return 0

    lax.fori_loop(0, tiles, project_out, 0)

    def residual(j, _):
        r = pl.ds(pl.multiple_of(j * block, 16), block)
        store_columns(mid_s, r, load_columns(mid_s, r) + x_s[r, :].astype(F32) + bout_ref[0:1, :])
        pltpu.make_async_copy(mid_s.at[:, r], mid_hbm.at[:, r], out_sem.at[3, 0, j]).start()
        return 0

    lax.fori_loop(0, 7, residual, 0)
    for step in remains:
        step()

    def drain(k, _):
        g, i = k // tiles, lax.rem(k, tiles)
        r = pl.ds(pl.multiple_of(i * tr, 16), tr)
        pltpu.make_async_copy(qkv_s.at[g, r], qkv_hbm.at[g, r], out_sem.at[0, g, i]).wait()
        pltpu.make_async_copy(ctx_s.at[g, r], ctx_hbm.at[g, r], out_sem.at[1, g, i]).wait()
        im = pl.ds(i * quad, quad)
        pltpu.make_async_copy(p_s.at[g, im], p_hbm.at[g, im], out_sem.at[2, g, i]).wait()
        return 0

    lax.fori_loop(0, groups * tiles, drain, 0)
    for g in range(groups):
        pltpu.make_async_copy(watt.at[g], watt_hbm.at[g], in_sem.at[2 + g]).wait()
    for j in range(7):
        r = pl.ds(j * block, block)
        pltpu.make_async_copy(mid_s.at[:, r], mid_hbm.at[:, r], out_sem.at[3, 0, j]).wait()
    late.wait()


def feed_forward_kernel(
    dims,
    counts_ref, norm_ref, bout_ref, bias_ref, mid_hbm, og_hbm, wff_hbm, own_hbm,
    bo_hbm, dmid_hbm, late_hbm, sums_ref, b1g_ref, gff_ref,
    wff, own, h2, h2t, dm, dmt, mlp, dh2, act, dpre, grad, mid_s,
    r0, r1a, r1b, r2, r3, rs_send, rs_recv,
    ag_send, ag_recv, ag_local, in_sem, mid_sem, out_sem,
):
    images, seq, sp, chunks, early, summed = dims
    rows = images * seq
    padded = h2.shape[0]
    block = rows // 7
    at = Place()
    og_copy = pltpu.make_async_copy(og_hbm, dm.at[pl.ds(0, rows)], in_sem.at[0])
    own_copy = pltpu.make_async_copy(own_hbm, own, in_sem.at[1])
    w_copies = [pltpu.make_async_copy(wff_hbm.at[f], wff.at[f], in_sem.at[2 + f]) for f in range(early)]
    own_copy.start()
    og_copy.start()

    def mid_copy(i):
        r = pl.ds(pl.multiple_of(i * block, 16), block)
        return pltpu.make_async_copy(mid_hbm.at[:, r], mid_s.at[lax.rem(i, 4)], mid_sem.at[lax.rem(i, 4)])

    mid_copy(0).start()
    mid_copy(1).start()
    start_all(w_copies)
    late = chunks - early
    gather = {
        early + k: gather_both(
            at, wff.at[early + k], own.at[k], (ag_send.at[k], ag_recv.at[k], ag_local.at[k])
        )
        for k in range(late)
    }
    scratch = (r0, r1a, r1b, r2, r3, rs_send, rs_recv)
    scatter = [
        scatter_both(
            at, k, (grad.at[k % 2, 0], grad.at[k % 2, 1]), scratch, (gff_ref.at[k, 0], gff_ref.at[k, 1])
        )
        for k in range(summed)
    ]
    at.barrier()
    own_copy.wait()
    for k in range(late):
        gather[early + k][0]()
    og_copy.wait()
    count = counts_ref[0]

    first = at.x * images
    image = lax.rem(lax.broadcasted_iota(jnp.int32, (block, 1), 0), images) + first
    live = jnp.where(image < count, 1.0, 0.0).astype(F32)

    def second_norm(i, _):
        pl.when(i + 2 < 7)(lambda: mid_copy(i + 2).start())
        mid_copy(i).wait()
        r = pl.ds(pl.multiple_of(i * block, 16), block)
        xhat, _r = normed(load_columns(mid_s.at[lax.rem(i, 4)], slice(None)))
        h2[r, :] = (xhat * norm_ref[2:3, :] + norm_ref[3:4, :]).astype(BF16)
        dm[r, :] = (dm[r, :].astype(F32) * live).astype(BF16)
        mlp[r, :] = jnp.zeros((block, mlp.shape[1]), F32)
        dh2[r, :] = jnp.zeros((block, mlp.shape[1]), F32)
        return 0

    rest = pl.ds(rows, padded - rows)
    for ref in (h2, dm, act, dpre):
        ref[rest, :] = jnp.zeros((padded - rows, ref.shape[1]), BF16)
    lax.fori_loop(0, 7, second_norm, 0)

    def turn(j, _):
        r = pl.ds(pl.multiple_of(j * 128, 128), 128)
        h2t[:, r] = h2[r, :].T
        dmt[:, r] = dm[r, :].T
        return 0

    lax.fori_loop(0, padded // 128, turn, 0)
    wait_all(w_copies)

    entries = []
    for k, slots in enumerate(
        ((None, 0, 2, 6, 8), (None, 2, 6, 10, 12), (None, 4, 7, 12, 16), (None, 6, 10, 14, 20))
    ):
        entries += [(n, gather[early + k][j]) for j, n in enumerate(slots) if n is not None]
    for k, slots in enumerate(((8, 10, 16, 18, 21), (12, 14, 17, 19, 23), (16, 18, 21, 23, 24))):
        entries += [(n, scatter[k][j]) for j, n in enumerate(slots)]
    entries.sort(key=lambda e: e[0])
    plan = planned([(slot % 4, (slot // 4,), step) for slot, step in entries if slot < 4 * chunks])
    tail = [step for slot, step in entries if slot >= 4 * chunks]

    def late_copy(k):
        return pltpu.make_async_copy(grad.at[k % 2], late_hbm.at[k - summed], out_sem.at[k - summed])

    def chunk(f, _):
        b1 = bias_ref[f]
        for i in range(2):
            run_slot(plan, i, (f,))
            r = pl.ds(i * (rows // 2), rows // 2)
            w1, w2 = matrix(wff.at[f, 0]), matrix(wff.at[f, 1])
            pre = dot(h2[r, :], w1, 1, 0) + b1
            phi = 0.5 + 0.5 * lax.erf(pre * 0.7071067811865476)
            a = (pre * phi).astype(BF16)
            slope = phi + pre * (jnp.exp(-0.5 * pre * pre) * 0.3989422804014327)
            d = (dot(dm[r, :], w2, 1, 0) * slope).astype(BF16)
            act[r, :] = a
            dpre[r, :] = d
            mlp[r, :] += dot(a, w2, 1, 1)
            dh2[r, :] += dot(d, w1, 1, 1)
        slot = lax.rem(f, 2)
        shape = grad.shape[2:]
        run_slot(plan, 2, (f,))
        for k in range(summed, chunks - 2):
            pl.when(f == k + 2)(late_copy(k).wait)
        b1g_ref[f] = jnp.sum(dpre[...].astype(F32), axis=0, keepdims=True)
        grad[slot, 0] = dot(h2t[...], dpre[...], 1, 0).astype(BF16).reshape(shape)
        run_slot(plan, 3, (f,))
        grad[slot, 1] = dot(dmt[...], act[...], 1, 0).astype(BF16).reshape(shape)

        for k in range(summed, chunks):
            pl.when(f == k)(late_copy(k).start)
        return 0

    mid_copy(0).start()
    mid_copy(1).start()
    lax.fori_loop(0, chunks, chunk, 0)

    def dmid_copy(i):
        r = pl.ds(pl.multiple_of(i * block, 16), block)
        return pltpu.make_async_copy(mid_s.at[lax.rem(i, 4)], dmid_hbm.at[:, r], out_sem.at[16 + lax.rem(i, 4)])

    def second_norm_back(i, acc):
        pl.when(i >= 2)(lambda: dmid_copy(i - 2).wait())
        pl.when(i + 2 < 7)(lambda: mid_copy(i + 2).start())
        mid_copy(i).wait()
        r = pl.ds(pl.multiple_of(i * block, 16), block)
        mid = load_columns(mid_s.at[lax.rem(i, 4)], slice(None))
        xhat, rstd = normed(mid)
        h2[r, :] = (mid + mlp[r, :] + bout_ref[1:2, :]).astype(BF16)
        e = dh2[r, :]
        live = dm[r, :].astype(F32)
        d = live + norm_back(e, norm_ref[2:3, :], xhat, rstd)
        store_columns(mid_s.at[lax.rem(i, 4)], slice(None), d)
        pltpu.make_async_copy(h2.at[r], bo_hbm.at[r], out_sem.at[8 + i]).start()
        dmid_copy(i).start()
        terms = (e * xhat, e, d, live)
        return tuple(a + jnp.sum(t, axis=0, keepdims=True) for a, t in zip(acc, terms))

    zero = jnp.zeros((1, mlp.shape[1]), F32)
    acc = lax.fori_loop(0, 7, second_norm_back, (zero,) * 4)
    sums_ref[...] = jnp.zeros(sums_ref.shape, F32)
    for k in range(4):
        sums_ref[k : k + 1, :] = acc[k]
    for step in tail:
        step()

    for i in range(7):
        r = pl.ds(i * block, block)
        pltpu.make_async_copy(h2.at[r], bo_hbm.at[r], out_sem.at[8 + i]).wait()
    dmid_copy(5).wait()
    dmid_copy(6).wait()
    for k in range(chunks - 2, chunks):
        late_copy(k).wait()


def attention_back_kernel(
    dims,
    norm_ref, sums_ref, b1g_ref, x_hbm, dmid_hbm, late_hbm, watt_hbm, qkv_hbm, ctx_hbm, p_hbm,
    gt_hbm, glate_ref, gatt_ref, small_ref,
    dattn, h1t, dh1, dqkv, watt, qkv_s, dc_s, ctx_s, ctxt, p_s, grad, x_s, dmid_s, gt_s, bias_s,
    small, small_line,
    r0, r1a, r1b, r2, r3, rs_send, rs_recv, sm_send, sm_recv,
    in_sem, ctx_sem, tile_sem, dmid_sem, gt_sem,
):
    images, seq, sp, groups, chunks, held = dims
    rows = images * seq
    block = rows // 7
    model = x_s.shape[1]
    quad = 4
    tr = quad * sp
    tiles = images // quad
    at = Place()
    dmid_in = pltpu.make_async_copy(dmid_hbm, dh1.at[:, pl.ds(0, rows)], in_sem.at[0])
    watt_copy = pltpu.make_async_copy(watt_hbm, watt, in_sem.at[1])
    x_copy = pltpu.make_async_copy(x_hbm, x_s, in_sem.at[2])
    late_copies = [pltpu.make_async_copy(late_hbm.at[k], grad.at[k], in_sem.at[3 + k]) for k in range(held)]

    def dmid_copy(i):
        r = pl.ds(pl.multiple_of(i * block, 16), block)
        return pltpu.make_async_copy(dmid_hbm.at[:, r], dmid_s.at[lax.rem(i, 3)], dmid_sem.at[lax.rem(i, 3)])

    def ctx_copy(g):
        return pltpu.make_async_copy(ctx_hbm.at[g], ctx_s, ctx_sem.at[0])

    def tile_copies(g, i):
        r, im = pl.ds(pl.multiple_of(i * tr, 16), tr), pl.ds(i * quad, quad)
        return [
            pltpu.make_async_copy(qkv_hbm.at[g, r], qkv_s.at[r], tile_sem.at[0, i]),
            pltpu.make_async_copy(p_hbm.at[g, im], p_s.at[im], tile_sem.at[1, i]),
        ]

    late_copies[0].start()
    dmid_in.start()
    x_copy.start()
    watt_copy.start()
    start_all(late_copies[1:])
    ctx_copy(0).start()
    for i in range(tiles):
        start_all(tile_copies(0, i))
    scratch = (r0, r1a, r1b, r2, r3, rs_send, rs_recv)
    scatter = [
        scatter_both(at, k, (grad.at[k, 0], grad.at[k, 1]), scratch, (glate_ref.at[k, 0], glate_ref.at[k, 1]))
        for k in range(held)
    ]
    for g in range(groups):
        scatter.append(
            scatter_both(
                at, held + g, (grad.at[g % held, 0], grad.at[g % held, 1]), scratch, (gatt_ref.at[g, 0], gatt_ref.at[g, 1])
            )
        )
    own_quad, own_line = small.at[at.quad], small_line.at[at.line]
    sm_quad = [remote(own_quad, own_quad, sm_send.at[k], sm_recv.at[k], d) for k, d in enumerate(at.quad_peers)]
    sm_line = [
        remote(own_line, own_line, sm_send.at[3 + k], sm_recv.at[3 + k], d) for k, d in enumerate(at.line_peers)
    ]
    at.barrier(at.quad_peers + at.line_peers)
    for k in range(held):
        late_copies[k].wait()
        scatter[k][0]()

    dmid_in.wait()

    def take_dattn(i, _):
        d = pad_rows(load_columns(dh1, pl.ds(i, seq, stride=images)), sp)
        dattn[pl.ds(pl.multiple_of(i * sp, 16), sp), :] = d.astype(BF16)
        return 0

    lax.fori_loop(0, images, take_dattn, 0)
    x_copy.wait()

    def first_norm(j, _):
        r = pl.ds(pl.multiple_of(j * block, 16), block)
        xhat, _r = normed(x_s[r, :].astype(F32))
        store_columns(dh1, r, xhat * norm_ref[0:1, :] + norm_ref[1:2, :])
        return 0

    lax.fori_loop(0, 7, first_norm, 0)

    def by_image(i, _):
        h = pad_rows(load_columns(dh1, pl.ds(i, seq, stride=images)), sp)
        dqkv[0, pl.ds(pl.multiple_of(i * sp, 16), sp), :] = h.astype(BF16)
        return 0

    lax.fori_loop(0, images, by_image, 0)

    scatter[0][1]()

    def turn(j, _):
        r = pl.ds(pl.multiple_of(j * 128, 128), 128)
        h1t[:, r] = dqkv[0, r, :].T
        return 0

    lax.fori_loop(0, images * sp // 128, turn, 0)
    watt_copy.wait()

    entries = []
    for k, slots in enumerate(((2, 8, 12), (2, 6, 10, 14), (5, 9, 12, 16))):
        entries += [(n, scatter[k][5 - len(slots) + j]) for j, n in enumerate(slots)]
    for g, slots in enumerate(((12, 15, 18, 21, 27), (14, 16, 20, 22, 30), (18, 20, 26, 30, 31))):
        entries += [(n, scatter[held + g][j]) for j, n in enumerate(slots)]
    entries.sort(key=lambda e: e[0])

    def spot(n):
        return (n % 2, (n // 6, n % 6 // 2)) if n % 6 < 4 else (n % 6, (n // 6,))

    tail_at = 6 * groups
    plan = planned(
        [spot(n) + (step,) for n, step in entries if n < tail_at]
        + [("through", (n - tail_at,), step) for n, step in entries if tail_at <= n < tail_at + 4]
        + [("norm", (n - tail_at - 4,), step) for n, step in entries if tail_at + 4 <= n < tail_at + 11]
    )
    tail = [[step for n, step in entries if n == at_end] for at_end in (tail_at + 12, tail_at + 13)]

    left = left_half(sp)
    scale = HEAD_DIM ** (-0.5)

    units = [(a, t) for a in range(quad) for t in range(NTP)]

    def group(g, _):
        keep = lax.rem(g, grad.shape[0])
        ctx_copy(g).wait()
        ctxt[...] = ctx_s[...].T
        pl.when(g + 1 < groups)(lambda: ctx_copy(g + 1).start())

        def tile(i, acc):
            wait_all(tile_copies(g, i))
            run_slot(plan, 0, (g, i))
            r = pl.ds(pl.multiple_of(i * tr, 16), tr)
            dc_s[...] = dot(dattn[r, :], out_columns(matrix(watt.at[g, 1])), 1, 0).astype(BF16)
            run_slot(plan, 1, (g, i))
            qkv, dc = qkv_s[r, :], dc_s[...]

            def cut(a, first):
                return qkv[a * sp : (a + 1) * sp, first : first + 128]

            def wide(v):
                return pad_rows(v, LANES)

            def grads_in(a, t):
                return wide(dc[a * sp : (a + 1) * sp, t * 128 : (t + 1) * 128])

            dps = [dot(split_heads(cut(a, 2 * HALF + t * 128), left), grads_in(a, t), 1, 1) for a, t in units]
            dss = []
            for (a, t), dp in zip(units, dps):
                ds = []
                for h in range(2):
                    p = p_s[i * quad + a, t, h].astype(F32)
                    pd = p * dp[h * sp : (h + 1) * sp]
                    ds.append((pd - p * jnp.sum(pd, axis=0, keepdims=True)).astype(BF16))
                dss.append(ds)
            parts = []
            for (a, t), ds in zip(units, dss):
                q = wide(cut(a, t * HALF) * jnp.asarray(scale, BF16))
                kt = cut(a, t * HALF + 128).T
                dqt = [dot(kt[h * HEAD_DIM : (h + 1) * HEAD_DIM], ds[h], 1, 0) for h in range(2)]
                dk = dot(jnp.concatenate(ds, axis=0), q, 1, 0)
                ps = jnp.concatenate([p_s[i * quad + a, t, h] for h in range(2)], axis=0)
                dv = dot(ps, grads_in(a, t), 1, 0)
                parts.append((
                    jnp.concatenate(dqt, axis=0).T[:sp] * scale,
                    jnp.where(left, dk[:sp], dk[sp:]),
                    jnp.where(left, dv[:sp], dv[sp:]),
                ))
            for a in range(quad):
                (q0, k0, v0), (q1, k1, v1) = parts[NTP * a], parts[NTP * a + 1]
                d = jnp.concatenate([q0, k0, q1, k1, v0, v1], axis=1).astype(BF16)
                dqkv[g, pl.ds(pl.multiple_of(i * tr + a * sp, 16), sp), :] = d
                acc = acc + jnp.sum(d.astype(F32), axis=0, keepdims=True)
            pl.when(g + 1 < groups)(lambda: start_all(tile_copies(g + 1, i)))
            return acc

        bias_s[g] = lax.fori_loop(0, tiles, tile, jnp.zeros((1, model), F32))
        run_slot(plan, 4, (g,))
        shape = grad.shape[2:]
        gw = dot(h1t[...], dqkv[g], 1, 0).astype(BF16)
        grad[keep, 0] = gw[:, : 2 * HALF].reshape(shape)
        run_slot(plan, 5, (g,))
        go = dot(ctxt[...], dattn[...], 1, 0).T.astype(BF16)
        grad[keep, 1] = jnp.concatenate(
            [gw[:, 2 * HALF : 2 * HALF + 128], go[:, :128], gw[:, 2 * HALF + 128 :], go[:, 128:]], axis=1
        ).reshape(shape)
        return 0

    dmid_copy(0).start()
    dmid_copy(1).start()
    lax.fori_loop(0, groups, group, 0)
    small_tr = 2 * sp

    def through(i, _):
        run_slot(plan, "through", (i,))
        r = pl.ds(pl.multiple_of(i * small_tr, 16), small_tr)
        d = jnp.concatenate([dqkv[g, r, :] for g in range(groups)], axis=1)
        w = jnp.concatenate(
            [projection(matrix(watt.at[g, 0]), matrix(watt.at[g, 1])) for g in range(groups)], axis=1
        )
        back = dot(d, w, 1, 1)
        for a in range(2):
            store_columns(dh1, pl.ds(i * 2 + a, seq, stride=images), back[a * sp : a * sp + seq])
        return 0

    lax.fori_loop(0, images // 2, through, 0)

    def gt_copy(i):
        r = pl.ds(pl.multiple_of(i * block, 16), block)
        return pltpu.make_async_copy(gt_s.at[lax.rem(i, 2)], gt_hbm.at[r], gt_sem.at[lax.rem(i, 2)])

    def first_norm_back(i, acc):
        run_slot(plan, "norm", (i,))
        pl.when(i >= 2)(lambda: gt_copy(i - 2).wait())
        pl.when(i + 2 < 7)(lambda: dmid_copy(i + 2).start())
        dmid_copy(i).wait()
        r = pl.ds(pl.multiple_of(i * block, 16), block)
        xhat, rstd = normed(x_s[r, :].astype(F32))
        e = load_columns(dh1, r)
        d = load_columns(dmid_s.at[lax.rem(i, 3)], slice(None))
        gt_s[lax.rem(i, 2)] = d + norm_back(e, norm_ref[0:1, :], xhat, rstd)
        gt_copy(i).start()
        return (acc[0] + jnp.sum(e * xhat, axis=0, keepdims=True), acc[1] + jnp.sum(e, axis=0, keepdims=True))

    zero = jnp.zeros((1, model), F32)
    acc = lax.fori_loop(0, 7, first_norm_back, (zero, zero))
    own_quad[...] = jnp.zeros(own_quad.shape, F32)
    own_quad[0:1, :] = acc[0]
    own_quad[1:2, :] = acc[1]
    own_quad[2:6, :] = sums_ref[0:4, :]
    own_cols = groups * 128
    for g in range(groups):
        for t in range(NTP):
            cols = slice(t * own_cols + 128 * g, t * own_cols + 128 * g + 128)
            own_quad[6:7, cols] = bias_s[g, :, t * HALF : t * HALF + 128]
            own_quad[7:8, cols] = bias_s[g, :, 2 * HALF + t * 128 : 2 * HALF + t * 128 + 128]
    for f in range(chunks):
        for t in range(NTP):
            first = t * chunks * HALF + f * HALF
            row, col = 8 + first // model, first % model
            own_quad[row : row + 1, col : col + HALF] = b1g_ref[f, :, t * HALF : t * HALF + HALF]
    start_all(sm_quad)
    for step in tail[0]:
        step()
    wait_all(sm_quad)
    own_line[...] = (small[0] + small[1]) + (small[2] + small[3])
    start_all(sm_line)
    for step in tail[1]:
        step()
    gt_copy(5).wait()
    gt_copy(6).wait()
    wait_all(sm_line)
    total = small_line[0]
    for k in range(1, NZ * NY):
        total = total + small_line[k]
    small_ref[...] = total


def step_kernel(dims, *refs):
    groups, chunks, held = dims
    names = ("norm", "qkv", "bqv", "out", "fc1", "bfc1", "fc2", "bout")
    bo_hbm, gt_hbm, gff_ref, glate_ref, gatt_ref, small_ref = refs[:6]
    n = len(names)
    ps, ms, vs = (dict(zip(names, refs[6 + k * n : 6 + (k + 1) * n])) for k in range(3))
    outs = refs[6 + 3 * n :]
    bo_out, gt_out = outs[:2]
    g_out, u_out, m_out, v_out = (dict(zip(names, outs[2 + k * n : 2 + (k + 1) * n])) for k in range(4))
    bo_s, gt_s, sem = outs[2 + 4 * n :]
    pieces = 7
    block = bo_s.shape[0] // pieces
    moves = []
    for j in range(pieces):
        r = pl.ds(j * block, block)
        for k, (src, mid, dst) in enumerate(((gt_hbm, gt_s, gt_out), (bo_hbm, bo_s, bo_out))):
            moves.append((
                pltpu.make_async_copy(src.at[r], mid.at[r], sem.at[0, k, j]),
                pltpu.make_async_copy(mid.at[r], dst.at[r], sem.at[1, k, j]),
            ))
    for first, _second in moves:
        first.start()
    for first, second in moves:
        first.wait()
        second.start()
    late = chunks - held

    def ff(f, h):
        return gff_ref[f, h] if f < late else glate_ref[f - late, h]

    whole = {"qkv": True, "fc1": True, "fc2": True}
    decays = ("qkv", "out", "fc1", "fc2")

    def update(name, index, g):
        p = ps[name][index]
        u, m, v = adamw(p, g, ms[name][index], vs[name][index], decay_rate if name in decays else 0.0)
        g_out[name][index] = g
        u_out[name][index] = p + u if name in whole else u
        m_out[name][index] = m
        v_out[name][index] = v

    for c in range(3):
        gs = [gatt_ref[g, c // 2][:, (c % 2) * 128 : (c % 2) * 128 + 128] for g in range(groups)]
        update("qkv", c, jnp.concatenate(gs, axis=1))
    update("out", ..., jnp.concatenate([gatt_ref[g, 1][:, 128:] for g in range(groups)], axis=1))
    for f in range(chunks):
        cols = slice(f * HALF, (f + 1) * HALF)
        update("fc1", (slice(None), cols), ff(f, 0))
        update("fc2", (slice(None), cols), ff(f, 1))
    update("norm", ..., small_ref[0:4, :])
    update("bout", ..., small_ref[4:6, :])
    part = lax.axis_index("tp") * (NZ * NY * NCORE) + lax.axis_index("fsdp")
    width = ps["bqv"].shape[1]
    model = small_ref.shape[1]
    update("bqv", ..., pltpu.roll(small_ref[0:8, :], lax.rem(model - part * width, model), 1)[6:8, :width])
    width = ps["bfc1"].shape[1]
    per = model // width
    turned = pltpu.roll(small_ref[8:16, :], lax.rem(model - lax.rem(part, per) * width, model), 1)[:, :width]
    at_row = lax.broadcasted_iota(jnp.int32, turned.shape, 0)
    update("bfc1", ..., jnp.sum(jnp.where(at_row == part // per, turned, 0.0), axis=0, keepdims=True))
    for _first, second in moves:
        second.wait()


def sds(shape, dtype):
    return jax.ShapeDtypeStruct(shape, dtype)


def fused_device(
    tokens_in, out_grad, image_counts,
    norm_params, w_qkv, bias_qv, w_out, w_fc1, bias_fc1, w_fc2, bias_out,
    *moments,
):
    images, seq, model = tokens_in.shape
    sp = -(-seq // 16) * 16
    rows = images * sp
    own_rows, own_cols = w_qkv.shape[1], w_qkv.shape[2]
    groups = own_cols // 128
    chunks = w_fc1.shape[1] // HALF
    early, summed = 2, chunks - 3
    held = chunks - summed
    wide = NTP * HALF
    cube = (NZ, NY, NCORE, own_rows, wide)
    any_, vm, sm = pl.BlockSpec(memory_space=pl.ANY), pl.BlockSpec(memory_space=pltpu.VMEM), pl.BlockSpec(memory_space=pltpu.SMEM)
    dma = pltpu.SemaphoreType.DMA

    def params(k):
        return pltpu.CompilerParams(collective_id=k, has_side_effects=True, vmem_limit_bytes=VMEM_BYTES)

    n_ag = groups + early + 2
    flat_rows = images * seq
    strided_rows = images * (-(-seq // 8) * 8)

    def by_token(a):
        return a.transpose(1, 0, 2).reshape(flat_rows, model)

    def by_image(a):
        return a.reshape(seq, images, model).transpose(1, 0, 2)

    x_rows, og_rows = by_token(tokens_in), by_token(out_grad)
    qkv, ctx, mid, p, watt, wff, own, bias1 = pl.pallas_call(
        functools.partial(attention_kernel, (images, seq, sp, groups, groups + chunks, early)),
        name="attention",
        in_specs=[any_] + [vm] * 8,
        out_specs=[any_] * 7 + [vm],
        out_shape=[
            sds((groups, rows, model), BF16), sds((groups, rows, HALF), BF16), sds((model // 128, flat_rows, 128), F32),
            sds((groups, images, NTP, 2, sp, LANES), BF16), sds((groups, 2) + cube, BF16), sds((early, 2) + cube, BF16),
            sds((chunks - early, 2, own_rows, HALF), BF16), sds((chunks, 1, wide), F32),
        ],
        scratch_shapes=[
            pltpu.VMEM((flat_rows, model), BF16), pltpu.VMEM((rows, model), BF16),
            pltpu.VMEM((groups, rows, model), BF16), pltpu.VMEM((groups, rows, HALF), BF16),
            pltpu.VMEM((model // 128, strided_rows, 128), F32),
            pltpu.VMEM((groups, images, NTP, 2, sp, LANES), BF16),
            pltpu.VMEM((groups, 2) + cube, BF16), pltpu.VMEM((groups + chunks, 2, own_rows, HALF), BF16),
            pltpu.VMEM((NTP, NZ, NY, NCORE, 8, 128), F32), pltpu.VMEM((groups, 1, model), F32),
            dma((n_ag, 2, AG_SEMS)), dma((n_ag, 2, AG_SEMS)), dma((n_ag, 2)), dma((6,)), dma((6,)),
            dma((4, groups, 8)), dma((2 + groups,)),
        ],
        compiler_params=params(0),
    )(x_rows, norm_params, bias_out, w_qkv, w_out.T, w_fc1, w_fc2.T, bias_qv, bias_fc1.reshape(1, -1))

    late = chunks - early
    bo, dmid, grad_late, sums, b1g, gff = pl.pallas_call(
        functools.partial(feed_forward_kernel, (images, seq, sp, chunks, early, summed)),
        name="feed_forward",
        in_specs=[sm, vm, vm, vm] + [any_] * 4,
        out_specs=[any_] * 3 + [vm] * 3,
        out_shape=[
            sds((flat_rows, model), BF16), sds((model // 128, flat_rows, 128), F32),
            sds((held, 2) + cube, BF16), sds((8, model), F32), sds((chunks, 1, wide), F32),
            sds((summed, 2, own_rows, HALF), F32),
        ],
        scratch_shapes=[
            pltpu.VMEM((chunks, 2) + cube, BF16), pltpu.VMEM((late, 2, own_rows, HALF), BF16),
            pltpu.VMEM((rows, model), BF16), pltpu.VMEM((model, rows), BF16),
            pltpu.VMEM((rows, model), BF16), pltpu.VMEM((model, rows), BF16),
            pltpu.VMEM((flat_rows, model), F32), pltpu.VMEM((flat_rows, model), F32),
            pltpu.VMEM((rows, wide), BF16), pltpu.VMEM((rows, wide), BF16),
            pltpu.VMEM((2, 2) + cube, BF16), pltpu.VMEM((4, model // 128, flat_rows // 7, 128), F32),
        ]
        + scatter_scratch(summed, own_rows)
        + [
            dma((late, 2, AG_SEMS)), dma((late, 2, AG_SEMS)), dma((late, 2)), dma((2 + early,)), dma((4,)),
            dma((24,)),
        ],
        compiler_params=params(1),
    )(image_counts, norm_params, bias_out, bias1, mid, og_rows, wff, own)

    gt, glate, gatt, small = pl.pallas_call(
        functools.partial(attention_back_kernel, (images, seq, sp, groups, chunks, held)),
        name="attention_back",
        in_specs=[vm] * 3 + [any_] * 7,
        out_specs=[any_] + [vm] * 3,
        out_shape=[
            sds((flat_rows, model), F32), sds((held, 2, own_rows, HALF), F32),
            sds((groups, 2, own_rows, HALF), F32), sds((16, model), F32),
        ],
        scratch_shapes=[
            pltpu.VMEM((rows, model), BF16), pltpu.VMEM((model, rows), BF16),
            pltpu.VMEM((model // 128, strided_rows, 128), F32), pltpu.VMEM((groups, rows, model), BF16),
            pltpu.VMEM((groups, 2) + cube, BF16),
            pltpu.VMEM((rows, model), BF16), pltpu.VMEM((4 * sp, HALF), BF16),
            pltpu.VMEM((rows, HALF), BF16), pltpu.VMEM((HALF, rows), BF16),
            pltpu.VMEM((images, NTP, 2, sp, LANES), BF16), pltpu.VMEM((held, 2) + cube, BF16),
            pltpu.VMEM((flat_rows, model), BF16), pltpu.VMEM((3, model // 128, flat_rows // 7, 128), F32),
            pltpu.VMEM((2, flat_rows // 7, model), F32), pltpu.VMEM((groups, 1, model), F32),
            pltpu.VMEM((4, 16, model), F32), pltpu.VMEM((NZ * NY, 16, model), F32),
        ]
        + scatter_scratch(held + groups, own_rows)
        + [dma((10,)), dma((10,)), dma((3 + held,)), dma((1,)), dma((2, 2)), dma((3,)), dma((2,))],
        compiler_params=params(2),
    )(norm_params, sums, b1g, x_rows, dmid, grad_late, watt, qkv, ctx, p)

    turned = (3, 6)

    def flat(a, k):
        return a.reshape(1, -1) if a.ndim == 1 else a.T if k in turned else a

    weights = [flat(a, k) for k, a in enumerate((norm_params, w_qkv, bias_qv, w_out, w_fc1, bias_fc1, w_fc2, bias_out))]
    moments = [flat(a, k % 8) for k, a in enumerate(moments)]
    shapes = [sds(a.shape, F32) for a in weights]
    outs = pl.pallas_call(
        functools.partial(step_kernel, (groups, chunks, held)),
        name="adamw_step",
        in_specs=[any_] * 2 + [vm] * 28,
        out_specs=[any_] * 2 + [vm] * 32,
        out_shape=[sds(bo.shape, BF16), sds(gt.shape, F32)] + shapes * 4,
        scratch_shapes=[pltpu.VMEM(bo.shape, BF16), pltpu.VMEM(gt.shape, F32), dma((2, 2, 7))],
        compiler_params=pltpu.CompilerParams(vmem_limit_bytes=VMEM_BYTES),
    )(bo, gt, gff, glate, gatt, small, *weights, *moments)
    bo, gt, *outs = outs
    outs = [o.reshape(-1) if k % 8 == 5 else o.T if k % 8 in turned else o for k, o in enumerate(outs)]
    return (by_image(bo), by_image(gt)) + tuple(outs)


def solution(mesh):
    placed = (
        P(("fsdp", "tp"), None, None),
        P(("fsdp", "tp"), None, None),
        P("fsdp"),
        P(),
        P(None, "fsdp", "tp"),
        P(None, ("tp", "fsdp")),
        P("tp", "fsdp"),
        P("fsdp", "tp"),
        P(("tp", "fsdp")),
        P("tp", "fsdp"),
        P(),
        P(),
        P(None, "fsdp", "tp"),
        P(None, ("tp", "fsdp")),
        P("tp", "fsdp"),
        P("fsdp", "tp"),
        P(("tp", "fsdp")),
        P("tp", "fsdp"),
        P(),
        P(),
        P(None, "fsdp", "tp"),
        P(None, ("tp", "fsdp")),
        P("tp", "fsdp"),
        P("fsdp", "tp"),
        P(("tp", "fsdp")),
        P("tp", "fsdp"),
        P(),
    )
    fits = mesh.shape["fsdp"] == NZ * NY * NCORE and mesh.shape["tp"] == NTP
    return jax.shard_map(
        fused_device if fits else per_device,
        mesh=mesh,
        in_specs=placed,
        out_specs=(
            P(("fsdp", "tp"), None, None),
            P(("fsdp", "tp"), None, None),
            P(),
            P(None, "fsdp", "tp"),
            P(None, ("tp", "fsdp")),
            P("tp", "fsdp"),
            P("fsdp", "tp"),
            P(("tp", "fsdp")),
            P("tp", "fsdp"),
            P(),
            P(),
            P(None, "fsdp", "tp"),
            P(None, ("tp", "fsdp")),
            P("tp", "fsdp"),
            P("fsdp", "tp"),
            P(("tp", "fsdp")),
            P("tp", "fsdp"),
            P(),
            P(),
            P(None, "fsdp", "tp"),
            P(None, ("tp", "fsdp")),
            P("tp", "fsdp"),
            P("fsdp", "tp"),
            P(("tp", "fsdp")),
            P("tp", "fsdp"),
            P(),
            P(),
            P(None, "fsdp", "tp"),
            P(None, ("tp", "fsdp")),
            P("tp", "fsdp"),
            P("fsdp", "tp"),
            P(("tp", "fsdp")),
            P("tp", "fsdp"),
            P(),
        ),
        check_vma=False,
    )
```
